512 devices in a mesh: blk: 16 (over z_hi, x, core), rep: 32 (over y, z_lo).
Axes of the slice: x: 4, y: 4, z: 16 (z_hi: 2, z_lo: 8; z = z_hi * 8 + z_lo), core: 2. Of those that a mesh axis runs over, the one named last changes fastest.
Arguments:
- features_t: bfloat16 [1024, 16384], P('rep', 'blk'), may hold values from -6 to 6
- tile_dst: int32 [1024], P('blk'), may hold values from 0 to 7, as said below
- tile_src: int32 [1024], P('blk'), may hold values from 0 to 127, as said below
- tile_edges: int32 [1024], P('blk'), may hold values from 0 to 16384, as said below
- tile_values: bfloat16 [1024, 128, 128], P('blk'), may hold values from -0.5 to 0.5
- weight: bfloat16 [1024, 1024], P('rep'), may hold values from -0.1875 to 0.1875
- cotangent: bfloat16 [1024, 16384], P('rep', 'blk'), may hold values from -6 to 6
Outputs:
- activated: bfloat16 [1024, 16384], P('rep', 'blk')
- grad_weight: float32 [1024, 1024], P('rep')
- grad_features: bfloat16 [1024, 16384], P('rep', 'blk')
The draws below stay inside these ranges and needn't reach their ends.
Inputs may be any that keep to these rules, and one draw needn't show every extreme that they name: In each group of 64 slots the live slots (tile_edges > 0) come first; the first 8 slots of group g are live with tile_dst b and tile_src g * 8 + b; a group has 8 to 64 live slots, and some group has all 64 live; empty slots have tile_dst 0. Empty slots have tile_src 0. Live slots of group g after the first 8 name source blocks of other groups; for any group g and any other group h at most 4 live slots of g name blocks of h, and in the group with all 64 slots live some h is named by exactly 4. `tile_edges`: zero exactly on empty slots.
All inputs are finite; a program needn't handle non-finite values.
Results may differ from the reference program's by a relative error of at most 0.006.
Values may be sent and summed in bfloat16 or wider, within the bound.
A program may use at most 64 MiB of HBM per device.

```python
import jax
import jax.numpy as jnp
from jax import lax

F = 1024
TB = 128
BPD = 8
NT = 64
NBT = 128
NODES = 16384
TILES = 1024
N_BLK = 16


def tile_lists(key):
    groups = TILES // NT
    keys = jax.random.split(key, 6)
    raw = jax.random.randint(keys[0], (groups,), 0, 1001)
    live = BPD + (NT - BPD) * raw * raw // 1000000
    fullest = jax.random.randint(keys[1], (), 0, groups)
    live = jnp.where(jnp.arange(groups) == fullest, NT, live)
    slot = jnp.arange(NT, dtype=jnp.int32)[None, :]
    group = jnp.arange(groups, dtype=jnp.int32)[:, None]
    rand_dst = jax.random.randint(keys[2], (groups, NT), 0, BPD)
    inner = jax.random.randint(keys[3], (groups, NT), 0, BPD)
    turn = jax.random.randint(keys[5], (groups, 1), 0, groups - 1)
    other = (group + 1 + (jnp.maximum(slot - BPD, 0) + turn) % (groups - 1)) % groups
    rand_src = other * BPD + inner
    first = slot < BPD
    dst = jnp.where(first, jnp.minimum(slot, BPD - 1), rand_dst)
    src = jnp.where(first, group * BPD + jnp.minimum(slot, BPD - 1), rand_src)
    alive = slot < live[:, None]
    edges = jax.random.randint(keys[4], (groups, NT), 1, TB * TB + 1)
    edges = jnp.where((group == fullest) & (slot == 0), TB * TB, edges)
    dst = jnp.where(alive, dst, 0)
    src = jnp.where(alive, src, 0)
    edges = jnp.where(alive, edges, 0)
    return (dst.reshape(-1).astype(jnp.int32), src.reshape(-1).astype(jnp.int32), edges.reshape(-1).astype(jnp.int32))


def draw_tile_dst(key, part):
    return tile_lists(key)[0]


def draw_tile_src(key, part):
    return tile_lists(key)[1]


def draw_tile_edges(key, part):
    return tile_lists(key)[2]


def block_scale(own_key, dims, cuts, least, top_value):
    level, own = 1.0, jax.random.fold_in(own_key, 6)
    for axis_at, shards_of in cuts:
        draws = jnp.exp(jax.random.uniform(jax.random.fold_in(own, axis_at), (shards_of,), jnp.float32, least / len(cuts), top_value / len(cuts)))
        level = level * jnp.repeat(draws, dims[axis_at] // shards_of).reshape([-1 if axis == axis_at else 1 for axis in range(len(dims))])
    return level


def bell_draw(own_key, dims, spread, most, cuts=(), kind=jnp.bfloat16):
    gain = block_scale(own_key, dims, cuts, -0.22, 0.18) if cuts else 1.0
    drawn = jax.random.normal(own_key, dims, jnp.float32) * spread * gain
    return jnp.minimum(jnp.maximum(drawn, -most), most).astype(kind)


def setup_inputs(seed: int = 0) -> dict:
    splits = jax.random.split(jax.random.key(seed), 8)
    features_t = bell_draw(splits[0], (F, NODES), 1.0, 6.0, ((0, 32), (1, 16)))
    tile_dst = draw_tile_dst(jax.random.fold_in(splits[7], 71), 0)
    tile_src = draw_tile_src(jax.random.fold_in(splits[7], 71), 0)
    tile_edges = draw_tile_edges(jax.random.fold_in(splits[7], 71), 0)
    tile_values = bell_draw(splits[4], (TILES, TB, TB), TB ** -0.5, 0.5, ((0, 16),))
    weight = bell_draw(splits[5], (F, F), F ** -0.5, 0.1875, ((0, 32),))
    cotangent = bell_draw(splits[6], (F, NODES), 1.0, 6.0, ((0, 32), (1, 16)))
    return {"features_t": features_t, "tile_dst": tile_dst, "tile_src": tile_src, "tile_edges": tile_edges, "tile_values": tile_values, "weight": weight, "cotangent": cotangent}


def mix_table(dst, edges):
    onehot = (dst[None, :] == jnp.arange(BPD, dtype=jnp.int32)[:, None]).astype(jnp.float32)
    weights = edges.astype(jnp.float32)
    totals = jnp.sum(onehot * weights[None, :], axis=1)
    return onehot * weights[None, :] / totals[:, None]


def reference(features_t, tile_dst, tile_src, tile_edges, tile_values, weight, cotangent):
    groups = N_BLK
    dst_all = tile_dst.reshape(groups, NT)
    src_all = tile_src.reshape(groups, NT)
    edge_all = tile_edges.reshape(groups, NT)
    vals_all = tile_values.reshape(groups, NT, TB, TB)
    blocks = features_t.reshape(F, NBT, TB)

    def forward_group(items):
        dst, src, edges, vals = items
        mixing = mix_table(dst, edges)
        picked = jnp.take(blocks, src, axis=1).astype(jnp.float32)
        contrib = jnp.einsum("ctk,tjk->tcj", picked, vals.astype(jnp.float32))
        return jnp.einsum("bt,tcj->cbj", mixing, contrib, precision=lax.Precision.HIGHEST)

    agg_groups = lax.map(forward_group, (dst_all, src_all, edge_all, vals_all))
    aggregated = agg_groups.transpose(1, 0, 2, 3).reshape(F, NODES).astype(jnp.bfloat16)
    pre = jnp.dot(weight.T, aggregated, preferred_element_type=jnp.float32)
    activated = (pre * jax.nn.sigmoid(pre)).astype(jnp.bfloat16)
    sig = jax.nn.sigmoid(pre)
    grad_pre = (cotangent.astype(jnp.float32) * sig * (1.0 + pre * (1.0 - sig))).astype(jnp.bfloat16)
    grad_weight = jnp.dot(aggregated, grad_pre.T, preferred_element_type=jnp.float32)
    grad_agg = jnp.dot(weight, grad_pre, preferred_element_type=jnp.float32).astype(jnp.bfloat16)
    grad_blocks = grad_agg.reshape(F, N_BLK, BPD, TB)

    def backward_group(total, items):
        dst, src, edges, vals, index = items
        mixing = mix_table(dst, edges)
        coef = jnp.sum(mixing, axis=0)
        own = lax.dynamic_index_in_dim(grad_blocks, index, axis=1, keepdims=False)
        picked = jnp.take(own, dst, axis=1).astype(jnp.float32)
        contrib = jnp.einsum("ctj,tjk->tck", picked, vals.astype(jnp.float32))
        contrib = contrib * coef[:, None, None]
        return total + jax.ops.segment_sum(contrib, src, num_segments=NBT), None

    start = jnp.zeros((NBT, F, TB), jnp.float32)
    indices = jnp.arange(N_BLK, dtype=jnp.int32)
    total, _ = lax.scan(backward_group, start, (dst_all, src_all, edge_all, vals_all, indices))
    grad_features = total.transpose(1, 0, 2).reshape(F, NODES).astype(jnp.bfloat16)
    return activated, grad_weight, grad_features
```

```python
import functools

import jax
import jax.numpy as jnp
from jax import lax
from jax.experimental import pallas as pl
from jax.experimental.pallas import tpu as pltpu
from jax.sharding import PartitionSpec as P

FULL = dict(ZH=2, X=4, C=2, Y=4, ZL=8)
PER = 4
MESH = pl.DeviceIdType.MESH
BF = jnp.bfloat16
F32 = jnp.float32


def dot(a, b, ca, cb):
    return lax.dot_general(a, b, (((ca,), (cb,)), ((), ())), preferred_element_type=F32)


def shapes(cfg, rb, tb, nt):
    X, C, Y, ZL = cfg["X"], cfg["C"], cfg["Y"], cfg["ZL"]
    Q = X * C
    F = rb * Y * ZL
    qw = F // Q
    qy = Q // Y
    bpd = ZL
    x1, y1, z1 = max(X - 1, 1), max(Y - 1, 1), max(ZL - 1, 1)
    nk = -(-cfg["ZH"] * Q * PER // 128) * 128
    bufs = dict(
        fv=((rb, bpd * tb), BF),
        wv=((rb, F), BF),
        cv=((rb, bpd * tb), BF),
        dv=((1, nt), jnp.int32),
        sv=((1, nt), jnp.int32),
        ev=((1, nt), jnp.int32),
        itv=((8, nk), jnp.int32),
        ftv=((2 * bpd + 8, nk), F32),
        gown=((Q * bpd, rb, tb), BF),
        goth=((Q * bpd, rb, tb), BF),
        tv=((nt, tb, tb), BF),
        wb=((Q, rb, qw), BF),
        wg=((Q, ZL, rb, qw), BF),
        cb=((bpd, rb, tb), BF),
        ct=((ZL, rb, tb), BF),
        aggb=((bpd, rb, tb), BF),
        A=((ZL, rb, tb), BF),
        pps=((y1, qy, qw, tb), BF),
        ppr=((y1, qy, qw, tb), BF),
        GP=((Q, qw, tb), BF),
        actb=((ZL, rb, tb), BF),
        actr=((bpd, rb, tb), BF),
        gab=((ZL, rb, tb), BF),
        GA=((bpd, rb, tb), BF),
        PS=((X, ZL, rb, qw), BF),
        PO=((X, ZL, rb, qw), F32),
        PR=((X, ZL, rb, qw), BF),
        DXs=((x1, ZL, rb, qw), BF),
        DXr=((x1, ZL, rb, qw), BF),
        Sb=((ZL, rb, qw), BF),
        S32=((ZL, rb, qw), F32),
        DZr=((z1, rb, qw), BF),
        Ts=((rb, qw), F32),
        Tr=((rb, qw), F32),
        OutW=((Q, rb, qw), F32),
        Dsib0=((X, bpd, rb, tb), BF),
        Dsib1=((X, bpd, rb, tb), BF),
        Drec0=((X, bpd, rb, tb), BF),
        Drec1=((X, bpd, rb, tb), BF),
        Dkeep0=((X, bpd, rb, tb), F32),
        Dkeep1=((X, bpd, rb, tb), F32),
        EXs0=((x1, bpd, rb, tb), BF),
        EXs1=((x1, bpd, rb, tb), BF),
        EXr0=((x1, bpd, rb, tb), BF),
        EXr1=((x1, bpd, rb, tb), BF),
        FZs=((bpd, rb, tb), BF),
        FZr=((bpd, rb, tb), BF),
    )
    sems = dict(
        fz=1, fx0=x1, fx1=x1, fc0=X, fc1=X, w1=z1, w2=x1, w3=X, ct=z1, ag=z1, pp=y1, gp=y1, act=z1, ga=z1,
        p=1, dx=x1, dz=z1, dt=1, ow=2 * X, d0=1, d1=1, e0=x1, e1=x1, gz=1,
    )
    smem = dict(itab=((8, nk), jnp.int32), ftab=((2 * bpd + 8, nk), F32))
    return bufs, sems, smem


def tables(bpd, dst, src, edges, itv, ftv):
    nt = dst.shape[1]
    nk = itv.shape[1]
    r0 = lax.broadcasted_iota(jnp.int32, (nt, nt), 0)
    r1 = lax.broadcasted_iota(jnp.int32, (nt, nt), 1)
    k1 = lax.broadcasted_iota(jnp.int32, (nt, nk), 1)
    t0 = lax.broadcasted_iota(jnp.int32, (nt, nk), 0)
    lane = lax.broadcasted_iota(jnp.int32, (1, nt), 1)

    def column(row):
        return jnp.sum(jnp.where(r0 == r1, row, jnp.zeros_like(row)), axis=1, keepdims=True)

    bits = bpd.bit_length() - 1
    group = jnp.where((edges > 0) & (lane >= bpd), lax.shift_right_logical(src, bits), -1)
    group_c = column(group)
    rank = jnp.sum(jnp.where((group_c == group) & (r1 < r0), 1, 0), axis=1, keepdims=True)
    pick = jnp.where(group_c >= 0, group_c * PER + rank, -1) == k1

    def by_k(col):
        return jnp.sum(jnp.where(pick, col, jnp.zeros_like(col)), axis=0, keepdims=True)

    at_src, at_dst = by_k(column(src & (bpd - 1))), by_k(column(dst))
    itv[0:1] = by_k(t0)
    itv[1:2] = at_src
    itv[2:3] = at_dst
    blocks = lax.broadcasted_iota(jnp.int32, (bpd, nt), 0)
    weights = jnp.where(dst == blocks, edges.astype(F32), 0.0)
    coef = jnp.sum(weights / jnp.sum(weights, axis=1, keepdims=True), axis=0, keepdims=True)
    coef_k = by_k(column(coef))
    blocks = lax.broadcasted_iota(jnp.int32, (bpd, nk), 0)
    ftv[0:bpd] = jnp.where(at_dst == blocks, coef_k, 0.0)
    ftv[bpd:2 * bpd] = jnp.where(at_src == blocks, coef_k, 0.0)
    ftv[2 * bpd:2 * bpd + 1, 0:nt] = coef


def body(cfg, buf_names, sem_names, feat_hbm, tv_hbm, w_hbm, cot_hbm, dst_hbm, src_hbm, edge_hbm, act_o, gw_o, gf_o, *scr):
    ZH, X, C, Y, ZL = cfg["ZH"], cfg["X"], cfg["C"], cfg["Y"], cfg["ZL"]
    nb, ns = len(buf_names), len(sem_names)
    B = dict(zip(buf_names, scr[:nb]))
    SS = dict(zip(sem_names, scr[nb:nb + ns]))
    RS = dict(zip(sem_names, scr[nb + ns:nb + 2 * ns]))
    load_sem, itab, ftab = scr[nb + 2 * ns:]
    feat, w, cot = B["fv"], B["wv"], B["cv"]
    Q = X * C
    bpd = ZL
    rb, tb = B["A"].shape[1:]
    qw = B["wb"].shape[2]
    qy = Q // Y
    rows = ZL * rb

    blk, rep = lax.axis_index("blk"), lax.axis_index("rep")
    zh = lax.div(blk, Q)
    me = lax.rem(blk, Q)
    x, c = lax.div(me, C), lax.rem(me, C)
    y, zl = lax.div(rep, ZL), lax.rem(rep, ZL)
    zo, co = 1 - zh, 1 - c

    def dev(zh_=zh, x_=x, c_=c, y_=y, zl_=zl):
        return ((zh_ * X + x_) * C + c_, y_ * ZL + zl_)

    def up(v, d, n):
        return lax.rem(v + d, n)

    def down(v, d, n):
        return lax.rem(v + n - d, n)

    anti, sib = dev(zh_=zo), dev(c_=co)
    sent = []

    def send(src, dst, name, i, to):
        cp = pltpu.make_async_remote_copy(
            src_ref=src, dst_ref=dst, send_sem=SS[name].at[i], recv_sem=RS[name].at[i],
            device_id=to, device_id_type=MESH,
        )
        cp.start()
        sent.append(cp)

    def got(dst, name, i):
        pltpu.make_async_remote_copy(
            src_ref=dst, dst_ref=dst, send_sem=SS[name].at[i], recv_sem=RS[name].at[i],
            device_id=sib, device_id_type=MESH,
        ).wait_recv()

    loads = [
        pltpu.make_async_copy(a, b, load_sem.at[i])
        for i, (a, b) in enumerate((
            (feat_hbm, feat), (w_hbm, w), (cot_hbm, cot), (tv_hbm, B["tv"]),
            (dst_hbm, B["dv"]), (src_hbm, B["sv"]), (edge_hbm, B["ev"]),
        ))
    ]
    for ld in loads:
        ld.start()

    barrier = pltpu.get_barrier_semaphore()
    partners = [anti]
    partners += [dev(x_=up(x, d, X), c_=(c if e == 0 else co)) for d in range(X) for e in range(C) if d or e]
    partners += [dev(zl_=up(zl, d, ZL)) for d in range(1, ZL)]
    partners += [dev(y_=up(y, d, Y)) for d in range(1, Y)]
    for p in partners:
        pl.semaphore_signal(barrier, inc=1, device_id=p, device_id_type=MESH)

    gown, goth, tv = B["gown"], B["goth"], B["tv"]
    loads[0].wait()
    for b in range(bpd):
        gown[me * bpd + b] = feat[:, b * tb:(b + 1) * tb]
    pl.semaphore_wait(barrier, len(partners))

    def seg(m):
        return pl.ds(m * bpd, bpd)

    mine = seg(me)
    send(gown.at[mine], goth.at[mine], "fz", 0, anti)
    for d in range(1, X):
        send(gown.at[mine], gown.at[mine], "fx0", d - 1, dev(x_=up(x, d, X)))
    send(gown.at[mine], gown.at[mine], "fc0", 0, sib)
    for ld in loads[4:]:
        ld.wait()
    tables(bpd, B["dv"][...], B["sv"][...], B["ev"][...], B["itv"], B["ftv"])
    to_smem = [
        pltpu.make_async_copy(B["itv"], itab, load_sem.at[7]),
        pltpu.make_async_copy(B["ftv"], ftab, load_sem.at[8]),
    ]
    for cp in to_smem:
        cp.start()
    loads[1].wait()
    loads[2].wait()
    for b in range(bpd):
        B["cb"][b] = cot[:, b * tb:(b + 1) * tb]
    for q in range(Q):
        B["wb"][q] = w[:, q * qw:(q + 1) * qw]
    B["wg"][me, zl] = B["wb"][me]
    B["ct"][zl] = B["cb"][zl]
    wg, wb = B["wg"], B["wb"]
    for d in range(1, ZL):
        z = up(zl, d, ZL)
        send(wb.at[me], wg.at[me, zl], "w1", d - 1, dev(zl_=z))
    for d in range(1, X):
        part = gown.at[seg(down(x, d, X) * C + c)]
        got(part, "fx0", d - 1)
        send(part, part, "fc0", d, sib)
    loads[3].wait()
    for cp in to_smem:
        cp.wait()
    acc = tuple(ftab[2 * bpd, b] * dot(gown[me * bpd + b], tv[b], 1, 1) for b in range(bpd))

    def forward(g, half, m, acc):
        acc = list(acc)
        for j in range(PER):
            k = (half * Q + m) * PER + j
            out = dot(g[m * bpd + itab[1, k]], tv[itab[0, k]], 1, 1)
            for b in range(bpd):
                acc[b] = acc[b] + ftab[b, k] * out
        return tuple(acc)

    got(goth.at[mine], "fz", 0)
    for d in range(1, X):
        send(goth.at[mine], goth.at[mine], "fx1", d - 1, dev(x_=up(x, d, X)))
    send(goth.at[mine], goth.at[mine], "fc1", 0, sib)
    for d in range(X):
        got(gown.at[seg(down(x, d, X) * C + co)], "fc0", d)
    acc = lax.fori_loop(1, Q, lambda d, a: forward(gown, zh, lax.rem(me + d, Q), a), acc)
    for d in range(1, X):
        part = goth.at[seg(down(x, d, X) * C + c)]
        got(part, "fx1", d - 1)
        send(part, part, "fc1", d, sib)
    for d in range(1, ZL):
        got(wg.at[me, down(zl, d, ZL)], "w1", d - 1)
    for d in range(1, X):
        send(wg.at[me], wg.at[me], "w2", d - 1, dev(x_=up(x, d, X)))
    send(wg.at[me], wg.at[me], "w3", 0, sib)
    for d in range(X):
        got(goth.at[seg(down(x, d, X) * C + co)], "fc1", d)
    acc = lax.fori_loop(0, Q, lambda m, a: forward(goth, zo, m, a), acc)

    A = B["A"]
    for b in range(bpd):
        B["aggb"][b] = acc[b].astype(BF)
    A[zl] = B["aggb"][zl]
    for d in range(1, ZL):
        z = up(zl, d, ZL)
        send(B["aggb"].at[z], A.at[zl], "ag", d - 1, dev(zl_=z))
    for d in range(1, ZL):
        z = up(zl, d, ZL)
        send(B["cb"].at[z], B["ct"].at[zl], "ct", d - 1, dev(zl_=z))
    for d in range(1, X):
        part = wg.at[down(x, d, X) * C + c]
        got(part, "w2", d - 1)
        send(part, part, "w3", d, sib)
    for d in range(X):
        got(wg.at[down(x, d, X) * C + co], "w3", d)
    for d in range(1, ZL):
        got(A.at[down(zl, d, ZL)], "ag", d - 1)

    a2 = A[...].reshape(rows, tb)

    def pre_part(y_, i):
        return dot(wg[y_ * qy + i].reshape(rows, qw), a2, 0, 0)

    pps, ppr, GP = B["pps"], B["ppr"], B["GP"]
    for d in range(1, Y):
        y_ = up(y, d, Y)
        for i in range(qy):
            pps[d - 1, i] = pre_part(y_, i).astype(BF)
        send(pps.at[d - 1], ppr.at[d - 1], "pp", d - 1, dev(y_=y_))
    pre = jnp.concatenate([pre_part(y, i) for i in range(qy)], axis=0)
    for d in range(1, ZL):
        got(B["ct"].at[down(zl, d, ZL)], "ct", d - 1)
    cotangent = B["ct"][...].reshape(rows, tb).astype(F32)
    for d in range(1, Y):
        got(ppr.at[d - 1], "pp", d - 1)
        pre = pre + ppr[d - 1].reshape(rows, tb).astype(F32)
    sig = jax.nn.sigmoid(pre)
    gp = (cotangent * sig * (1.0 + pre * (1.0 - sig))).astype(BF).reshape(qy, qw, tb)
    for i in range(qy):
        GP[y * qy + i] = gp[i]
    for d in range(1, Y):
        part = GP.at[pl.ds(y * qy, qy)]
        send(part, part, "gp", d - 1, dev(y_=up(y, d, Y)))
    actb, actr = B["actb"], B["actr"]
    actb[...] = (pre * sig).astype(BF).reshape(ZL, rb, tb)
    actr[zl] = actb[zl]
    for d in range(1, ZL):
        z = up(zl, d, ZL)
        send(actb.at[z], actr.at[zl], "act", d - 1, dev(zl_=z))
    for d in range(1, Y):
        got(GP.at[pl.ds(down(y, d, Y) * qy, qy)], "gp", d - 1)

    ga = dot(wg[0].reshape(rows, qw), GP[0], 1, 0)
    for q in range(1, Q):
        ga = ga + dot(wg[q].reshape(rows, qw), GP[q], 1, 0)
    gab, GA = B["gab"], B["GA"]
    gab[...] = ga.astype(BF).reshape(ZL, rb, tb)
    GA[zl] = gab[zl]
    for d in range(1, ZL):
        z = up(zl, d, ZL)
        send(gab.at[z], GA.at[zl], "ga", d - 1, dev(zl_=z))

    PS, PO, PR = B["PS"], B["PO"], B["PR"]
    for i in range(X):
        PS[i] = dot(a2, GP[i * C + co], 1, 1).astype(BF).reshape(ZL, rb, qw)
    send(PS, PR, "p", 0, sib)
    for i in range(X):
        PO[i] = dot(a2, GP[i * C + c], 1, 1).reshape(ZL, rb, qw)
    got(PR, "p", 0)
    DXs, DXr = B["DXs"], B["DXr"]
    for d in range(1, X):
        x_ = up(x, d, X)
        DXs[d - 1] = (PO[x_] + PR[x_].astype(F32)).astype(BF)
        send(DXs.at[d - 1], DXr.at[d - 1], "dx", d - 1, dev(x_=x_))
    for d in range(1, ZL):
        got(GA.at[down(zl, d, ZL)], "ga", d - 1)

    def backward(half, m):
        outs = [None] * bpd
        for j in range(PER):
            k = (half * Q + m) * PER + j
            back = dot(GA[itab[2, k]], tv[itab[0, k]], 1, 0)
            for b in range(bpd):
                term = ftab[bpd + b, k] * back
                outs[b] = term if j == 0 else outs[b] + term
        return outs

    def contribute(half, core, start, stop, at, into):
        def step(i, carry):
            i = at(i)
            for b, out in enumerate(backward(half, i * C + core)):
                into[i, b] = out.astype(into.dtype)
            return carry
        lax.fori_loop(start, stop, step, 0)

    Dsib, Drec, Dkeep = (B["Dsib0"], B["Dsib1"]), (B["Drec0"], B["Drec1"]), (B["Dkeep0"], B["Dkeep1"])
    EXs, EXr = (B["EXs0"], B["EXs1"]), (B["EXr0"], B["EXr1"])

    def to_x(n):
        got(Drec[n], "d%d" % n, 0)
        for d in range(1, X):
            x_ = up(x, d, X)
            EXs[n][d - 1] = (Dkeep[n][x_] + Drec[n][x_].astype(F32)).astype(BF)
            send(EXs[n].at[d - 1], EXr[n].at[d - 1], "e%d" % n, d - 1, dev(x_=x_))

    def from_x(n):
        total = Dkeep[n][x] + Drec[n][x].astype(F32)
        for d in range(1, X):
            got(EXr[n].at[d - 1], "e%d" % n, d - 1)
            total = total + EXr[n][d - 1].astype(F32)
        return total

    contribute(zo, co, 0, X, lambda i: i, Dsib[0])
    send(Dsib[0], Drec[0], "d0", 0, sib)
    contribute(zo, c, 0, X, lambda i: i, Dkeep[0])

    to_x(0)
    S32, Sb, DZr = B["S32"], B["Sb"], B["DZr"]
    total = PO[x] + PR[x].astype(F32)
    for d in range(1, X):
        got(DXr.at[d - 1], "dx", d - 1)
        total = total + DXr[d - 1].astype(F32)
    S32[...] = total
    Sb[...] = total.astype(BF)
    for d in range(1, ZL):
        z = up(zl, d, ZL)
        send(Sb.at[z], DZr.at[d - 1], "dz", d - 1, dev(zl_=z))
    contribute(zh, co, 0, X, lambda i: i, Dsib[1])
    send(Dsib[1], Drec[1], "d1", 0, sib)
    contribute(zh, c, 1, X, lambda i: lax.rem(x + i, X), Dkeep[1])
    for b in range(bpd):
        Dkeep[1][x, b] = ftab[2 * bpd, b] * dot(GA[b], tv[b], 1, 0)
    FZs, FZr = B["FZs"], B["FZr"]
    FZs[...] = from_x(0).astype(BF)
    send(FZs, FZr, "gz", 0, anti)

    total = S32[zl]
    for d in range(1, ZL):
        got(DZr.at[d - 1], "dz", d - 1)
        total = total + DZr[d - 1].astype(F32)
    Ts, Tr, OutW = B["Ts"], B["Tr"], B["OutW"]
    Ts[...] = total
    send(Ts, Tr, "dt", 0, anti)
    to_x(1)
    for d in range(1, ZL):
        got(actr.at[down(zl, d, ZL)], "act", d - 1)
    for b in range(bpd):
        act_o[:, b * tb:(b + 1) * tb] = actr[b]
    got(Tr, "dt", 0)
    OutW[me] = Ts[...] + Tr[...]
    others = [(d, e) for d in range(X) for e in range(C) if d or e]
    for n, (d, e) in enumerate(others):
        to = dev(x_=up(x, d, X), c_=(co if e else c))
        send(OutW.at[me], OutW.at[me], "ow", n, to)
    own = from_x(1)
    for n, (d, e) in enumerate(others):
        got(OutW.at[down(x, d, X) * C + (co if e else c)], "ow", n)
    for q in range(Q):
        gw_o[:, q * qw:(q + 1) * qw] = OutW[q]
    got(FZr, "gz", 0)
    own = (own + FZr[...].astype(F32)).astype(BF)
    for b in range(bpd):
        gf_o[:, b * tb:(b + 1) * tb] = own[b]
    for cp in sent:
        cp.wait_send()


def hand_over(*refs):
    sem = refs[-1]
    n = (len(refs) - 1) // 2
    copies = [pltpu.make_async_copy(refs[i], refs[n + i], sem.at[i]) for i in range(n)]
    for cp in copies:
        cp.start()
    for cp in copies:
        cp.wait()


def on_device(cfg, features_t, tile_dst, tile_src, tile_edges, tile_values, weight, cotangent):
    rb = features_t.shape[0]
    nt, tb = tile_values.shape[:2]
    bufs, sems, smem = shapes(cfg, rb, tb, nt)
    vm, hbm = pl.BlockSpec(memory_space=pltpu.VMEM), pl.BlockSpec(memory_space=pltpu.HBM)
    kernel = functools.partial(body, cfg, tuple(bufs), tuple(sems))
    outs = (
        jax.ShapeDtypeStruct(features_t.shape, BF),
        jax.ShapeDtypeStruct(weight.shape, F32),
        jax.ShapeDtypeStruct(features_t.shape, BF),
    )
    results = pl.pallas_call(
        kernel,
        out_shape=outs,
        in_specs=[hbm] * 7,
        out_specs=(vm, vm, vm),
        scratch_shapes=[pltpu.VMEM(s, t) for s, t in bufs.values()]
        + [pltpu.SemaphoreType.DMA((n,)) for n in sems.values()] * 2
        + [pltpu.SemaphoreType.DMA((9,))]
        + [pltpu.SMEM(s, t) for s, t in smem.values()],
        compiler_params=pltpu.CompilerParams(
            collective_id=0, has_side_effects=True, vmem_limit_bytes=63 * 1024 * 1024
        ),
        name="graph_conv",
    )(features_t, tile_values, weight, cotangent, *(v.reshape(1, nt) for v in (tile_dst, tile_src, tile_edges)))
    return pl.pallas_call(
        hand_over,
        out_shape=outs,
        in_specs=[hbm] * len(outs),
        out_specs=(hbm,) * len(outs),
        scratch_shapes=[pltpu.SemaphoreType.DMA((len(outs),))],
        compiler_params=pltpu.CompilerParams(vmem_limit_bytes=63 * 1024 * 1024),
        name="hand_over",
    )(*results)


def solution(mesh, cfg=None):
    in_specs = (
        P("rep", "blk"),
        P("blk"),
        P("blk"),
        P("blk"),
        P("blk", None, None),
        P("rep", None),
        P("rep", "blk"),
    )
    out_specs = (P("rep", "blk"), P("rep", None), P("rep", "blk"))
    return jax.shard_map(
        functools.partial(on_device, cfg or FULL), mesh=mesh, in_specs=in_specs, out_specs=out_specs, check_vma=False
    )
```

```python
import functools

import jax
import jax.numpy as jnp
from jax import lax
from jax.experimental import pallas as pl
from jax.experimental.pallas import tpu as pltpu
from jax.sharding import PartitionSpec as P

FULL = dict(ZH=2, X=4, C=2, Y=4, ZL=8)
PER = 4
MESH = pl.DeviceIdType.MESH
BF = jnp.bfloat16
F32 = jnp.float32


def dot(a, b, ca, cb):
    return lax.dot_general(a, b, (((ca,), (cb,)), ((), ())), preferred_element_type=F32)


def shapes(cfg, rb, tb, nt):
    X, C, Y, ZL = cfg["X"], cfg["C"], cfg["Y"], cfg["ZL"]
    Q = X * C
    F = rb * Y * ZL
    qw = F // Q
    qy = Q // Y
    bpd = ZL
    x1, y1, z1 = max(X - 1, 1), max(Y - 1, 1), max(ZL - 1, 1)
    nk = -(-cfg["ZH"] * Q * PER // 128) * 128
    bufs = dict(
        fv=((rb, bpd * tb), BF),
        wv=((rb, F), BF),
        cv=((rb, bpd * tb), BF),
        dv=((1, nt), jnp.int32),
        sv=((1, nt), jnp.int32),
        ev=((1, nt), jnp.int32),
        itv=((8, nk), jnp.int32),
        ftv=((2 * bpd + 8, nk), F32),
        gown=((Q * bpd, rb, tb), BF),
        goth=((Q * bpd, rb, tb), BF),
        tv=((nt, tb, tb), BF),
        wb=((Q, rb, qw), BF),
        wg=((Q, ZL, rb, qw), BF),
        cb=((bpd, rb, tb), BF),
        ct=((ZL, rb, tb), BF),
        aggb=((bpd, rb, tb), BF),
        A=((ZL, rb, tb), BF),
        pps=((y1, qy, qw, tb), BF),
        ppr=((y1, qy, qw, tb), BF),
        GP=((Q, qw, tb), BF),
        actb=((ZL, rb, tb), BF),
        actr=((bpd, rb, tb), BF),
        gab=((ZL, rb, tb), BF),
        GA=((bpd, rb, tb), BF),
        PS=((X, ZL, rb, qw), BF),
        PO=((X, ZL, rb, qw), F32),
        PR=((X, ZL, rb, qw), BF),
        DXs=((x1, ZL, rb, qw), BF),
        DXr=((x1, ZL, rb, qw), BF),
        Sb=((ZL, rb, qw), BF),
        S32=((ZL, rb, qw), F32),
        DZr=((z1, rb, qw), BF),
        Ts=((rb, qw), F32),
        Tr=((rb, qw), F32),
        OutW=((Q, rb, qw), F32),
        Dsib0=((X, bpd, rb, tb), BF),
        Dsib1=((X, bpd, rb, tb), BF),
        Drec0=((X, bpd, rb, tb), BF),
        Drec1=((X, bpd, rb, tb), BF),
        Dkeep0=((X, bpd, rb, tb), F32),
        Dkeep1=((X, bpd, rb, tb), F32),
        EXs0=((x1, bpd, rb, tb), BF),
        EXs1=((x1, bpd, rb, tb), BF),
        EXr0=((x1, bpd, rb, tb), BF),
        EXr1=((x1, bpd, rb, tb), BF),
        FZs=((bpd, rb, tb), BF),
        FZr=((bpd, rb, tb), BF),
    )
    sems = dict(
        fz=1, fx0=x1, fx1=x1, fc0=X, fc1=X, w1=z1, w2=x1, w3=X, ct=z1, ag=z1, pp=y1, gp=y1, act=z1, ga=z1,
        p=1, dx=x1, dz=z1, dt=1, ow=2 * X, d0=1, d1=1, e0=2 * x1, e1=x1, gz=2,
    )
    smem = dict(itab=((8, nk), jnp.int32), ftab=((2 * bpd + 8, nk), F32))
    return bufs, sems, smem


def tables(bpd, dst, src, edges, itv, ftv):
    nt = dst.shape[1]
    nk = itv.shape[1]
    r0 = lax.broadcasted_iota(jnp.int32, (nt, nt), 0)
    r1 = lax.broadcasted_iota(jnp.int32, (nt, nt), 1)
    k1 = lax.broadcasted_iota(jnp.int32, (nt, nk), 1)
    t0 = lax.broadcasted_iota(jnp.int32, (nt, nk), 0)
    lane = lax.broadcasted_iota(jnp.int32, (1, nt), 1)

    def column(row):
        return jnp.sum(jnp.where(r0 == r1, row, jnp.zeros_like(row)), axis=1, keepdims=True)

    bits = bpd.bit_length() - 1
    group = jnp.where((edges > 0) & (lane >= bpd), lax.shift_right_logical(src, bits), -1)
    group_c = column(group)
    rank = jnp.sum(jnp.where((group_c == group) & (r1 < r0), 1, 0), axis=1, keepdims=True)
    pick = jnp.where(group_c >= 0, group_c * PER + rank, -1) == k1

    def by_k(col):
        return jnp.sum(jnp.where(pick, col, jnp.zeros_like(col)), axis=0, keepdims=True)

    at_src, at_dst = by_k(column(src & (bpd - 1))), by_k(column(dst))
    itv[0:1] = by_k(t0)
    itv[1:2] = at_src
    itv[2:3] = at_dst
    blocks = lax.broadcasted_iota(jnp.int32, (bpd, nt), 0)
    weights = jnp.where(dst == blocks, edges.astype(F32), 0.0)
    coef = jnp.sum(weights / jnp.sum(weights, axis=1, keepdims=True), axis=0, keepdims=True)
    coef_k = by_k(column(coef))
    blocks = lax.broadcasted_iota(jnp.int32, (bpd, nk), 0)
    ftv[0:bpd] = jnp.where(at_dst == blocks, coef_k, 0.0)
    ftv[bpd:2 * bpd] = jnp.where(at_src == blocks, coef_k, 0.0)
    ftv[2 * bpd:2 * bpd + 1, 0:nt] = coef


def body(cfg, buf_names, sem_names, feat_hbm, tv_hbm, w_hbm, cot_hbm, dst_hbm, src_hbm, edge_hbm, act_o, gw_o, gf_o, *scr):
    ZH, X, C, Y, ZL = cfg["ZH"], cfg["X"], cfg["C"], cfg["Y"], cfg["ZL"]
    nb, ns = len(buf_names), len(sem_names)
    B = dict(zip(buf_names, scr[:nb]))
    SS = dict(zip(sem_names, scr[nb:nb + ns]))
    RS = dict(zip(sem_names, scr[nb + ns:nb + 2 * ns]))
    load_sem, itab, ftab = scr[nb + 2 * ns:]
    feat, w, cot = B["fv"], B["wv"], B["cv"]
    Q = X * C
    bpd = ZL
    rb, tb = B["A"].shape[1:]
    qw = B["wb"].shape[2]
    qy = Q // Y
    rows = ZL * rb

    blk, rep = lax.axis_index("blk"), lax.axis_index("rep")
    zh = lax.div(blk, Q)
    me = lax.rem(blk, Q)
    x, c = lax.div(me, C), lax.rem(me, C)
    y, zl = lax.div(rep, ZL), lax.rem(rep, ZL)
    zo, co = 1 - zh, 1 - c

    def dev(zh_=zh, x_=x, c_=c, y_=y, zl_=zl):
        return ((zh_ * X + x_) * C + c_, y_ * ZL + zl_)

    def up(v, d, n):
        return lax.rem(v + d, n)

    def down(v, d, n):
        return lax.rem(v + n - d, n)

    anti, sib = dev(zh_=zo), dev(c_=co)
    sent = []

    def send(src, dst, name, i, to):
        cp = pltpu.make_async_remote_copy(
            src_ref=src, dst_ref=dst, send_sem=SS[name].at[i], recv_sem=RS[name].at[i],
            device_id=to, device_id_type=MESH,
        )
        cp.start()
        sent.append(cp)

    def got(dst, name, i):
        pltpu.make_async_remote_copy(
            src_ref=dst, dst_ref=dst, send_sem=SS[name].at[i], recv_sem=RS[name].at[i],
            device_id=sib, device_id_type=MESH,
        ).wait_recv()

    loads = [
        pltpu.make_async_copy(a, b, load_sem.at[i])
        for i, (a, b) in enumerate((
            (feat_hbm, feat), (w_hbm, w), (cot_hbm, cot), (tv_hbm, B["tv"]),
            (dst_hbm, B["dv"]), (src_hbm, B["sv"]), (edge_hbm, B["ev"]),
        ))
    ]
    for ld in loads:
        ld.start()

    barrier = pltpu.get_barrier_semaphore()
    partners = [anti]
    partners += [dev(x_=up(x, d, X), c_=(c if e == 0 else co)) for d in range(X) for e in range(C) if d or e]
    partners += [dev(zl_=up(zl, d, ZL)) for d in range(1, ZL)]
    partners += [dev(y_=up(y, d, Y)) for d in range(1, Y)]
    for p in partners:
        pl.semaphore_signal(barrier, inc=1, device_id=p, device_id_type=MESH)

    gown, goth, tv = B["gown"], B["goth"], B["tv"]
    loads[0].wait()
    for b in range(bpd):
        gown[me * bpd + b] = feat[:, b * tb:(b + 1) * tb]
    pl.semaphore_wait(barrier, len(partners))

    def seg(m):
        return pl.ds(m * bpd, bpd)

    mine = seg(me)
    send(gown.at[mine], goth.at[mine], "fz", 0, anti)
    for d in range(1, X):
        send(gown.at[mine], gown.at[mine], "fx0", d - 1, dev(x_=up(x, d, X)))
    send(gown.at[mine], gown.at[mine], "fc0", 0, sib)
    for ld in loads[4:]:
        ld.wait()
    tables(bpd, B["dv"][...], B["sv"][...], B["ev"][...], B["itv"], B["ftv"])
    to_smem = [
        pltpu.make_async_copy(B["itv"], itab, load_sem.at[7]),
        pltpu.make_async_copy(B["ftv"], ftab, load_sem.at[8]),
    ]
    for cp in to_smem:
        cp.start()
    loads[1].wait()
    loads[2].wait()
    for b in range(bpd):
        B["cb"][b] = cot[:, b * tb:(b + 1) * tb]
    for q in range(Q):
        B["wb"][q] = w[:, q * qw:(q + 1) * qw]
    B["wg"][me, zl] = B["wb"][me]
    B["ct"][zl] = B["cb"][zl]
    wg, wb = B["wg"], B["wb"]
    for d in range(1, ZL):
        z = up(zl, d, ZL)
        send(wb.at[me], wg.at[me, zl], "w1", d - 1, dev(zl_=z))
    for d in range(1, X):
        part = gown.at[seg(down(x, d, X) * C + c)]
        got(part, "fx0", d - 1)
        send(part, part, "fc0", d, sib)
    loads[3].wait()
    for cp in to_smem:
        cp.wait()
    acc = tuple(ftab[2 * bpd, b] * dot(gown[me * bpd + b], tv[b], 1, 1) for b in range(bpd))

    def forward(g, half, i, acc):
        acc = list(acc)
        for j in range(C * PER):
            m = i * C + j // PER
            k = (half * Q + i * C) * PER + j
            out = dot(g[m * bpd + itab[1, k]], tv[itab[0, k]], 1, 1)
            for b in range(bpd):
                acc[b] = acc[b] + ftab[b, k] * out
        return tuple(acc)

    got(goth.at[mine], "fz", 0)
    for d in range(1, X):
        send(goth.at[mine], goth.at[mine], "fx1", d - 1, dev(x_=up(x, d, X)))
    send(goth.at[mine], goth.at[mine], "fc1", 0, sib)
    for d in range(X):
        got(gown.at[seg(down(x, d, X) * C + co)], "fc0", d)
    acc = lax.fori_loop(0, Q // C, lambda i, a: forward(gown, zh, i, a), acc)
    for d in range(1, X):
        part = goth.at[seg(down(x, d, X) * C + c)]
        got(part, "fx1", d - 1)
        send(part, part, "fc1", d, sib)
    for d in range(1, ZL):
        got(wg.at[me, down(zl, d, ZL)], "w1", d - 1)
    for d in range(1, X):
        send(wg.at[me], wg.at[me], "w2", d - 1, dev(x_=up(x, d, X)))
    send(wg.at[me], wg.at[me], "w3", 0, sib)
    for d in range(X):
        got(goth.at[seg(down(x, d, X) * C + co)], "fc1", d)
    acc = lax.fori_loop(0, Q // C, lambda i, a: forward(goth, zo, i, a), acc)

    A = B["A"]
    for b in range(bpd):
        B["aggb"][b] = acc[b].astype(BF)
    A[zl] = B["aggb"][zl]
    for d in range(1, ZL):
        z = up(zl, d, ZL)
        send(B["aggb"].at[z], A.at[zl], "ag", d - 1, dev(zl_=z))
    for d in range(1, ZL):
        z = up(zl, d, ZL)
        send(B["cb"].at[z], B["ct"].at[zl], "ct", d - 1, dev(zl_=z))
    for d in range(1, X):
        part = wg.at[down(x, d, X) * C + c]
        got(part, "w2", d - 1)
        send(part, part, "w3", d, sib)
    for d in range(X):
        got(wg.at[down(x, d, X) * C + co], "w3", d)
    for d in range(1, ZL):
        got(A.at[down(zl, d, ZL)], "ag", d - 1)

    a2 = A[...].reshape(rows, tb)

    def pre_part(y_, i):
        return dot(wg[y_ * qy + i].reshape(rows, qw), a2, 0, 0)

    pps, ppr, GP = B["pps"], B["ppr"], B["GP"]
    for d in range(1, Y):
        y_ = up(y, d, Y)
        for i in range(qy):
            pps[d - 1, i] = pre_part(y_, i).astype(BF)
        send(pps.at[d - 1], ppr.at[d - 1], "pp", d - 1, dev(y_=y_))
    pre = jnp.concatenate([pre_part(y, i) for i in range(qy)], axis=0)
    for d in range(1, ZL):
        got(B["ct"].at[down(zl, d, ZL)], "ct", d - 1)
    cotangent = B["ct"][...].reshape(rows, tb).astype(F32)
    for d in range(1, Y):
        got(ppr.at[d - 1], "pp", d - 1)
        pre = pre + ppr[d - 1].reshape(rows, tb).astype(F32)
    sig = jax.nn.sigmoid(pre)
    gp = (cotangent * sig * (1.0 + pre * (1.0 - sig))).astype(BF).reshape(qy, qw, tb)
    for i in range(qy):
        GP[y * qy + i] = gp[i]
    for d in range(1, Y):
        part = GP.at[pl.ds(y * qy, qy)]
        send(part, part, "gp", d - 1, dev(y_=up(y, d, Y)))
    actb, actr = B["actb"], B["actr"]
    actb[...] = (pre * sig).astype(BF).reshape(ZL, rb, tb)
    actr[zl] = actb[zl]
    for d in range(1, ZL):
        z = up(zl, d, ZL)
        send(actb.at[z], actr.at[zl], "act", d - 1, dev(zl_=z))
    for d in range(1, Y):
        got(GP.at[pl.ds(down(y, d, Y) * qy, qy)], "gp", d - 1)

    ga = dot(wg[0].reshape(rows, qw), GP[0], 1, 0)
    for q in range(1, Q):
        ga = ga + dot(wg[q].reshape(rows, qw), GP[q], 1, 0)
    gab, GA = B["gab"], B["GA"]
    gab[...] = ga.astype(BF).reshape(ZL, rb, tb)
    GA[zl] = gab[zl]
    for d in range(1, ZL):
        z = up(zl, d, ZL)
        send(gab.at[z], GA.at[zl], "ga", d - 1, dev(zl_=z))

    PS, PO, PR = B["PS"], B["PO"], B["PR"]
    for i in range(X):
        PS[i] = dot(a2, GP[i * C + co], 1, 1).astype(BF).reshape(ZL, rb, qw)
    send(PS, PR, "p", 0, sib)
    for i in range(X):
        PO[i] = dot(a2, GP[i * C + c], 1, 1).reshape(ZL, rb, qw)
    got(PR, "p", 0)
    DXs, DXr = B["DXs"], B["DXr"]
    for d in range(1, X):
        x_ = up(x, d, X)
        DXs[d - 1] = (PO[x_] + PR[x_].astype(F32)).astype(BF)
        send(DXs.at[d - 1], DXr.at[d - 1], "dx", d - 1, dev(x_=x_))
    for d in range(1, ZL):
        got(GA.at[down(zl, d, ZL)], "ga", d - 1)

    def backward(half, m):
        outs = [None] * bpd
        for j in range(PER):
            k = (half * Q + m) * PER + j
            back = dot(GA[itab[2, k]], tv[itab[0, k]], 1, 0)
            for b in range(bpd):
                term = ftab[bpd + b, k] * back
                outs[b] = term if j == 0 else outs[b] + term
        return outs

    def contribute(half, core, into):
        step = 2 if X % 2 == 0 else 1

        def some(i, carry):
            for n in range(step):
                for b, out in enumerate(backward(half, (i * step + n) * C + core)):
                    into[i * step + n, b] = out.astype(into.dtype)
            return carry
        lax.fori_loop(0, X // step, some, 0)

    Dsib, Drec, Dkeep = (B["Dsib0"], B["Dsib1"]), (B["Drec0"], B["Drec1"]), (B["Dkeep0"], B["Dkeep1"])
    EXs, EXr = (B["EXs0"], B["EXs1"]), (B["EXr0"], B["EXr1"])

    parts = 2 if bpd % 2 == 0 else 1

    def cut(i):
        return pl.ds(i * (bpd // parts), bpd // parts)

    whole = pl.ds(0, bpd)

    def to_x(n, at=whole, i=0):
        for d in range(1, X):
            x_ = up(x, d, X)
            EXs[n][d - 1, at] = (Dkeep[n][x_, at] + Drec[n][x_, at].astype(F32)).astype(BF)
            send(EXs[n].at[d - 1, at], EXr[n].at[d - 1, at], "e%d" % n, i * (X - 1) + d - 1, dev(x_=x_))

    def from_x(n, at=whole, i=0):
        total = Dkeep[n][x, at] + Drec[n][x, at].astype(F32)
        for d in range(1, X):
            got(EXr[n].at[d - 1, at], "e%d" % n, i * (X - 1) + d - 1)
            total = total + EXr[n][d - 1, at].astype(F32)
        return total

    contribute(zo, co, Dsib[0])
    send(Dsib[0], Drec[0], "d0", 0, sib)
    contribute(zo, c, Dkeep[0])

    got(Drec[0], "d0", 0)
    for i in range(parts):
        to_x(0, cut(i), i)
    S32, Sb, DZr = B["S32"], B["Sb"], B["DZr"]
    total = PO[x] + PR[x].astype(F32)
    for d in range(1, X):
        got(DXr.at[d - 1], "dx", d - 1)
        total = total + DXr[d - 1].astype(F32)
    S32[...] = total
    Sb[...] = total.astype(BF)
    for d in range(1, ZL):
        z = up(zl, d, ZL)
        send(Sb.at[z], DZr.at[d - 1], "dz", d - 1, dev(zl_=z))
    contribute(zh, co, Dsib[1])
    send(Dsib[1], Drec[1], "d1", 0, sib)
    contribute(zh, c, Dkeep[1])
    for b in range(bpd):
        Dkeep[1][x, b] = ftab[2 * bpd, b] * dot(GA[b], tv[b], 1, 0)
    total = S32[zl]
    for d in range(1, ZL):
        got(DZr.at[d - 1], "dz", d - 1)
        total = total + DZr[d - 1].astype(F32)
    Ts, Tr, OutW = B["Ts"], B["Tr"], B["OutW"]
    Ts[...] = total
    send(Ts, Tr, "dt", 0, anti)
    FZs, FZr = B["FZs"], B["FZr"]
    for i in range(parts):
        at = cut(i)
        FZs[at] = from_x(0, at, i).astype(BF)
        send(FZs.at[at], FZr.at[at], "gz", i, anti)
    got(Drec[1], "d1", 0)
    to_x(1)
    for d in range(1, ZL):
        got(actr.at[down(zl, d, ZL)], "act", d - 1)
    for b in range(bpd):
        act_o[:, b * tb:(b + 1) * tb] = actr[b]
    got(Tr, "dt", 0)
    OutW[me] = Ts[...] + Tr[...]
    others = [(d, e) for d in range(X) for e in range(C) if d or e]
    for n, (d, e) in enumerate(others):
        to = dev(x_=up(x, d, X), c_=(co if e else c))
        send(OutW.at[me], OutW.at[me], "ow", n, to)
    own = from_x(1)
    for n, (d, e) in enumerate(others):
        got(OutW.at[down(x, d, X) * C + (co if e else c)], "ow", n)
    for q in range(Q):
        gw_o[:, q * qw:(q + 1) * qw] = OutW[q]
    for i in range(parts):
        got(FZr.at[cut(i)], "gz", i)
    own = (own + FZr[...].astype(F32)).astype(BF)
    for b in range(bpd):
        gf_o[:, b * tb:(b + 1) * tb] = own[b]
    for cp in sent:
        cp.wait_send()


def on_device(cfg, features_t, tile_dst, tile_src, tile_edges, tile_values, weight, cotangent):
    rb = features_t.shape[0]
    nt, tb = tile_values.shape[:2]
    bufs, sems, smem = shapes(cfg, rb, tb, nt)
    vm, hbm = pl.BlockSpec(memory_space=pltpu.VMEM), pl.BlockSpec(memory_space=pltpu.HBM)
    kernel = functools.partial(body, cfg, tuple(bufs), tuple(sems))
    outs = (
        pltpu.VMEM(features_t.shape, BF),
        pltpu.VMEM(weight.shape, F32),
        pltpu.VMEM(features_t.shape, BF),
    )
    return pl.pallas_call(
        kernel,
        out_shape=outs,
        in_specs=[hbm] * 7,
        out_specs=(vm, vm, vm),
        scratch_shapes=[pltpu.VMEM(s, t) for s, t in bufs.values()]
        + [pltpu.SemaphoreType.DMA((n,)) for n in sems.values()] * 2
        + [pltpu.SemaphoreType.DMA((9,))]
        + [pltpu.SMEM(s, t) for s, t in smem.values()],
        compiler_params=pltpu.CompilerParams(
            collective_id=0, has_side_effects=True, vmem_limit_bytes=62 * 1024 * 1024
        ),
        name="graph_conv",
    )(features_t, tile_values, weight, cotangent, *(v.reshape(1, nt) for v in (tile_dst, tile_src, tile_edges)))


def solution(mesh, cfg=None):
    in_specs = (
        P("rep", "blk"),
        P("blk"),
        P("blk"),
        P("blk"),
        P("blk", None, None),
        P("rep", None),
        P("rep", "blk"),
    )
    out_specs = (P("rep", "blk"), P("rep", None), P("rep", "blk"))
    return jax.shard_map(
        functools.partial(on_device, cfg or FULL), mesh=mesh, in_specs=in_specs, out_specs=out_specs, check_vma=False
    )
```

```python
import functools

import jax
import jax.numpy as jnp
from jax import lax
from jax.experimental import pallas as pl
from jax.experimental.pallas import tpu as pltpu
from jax.sharding import PartitionSpec as P

FULL = dict(ZH=2, X=4, C=2, Y=4, ZL=8)
PER = 4
MESH = pl.DeviceIdType.MESH
BF = jnp.bfloat16
F32 = jnp.float32


def dot(a, b, ca, cb):
    return lax.dot_general(a, b, (((ca,), (cb,)), ((), ())), preferred_element_type=F32)


def shapes(cfg, rb, tb, nt):
    X, C, Y, ZL = cfg["X"], cfg["C"], cfg["Y"], cfg["ZL"]
    Q = X * C
    F = rb * Y * ZL
    qw = F // Q
    bpd = ZL
    x1, y1, z1 = max(X - 1, 1), max(Y - 1, 1), max(ZL - 1, 1)
    nk = -(-cfg["ZH"] * Q * PER // 128) * 128
    bufs = dict(
        fv=((rb, bpd * tb), BF),
        wv=((rb, F), BF),
        cv=((rb, bpd * tb), BF),
        dv=((1, nt), jnp.int32),
        sv=((1, nt), jnp.int32),
        ev=((1, nt), jnp.int32),
        itv=((8, nk), jnp.int32),
        ftv=((2 * bpd + 8, nk), F32),
        gown=((Q * bpd, rb, tb), BF),
        goth=((Q * bpd, rb, tb), BF),
        tv=((nt, tb, tb), BF),
        wb=((Q, rb, qw), BF),
        wg=((Y, C, X, ZL, rb, qw), BF),
        cb=((bpd, rb, tb), BF),
        ct=((ZL, rb, tb), BF),
        aggb=((bpd, rb, tb), BF),
        A=((ZL, rb, tb), BF),
        ctT=((Y, tb, rb * ZL), BF),
        AT=((Y, tb, rb * ZL), BF),
        preT=((X, tb, C * qw), F32),
        gpT=((Q, tb, qw), BF),
        actb=((ZL, rb, tb), BF),
        actr=((bpd, rb, tb), BF),
        gab=((ZL, rb, tb), BF),
        GA=((bpd, rb, tb), BF),
        PS=((X, ZL, rb, qw), BF),
        PO=((X, ZL, rb, qw), F32),
        PR=((X, ZL, rb, qw), BF),
        DXs=((x1, ZL, rb, qw), BF),
        DXr=((x1, ZL, rb, qw), BF),
        Sb=((ZL, rb, qw), BF),
        S32=((ZL, rb, qw), F32),
        DZr=((z1, rb, qw), BF),
        Ts=((rb, qw), F32),
        Tr=((rb, qw), F32),
        OutW=((Q, rb, qw), F32),
        Dsib0=((X, bpd, rb, tb), BF),
        Dsib1=((X, bpd, rb, tb), BF),
        Drec0=((X, bpd, rb, tb), BF),
        Drec1=((X, bpd, rb, tb), BF),
        Dkeep0=((X, bpd, rb, tb), F32),
        Dkeep1=((X, bpd, rb, tb), F32),
        EXs0=((x1, bpd, rb, tb), BF),
        EXs1=((x1, bpd, rb, tb), BF),
        EXr0=((x1, bpd, rb, tb), BF),
        EXr1=((x1, bpd, rb, tb), BF),
        FZs=((bpd, rb, tb), BF),
        FZr=((bpd, rb, tb), BF),
    )
    sems = dict(
        fz=1, fx0=x1, fx1=x1, fc0=X, fc1=X, w1=z1, w2=x1, w3=Y, w4=2, w5=2, ct=z1, cty=y1, ag=z1, agy=y1, act=z1, ga=z1,
        p=1, dx=x1, dz=z1, dt=1, ow=2 * X, d0=1, d1=1, e0=2 * x1, e1=x1, gz=2,
    )
    smem = dict(itab=((8, nk), jnp.int32), ftab=((2 * bpd + 8, nk), F32))
    return bufs, sems, smem


def tables(bpd, dst, src, edges, itv, ftv):
    nt = dst.shape[1]
    nk = itv.shape[1]
    r0 = lax.broadcasted_iota(jnp.int32, (nt, nt), 0)
    r1 = lax.broadcasted_iota(jnp.int32, (nt, nt), 1)
    k1 = lax.broadcasted_iota(jnp.int32, (nt, nk), 1)
    t0 = lax.broadcasted_iota(jnp.int32, (nt, nk), 0)
    lane = lax.broadcasted_iota(jnp.int32, (1, nt), 1)

    def column(row):
        return jnp.sum(jnp.where(r0 == r1, row, jnp.zeros_like(row)), axis=1, keepdims=True)

    bits = bpd.bit_length() - 1
    group = jnp.where((edges > 0) & (lane >= bpd), lax.shift_right_logical(src, bits), -1)
    group_c = column(group)
    rank = jnp.sum(jnp.where((group_c == group) & (r1 < r0), 1, 0), axis=1, keepdims=True)
    pick = jnp.where(group_c >= 0, group_c * PER + rank, -1) == k1

    def by_k(col):
        return jnp.sum(jnp.where(pick, col, jnp.zeros_like(col)), axis=0, keepdims=True)

    at_src, at_dst = by_k(column(src & (bpd - 1))), by_k(column(dst))
    itv[0:1] = by_k(t0)
    itv[1:2] = at_src
    itv[2:3] = at_dst
    blocks = lax.broadcasted_iota(jnp.int32, (bpd, nt), 0)
    weights = jnp.where(dst == blocks, edges.astype(F32), 0.0)
    coef = jnp.sum(weights / jnp.sum(weights, axis=1, keepdims=True), axis=0, keepdims=True)
    coef_k = by_k(column(coef))
    blocks = lax.broadcasted_iota(jnp.int32, (bpd, nk), 0)
    ftv[0:bpd] = jnp.where(at_dst == blocks, coef_k, 0.0)
    ftv[bpd:2 * bpd] = jnp.where(at_src == blocks, coef_k, 0.0)
    ftv[2 * bpd:2 * bpd + 1, 0:nt] = coef


def body(cfg, buf_names, sem_names, feat_hbm, tv_hbm, w_hbm, cot_hbm, dst_hbm, src_hbm, edge_hbm, act_o, gw_o, gf_o, *scr):
    ZH, X, C, Y, ZL = cfg["ZH"], cfg["X"], cfg["C"], cfg["Y"], cfg["ZL"]
    nb, ns = len(buf_names), len(sem_names)
    B = dict(zip(buf_names, scr[:nb]))
    SS = dict(zip(sem_names, scr[nb:nb + ns]))
    RS = dict(zip(sem_names, scr[nb + ns:nb + 2 * ns]))
    load_sem, itab, ftab = scr[nb + 2 * ns:]
    feat, w, cot = B["fv"], B["wv"], B["cv"]
    Q = X * C
    bpd = ZL
    rb, tb = B["A"].shape[1:]
    qw = B["wb"].shape[2]
    rows = ZL * rb

    blk, rep = lax.axis_index("blk"), lax.axis_index("rep")
    zh = lax.div(blk, Q)
    me = lax.rem(blk, Q)
    x, c = lax.div(me, C), lax.rem(me, C)
    y, zl = lax.div(rep, ZL), lax.rem(rep, ZL)
    zo, co = 1 - zh, 1 - c

    def dev(zh_=zh, x_=x, c_=c, y_=y, zl_=zl):
        return ((zh_ * X + x_) * C + c_, y_ * ZL + zl_)

    def up(v, d, n):
        return lax.rem(v + d, n)

    def down(v, d, n):
        return lax.rem(v + n - d, n)

    anti, sib = dev(zh_=zo), dev(c_=co)
    sent = []

    def send(src, dst, name, i, to):
        cp = pltpu.make_async_remote_copy(
            src_ref=src, dst_ref=dst, send_sem=SS[name].at[i], recv_sem=RS[name].at[i],
            device_id=to, device_id_type=MESH,
        )
        cp.start()
        sent.append(cp)

    def got(dst, name, i):
        pltpu.make_async_remote_copy(
            src_ref=dst, dst_ref=dst, send_sem=SS[name].at[i], recv_sem=RS[name].at[i],
            device_id=sib, device_id_type=MESH,
        ).wait_recv()

    loads = [
        pltpu.make_async_copy(a, b, load_sem.at[i])
        for i, (a, b) in enumerate((
            (feat_hbm, feat), (w_hbm, w), (cot_hbm, cot), (tv_hbm, B["tv"]),
            (dst_hbm, B["dv"]), (src_hbm, B["sv"]), (edge_hbm, B["ev"]),
        ))
    ]
    for ld in loads:
        ld.start()

    barrier = pltpu.get_barrier_semaphore()
    partners = [anti]
    partners += [dev(x_=up(x, d, X), c_=(c if e == 0 else co)) for d in range(X) for e in range(C) if d or e]
    partners += [dev(zl_=up(zl, d, ZL)) for d in range(1, ZL)]
    partners += [dev(y_=up(y, d, Y)) for d in range(1, Y)]
    for p in partners:
        pl.semaphore_signal(barrier, inc=1, device_id=p, device_id_type=MESH)

    gown, goth, tv = B["gown"], B["goth"], B["tv"]
    loads[0].wait()
    for b in range(bpd):
        gown[me * bpd + b] = feat[:, b * tb:(b + 1) * tb]
    pl.semaphore_wait(barrier, len(partners))

    def seg(m):
        return pl.ds(m * bpd, bpd)

    mine = seg(me)
    send(gown.at[mine], goth.at[mine], "fz", 0, anti)
    for d in range(1, X):
        send(gown.at[mine], gown.at[mine], "fx0", d - 1, dev(x_=up(x, d, X)))
    send(gown.at[mine], gown.at[mine], "fc0", 0, sib)
    for ld in loads[4:]:
        ld.wait()
    tables(bpd, B["dv"][...], B["sv"][...], B["ev"][...], B["itv"], B["ftv"])
    to_smem = [
        pltpu.make_async_copy(B["itv"], itab, load_sem.at[7]),
        pltpu.make_async_copy(B["ftv"], ftab, load_sem.at[8]),
    ]
    for cp in to_smem:
        cp.start()
    loads[1].wait()
    loads[2].wait()
    for b in range(bpd):
        B["cb"][b] = cot[:, b * tb:(b + 1) * tb]
    for q in range(Q):
        B["wb"][q] = w[:, q * qw:(q + 1) * qw]
    B["wg"][y, c, x, zl] = B["wb"][me]
    B["ct"][zl] = B["cb"][zl]
    wg, wb = B["wg"], B["wb"]
    for d in range(1, ZL):
        z = up(zl, d, ZL)
        send(wb.at[me], wg.at[y, c, x, zl], "w1", d - 1, dev(zl_=z))
    for d in range(1, X):
        part = gown.at[seg(down(x, d, X) * C + c)]
        got(part, "fx0", d - 1)
        send(part, part, "fc0", d, sib)
    loads[3].wait()
    for cp in to_smem:
        cp.wait()
    acc = tuple(ftab[2 * bpd, b] * dot(gown[me * bpd + b], tv[b], 1, 1) for b in range(bpd))

    def forward(g, half, i, acc):
        acc = list(acc)
        for j in range(C * PER):
            m = i * C + j // PER
            k = (half * Q + i * C) * PER + j
            out = dot(g[m * bpd + itab[1, k]], tv[itab[0, k]], 1, 1)
            for b in range(bpd):
                acc[b] = acc[b] + ftab[b, k] * out
        return tuple(acc)

    for d in range(1, ZL):
        got(wg.at[y, c, x, down(zl, d, ZL)], "w1", d - 1)
    for d in range(1, X):
        send(wg.at[y, c, x], wg.at[y, c, x], "w2", d - 1, dev(x_=up(x, d, X)))
    got(goth.at[mine], "fz", 0)
    for d in range(1, X):
        send(goth.at[mine], goth.at[mine], "fx1", d - 1, dev(x_=up(x, d, X)))
    send(goth.at[mine], goth.at[mine], "fc1", 0, sib)
    for d in range(1, ZL):
        z = up(zl, d, ZL)
        send(B["cb"].at[z], B["ct"].at[zl], "ct", d - 1, dev(zl_=z))
    for d in range(X):
        got(gown.at[seg(down(x, d, X) * C + co)], "fc0", d)
    acc = lax.fori_loop(0, Q // C, lambda i, a: forward(gown, zh, i, a), acc)
    for d in range(1, X):
        got(wg.at[y, c, down(x, d, X)], "w2", d - 1)
    y_up, y_down, y_far = up(y, 1, Y), down(y, 1, Y), up(y, 2, Y)
    send(wg.at[y, c], wg.at[y, c], "w4", 0, dev(y_=y_up))
    if Y > 2:
        send(wg.at[y, c], wg.at[y, c], "w4", 1, dev(y_=y_down))
    send(wg.at[y, c], wg.at[y, c], "w3", 0, sib)
    for d in range(1, X):
        part = goth.at[seg(down(x, d, X) * C + c)]
        got(part, "fx1", d - 1)
        send(part, part, "fc1", d, sib)
    for d in range(1, ZL):
        got(B["ct"].at[down(zl, d, ZL)], "ct", d - 1)
    ctT, AT = B["ctT"], B["AT"]
    ctT[y] = B["ct"][...].reshape(rows, tb).astype(F32).T.astype(BF)
    for d in range(1, Y):
        send(ctT.at[y], ctT.at[y], "cty", d - 1, dev(y_=up(y, d, Y)))
    for d in range(X):
        got(goth.at[seg(down(x, d, X) * C + co)], "fc1", d)
    acc = lax.fori_loop(0, Q // C, lambda i, a: forward(goth, zo, i, a), acc)

    A = B["A"]
    for b in range(bpd):
        B["aggb"][b] = acc[b].astype(BF)
    A[zl] = B["aggb"][zl]
    for d in range(1, ZL):
        z = up(zl, d, ZL)
        send(B["aggb"].at[z], A.at[zl], "ag", d - 1, dev(zl_=z))
    half = X // 2
    got(wg.at[y_down, c], "w4", 0)
    send(wg.at[y_down, c], wg.at[y_down, c], "w3", 1, sib)
    if Y > 2:
        part = wg.at[y_down, c, pl.ds(0, half)]
        send(part, part, "w5", 0, dev(y_=y_up))
        got(wg.at[y_up, c], "w4", 1)
        send(wg.at[y_up, c], wg.at[y_up, c], "w3", 2, sib)
        part = wg.at[y_up, c, pl.ds(half, half)]
        send(part, part, "w5", 1, dev(y_=y_down))
    for d in range(1, ZL):
        got(A.at[down(zl, d, ZL)], "ag", d - 1)

    a2 = A[...].reshape(rows, tb)
    AT[y] = a2.astype(F32).T.astype(BF)
    for d in range(1, Y):
        send(AT.at[y], AT.at[y], "agy", d - 1, dev(y_=up(y, d, Y)))

    def weight_of(y_, i):
        return jnp.concatenate([wg[y_, e, i].reshape(rows, qw) for e in range(C)], axis=1)

    preT, gpT = B["preT"], B["gpT"]
    got(wg.at[y, co], "w3", 0)
    for i in range(X):
        preT[i] = dot(AT[y], weight_of(y, i), 1, 0)
    if Y > 2:
        got(wg.at[y_far, c, pl.ds(0, half)], "w5", 0)
        got(wg.at[y_far, c, pl.ds(half, half)], "w5", 1)
        send(wg.at[y_far, c], wg.at[y_far, c], "w3", 3, sib)
    for d in range(1, Y):
        got(ctT.at[down(y, d, Y)], "cty", d - 1)
    order = [(1, 1), (3, 2), (2, 3)] if Y > 2 else [(1, 1)]
    for n, (d, at) in enumerate(order):
        y_ = down(y, d, Y)
        got(wg.at[y_, co], "w3", at)
        got(AT.at[y_], "agy", d - 1)
        for i in range(X):
            pre = preT[i] + dot(AT[y_], weight_of(y_, i), 1, 0)
            preT[i] = pre
            if n == len(order) - 1:
                sig = jax.nn.sigmoid(pre)
                gp = (ctT[i].astype(F32) * sig * (1.0 + pre * (1.0 - sig))).astype(BF)
                for e in range(C):
                    gpT[i * C + e] = gp[:, e * qw:(e + 1) * qw]

    def grad_pre(i):
        return jnp.concatenate([gpT[i * C + e] for e in range(C)], axis=1)

    ga = dot(weight_of(y, 0), grad_pre(0), 1, 1)
    for i in range(1, X):
        ga = ga + dot(weight_of(y, i), grad_pre(i), 1, 1)
    gab, GA = B["gab"], B["GA"]
    gab[...] = ga.astype(BF).reshape(ZL, rb, tb)
    GA[zl] = gab[zl]
    for d in range(1, ZL):
        z = up(zl, d, ZL)
        send(gab.at[z], GA.at[zl], "ga", d - 1, dev(zl_=z))

    PS, PO, PR = B["PS"], B["PO"], B["PR"]
    for i in range(X):
        PS[i] = dot(a2, gpT[i * C + co], 1, 0).astype(BF).reshape(ZL, rb, qw)
    send(PS, PR, "p", 0, sib)
    for i in range(X):
        PO[i] = dot(a2, gpT[i * C + c], 1, 0).reshape(ZL, rb, qw)
    got(PR, "p", 0)
    DXs, DXr = B["DXs"], B["DXr"]
    for d in range(1, X):
        x_ = up(x, d, X)
        DXs[d - 1] = (PO[x_] + PR[x_].astype(F32)).astype(BF)
        send(DXs.at[d - 1], DXr.at[d - 1], "dx", d - 1, dev(x_=x_))
    for d in range(1, ZL):
        got(GA.at[down(zl, d, ZL)], "ga", d - 1)

    def backward(half, m):
        outs = [None] * bpd
        for j in range(PER):
            k = (half * Q + m) * PER + j
            back = dot(GA[itab[2, k]], tv[itab[0, k]], 1, 0)
            for b in range(bpd):
                term = ftab[bpd + b, k] * back
                outs[b] = term if j == 0 else outs[b] + term
        return outs

    def contribute(half, core, into):
        step = 2 if X % 2 == 0 else 1

        def some(i, carry):
            for n in range(step):
                for b, out in enumerate(backward(half, (i * step + n) * C + core)):
                    into[i * step + n, b] = out.astype(into.dtype)
            return carry
        lax.fori_loop(0, X // step, some, 0)

    Dsib, Drec, Dkeep = (B["Dsib0"], B["Dsib1"]), (B["Drec0"], B["Drec1"]), (B["Dkeep0"], B["Dkeep1"])
    EXs, EXr = (B["EXs0"], B["EXs1"]), (B["EXr0"], B["EXr1"])

    parts = 2 if bpd % 2 == 0 else 1

    def cut(i):
        return pl.ds(i * (bpd // parts), bpd // parts)

    whole = pl.ds(0, bpd)

    def to_x(n, at=whole, i=0):
        for d in range(1, X):
            x_ = up(x, d, X)
            EXs[n][d - 1, at] = (Dkeep[n][x_, at] + Drec[n][x_, at].astype(F32)).astype(BF)
            send(EXs[n].at[d - 1, at], EXr[n].at[d - 1, at], "e%d" % n, i * (X - 1) + d - 1, dev(x_=x_))

    def from_x(n, at=whole, i=0):
        total = Dkeep[n][x, at] + Drec[n][x, at].astype(F32)
        for d in range(1, X):
            got(EXr[n].at[d - 1, at], "e%d" % n, i * (X - 1) + d - 1)
            total = total + EXr[n][d - 1, at].astype(F32)
        return total

    contribute(zo, co, Dsib[0])
    send(Dsib[0], Drec[0], "d0", 0, sib)
    contribute(zo, c, Dkeep[0])

    got(Drec[0], "d0", 0)
    for i in range(parts):
        to_x(0, cut(i), i)
    S32, Sb, DZr = B["S32"], B["Sb"], B["DZr"]
    total = PO[x] + PR[x].astype(F32)
    for d in range(1, X):
        got(DXr.at[d - 1], "dx", d - 1)
        total = total + DXr[d - 1].astype(F32)
    S32[...] = total
    Sb[...] = total.astype(BF)
    for d in range(1, ZL):
        z = up(zl, d, ZL)
        send(Sb.at[z], DZr.at[d - 1], "dz", d - 1, dev(zl_=z))
    contribute(zh, co, Dsib[1])
    send(Dsib[1], Drec[1], "d1", 0, sib)
    actb, actr = B["actb"], B["actr"]
    pre = preT[y]
    actb[...] = (pre * jax.nn.sigmoid(pre)).T.astype(BF).reshape(ZL, rb, tb)
    actr[zl] = actb[zl]
    for d in range(1, ZL):
        z = up(zl, d, ZL)
        send(actb.at[z], actr.at[zl], "act", d - 1, dev(zl_=z))
    contribute(zh, c, Dkeep[1])
    for b in range(bpd):
        Dkeep[1][x, b] = ftab[2 * bpd, b] * dot(GA[b], tv[b], 1, 0)
    total = S32[zl]
    for d in range(1, ZL):
        got(DZr.at[d - 1], "dz", d - 1)
        total = total + DZr[d - 1].astype(F32)
    Ts, Tr, OutW = B["Ts"], B["Tr"], B["OutW"]
    Ts[...] = total
    send(Ts, Tr, "dt", 0, anti)
    FZs, FZr = B["FZs"], B["FZr"]
    for i in range(parts):
        at = cut(i)
        FZs[at] = from_x(0, at, i).astype(BF)
        send(FZs.at[at], FZr.at[at], "gz", i, anti)
    got(Drec[1], "d1", 0)
    to_x(1)
    for d in range(1, ZL):
        got(actr.at[down(zl, d, ZL)], "act", d - 1)
    for b in range(bpd):
        act_o[:, b * tb:(b + 1) * tb] = actr[b]
    got(Tr, "dt", 0)
    OutW[me] = Ts[...] + Tr[...]
    others = [(d, e) for d in range(X) for e in range(C) if d or e]
    for n, (d, e) in enumerate(others):
        to = dev(x_=up(x, d, X), c_=(co if e else c))
        send(OutW.at[me], OutW.at[me], "ow", n, to)
    own = from_x(1)
    for n, (d, e) in enumerate(others):
        got(OutW.at[down(x, d, X) * C + (co if e else c)], "ow", n)
    for q in range(Q):
        gw_o[:, q * qw:(q + 1) * qw] = OutW[q]
    for i in range(parts):
        got(FZr.at[cut(i)], "gz", i)
    own = (own + FZr[...].astype(F32)).astype(BF)
    for b in range(bpd):
        gf_o[:, b * tb:(b + 1) * tb] = own[b]
    for cp in sent:
        cp.wait_send()


def on_device(cfg, features_t, tile_dst, tile_src, tile_edges, tile_values, weight, cotangent):
    rb = features_t.shape[0]
    nt, tb = tile_values.shape[:2]
    bufs, sems, smem = shapes(cfg, rb, tb, nt)
    vm, hbm = pl.BlockSpec(memory_space=pltpu.VMEM), pl.BlockSpec(memory_space=pltpu.HBM)
    kernel = functools.partial(body, cfg, tuple(bufs), tuple(sems))
    outs = (
        pltpu.VMEM(features_t.shape, BF),
        pltpu.VMEM(weight.shape, F32),
        pltpu.VMEM(features_t.shape, BF),
    )
    return pl.pallas_call(
        kernel,
        out_shape=outs,
        in_specs=[hbm] * 7,
        out_specs=(vm, vm, vm),
        scratch_shapes=[pltpu.VMEM(s, t) for s, t in bufs.values()]
        + [pltpu.SemaphoreType.DMA((n,)) for n in sems.values()] * 2
        + [pltpu.SemaphoreType.DMA((9,))]
        + [pltpu.SMEM(s, t) for s, t in smem.values()],
        compiler_params=pltpu.CompilerParams(
            collective_id=0, has_side_effects=True, vmem_limit_bytes=62 * 1024 * 1024
        ),
        name="graph_conv",
    )(features_t, tile_values, weight, cotangent, *(v.reshape(1, nt) for v in (tile_dst, tile_src, tile_edges)))


def solution(mesh, cfg=None):
    in_specs = (
        P("rep", "blk"),
        P("blk"),
        P("blk"),
        P("blk"),
        P("blk", None, None),
        P("rep", None),
        P("rep", "blk"),
    )
    out_specs = (P("rep", "blk"), P("rep", None), P("rep", "blk"))
    return jax.shard_map(
        functools.partial(on_device, cfg or FULL), mesh=mesh, in_specs=in_specs, out_specs=out_specs, check_vma=False
    )
```

```python
import functools

import jax
import jax.numpy as jnp
from jax import lax
from jax.experimental import pallas as pl
from jax.experimental.pallas import tpu as pltpu
from jax.sharding import PartitionSpec as P

FULL = dict(ZH=2, X=4, C=2, Y=4, ZL=8)
PER = 4
MESH = pl.DeviceIdType.MESH
BF = jnp.bfloat16
F32 = jnp.float32


def dot(a, b, ca, cb):
    return lax.dot_general(a, b, (((ca,), (cb,)), ((), ())), preferred_element_type=F32)


def groups(n):
    return 2 if n % 2 == 0 else 1


def shapes(cfg, rb, tb, nt):
    X, C, Y, ZL = cfg["X"], cfg["C"], cfg["Y"], cfg["ZL"]
    Q = X * C
    F = rb * Y * ZL
    qw = F // Q
    bpd = ZL
    x1, y1, z1 = max(X - 1, 1), max(Y - 1, 1), max(ZL - 1, 1)
    nk = -(-cfg["ZH"] * Q * PER // 128) * 128
    bufs = dict(
        fv=((rb, bpd * tb), BF),
        wv=((rb, F), BF),
        cv=((rb, bpd * tb), BF),
        dv=((1, nt), jnp.int32),
        sv=((1, nt), jnp.int32),
        ev=((1, nt), jnp.int32),
        itv=((8, nk), jnp.int32),
        ftv=((2 * bpd + 8, nk), F32),
        ZR=((bpd // groups(bpd), rb, tb), BF),
        FR=((bpd // groups(bpd), rb, tb), BF),
        gown=((Q * bpd, rb, tb), BF),
        goth=((Q * bpd, rb, tb), BF),
        tv=((nt, tb, tb), BF),
        wb=((Q, rb, qw), BF),
        wg=((Y, C, X, ZL, rb, qw), BF),
        cb=((bpd, rb, tb), BF),
        ct=((ZL, rb, tb), BF),
        aggb=((bpd, rb, tb), BF),
        A=((ZL, rb, tb), BF),
        ctT=((Y, tb, rb * ZL), BF),
        AT=((Y, groups(ZL), tb, rb * ZL // groups(ZL)), BF),
        preT=((X, tb, C * qw), F32),
        gpT=((Q, tb, qw), BF),
        actb=((ZL, rb, tb), BF),
        actr=((bpd, rb, tb), BF),
        gab=((ZL, rb, tb), BF),
        GA=((bpd, rb, tb), BF),
        PS=((X, ZL, rb, qw), BF),
        PO=((X, ZL, rb, qw), F32),
        PR=((X, ZL, rb, qw), BF),
        DXs=((x1, ZL, rb, qw), BF),
        DXr=((x1, ZL, rb, qw), BF),
        Sb=((ZL, rb, qw), BF),
        S32=((ZL, rb, qw), F32),
        DZr=((z1, rb, qw), BF),
        Ts=((rb, qw), F32),
        Tr=((rb, qw), F32),
        OutW=((Q, rb, qw), F32),
        Dsib0=((X, bpd, rb, tb), BF),
        Dsib1=((X, bpd, rb, tb), BF),
        Drec0=((X, bpd, rb, tb), BF),
        Drec1=((X, bpd, rb, tb), BF),
        Dkeep0=((X, bpd, rb, tb), F32),
        Dkeep1=((X, bpd, rb, tb), F32),
        EXs0=((x1, bpd, rb, tb), BF),
        EXs1=((x1, bpd, rb, tb), BF),
        EXr0=((x1, bpd, rb, tb), BF),
        EXr1=((x1, bpd, rb, tb), BF),
        FZs=((bpd, rb, tb), BF),
        FZr=((bpd, rb, tb), BF),
    )
    sems = dict(
        zr=1, fz=2, fx0=x1, fx1=2 * x1, fc0=X, fc1=2 * X, w1=z1, w2=x1, w3=Y, w4=2, w5=2, ct=z1, cty=y1, ag=z1, agy=2 * y1, act=z1, ga=z1,
        p=1, dx=x1, dz=z1, dt=1, ow=2 * X, d0=1, d1=1, e0=2 * x1, e1=x1, fr=1, gz=2,
    )
    smem = dict(itab=((8, nk), jnp.int32), ftab=((2 * bpd + 8, nk), F32))
    return bufs, sems, smem


def tables(bpd, dst, src, edges, itv, ftv):
    nt = dst.shape[1]
    nk = itv.shape[1]
    r0 = lax.broadcasted_iota(jnp.int32, (nt, nt), 0)
    r1 = lax.broadcasted_iota(jnp.int32, (nt, nt), 1)
    k1 = lax.broadcasted_iota(jnp.int32, (nt, nk), 1)
    t0 = lax.broadcasted_iota(jnp.int32, (nt, nk), 0)
    lane = lax.broadcasted_iota(jnp.int32, (1, nt), 1)

    def column(row):
        return jnp.sum(jnp.where(r0 == r1, row, jnp.zeros_like(row)), axis=1, keepdims=True)

    bits = bpd.bit_length() - 1
    group = jnp.where((edges > 0) & (lane >= bpd), lax.shift_right_logical(src, bits), -1)
    group_c = column(group)
    rank = jnp.sum(jnp.where((group_c == group) & (r1 < r0), 1, 0), axis=1, keepdims=True)
    pick = jnp.where(group_c >= 0, group_c * PER + rank, -1) == k1

    def by_k(col):
        return jnp.sum(jnp.where(pick, col, jnp.zeros_like(col)), axis=0, keepdims=True)

    at_src, at_dst = by_k(column(src & (bpd - 1))), by_k(column(dst))
    itv[0:1] = by_k(t0)
    itv[1:2] = at_src
    itv[2:3] = at_dst
    blocks = lax.broadcasted_iota(jnp.int32, (bpd, nt), 0)
    weights = jnp.where(dst == blocks, edges.astype(F32), 0.0)
    coef = jnp.sum(weights / jnp.sum(weights, axis=1, keepdims=True), axis=0, keepdims=True)
    coef_k = by_k(column(coef))
    blocks = lax.broadcasted_iota(jnp.int32, (bpd, nk), 0)
    ftv[0:bpd] = jnp.where(at_dst == blocks, coef_k, 0.0)
    ftv[bpd:2 * bpd] = jnp.where(at_src == blocks, coef_k, 0.0)
    ftv[2 * bpd:2 * bpd + 1, 0:nt] = coef


def body(cfg, buf_names, sem_names, feat_hbm, tv_hbm, w_hbm, cot_hbm, dst_hbm, src_hbm, edge_hbm, act_o, gw_o, gf_o, *scr):
    ZH, X, C, Y, ZL = cfg["ZH"], cfg["X"], cfg["C"], cfg["Y"], cfg["ZL"]
    nb, ns = len(buf_names), len(sem_names)
    B = dict(zip(buf_names, scr[:nb]))
    SS = dict(zip(sem_names, scr[nb:nb + ns]))
    RS = dict(zip(sem_names, scr[nb + ns:nb + 2 * ns]))
    load_sem, itab, ftab = scr[nb + 2 * ns:]
    feat, w, cot = B["fv"], B["wv"], B["cv"]
    Q = X * C
    bpd = ZL
    rb, tb = B["A"].shape[1:]
    qw = B["wb"].shape[2]
    rows = ZL * rb

    blk, rep = lax.axis_index("blk"), lax.axis_index("rep")
    zh = lax.div(blk, Q)
    me = lax.rem(blk, Q)
    x, c = lax.div(me, C), lax.rem(me, C)
    y, zl = lax.div(rep, ZL), lax.rem(rep, ZL)
    zo, co = 1 - zh, 1 - c

    def dev(zh_=zh, x_=x, c_=c, y_=y, zl_=zl):
        return ((zh_ * X + x_) * C + c_, y_ * ZL + zl_)

    def up(v, d, n):
        return lax.rem(v + d, n)

    def down(v, d, n):
        return lax.rem(v + n - d, n)

    anti, sib = dev(zh_=zo), dev(c_=co)
    nz = ZH * ZL

    def dev_z(d):
        z_ = lax.rem(zh * ZL + zl + d + nz, nz)
        return dev(zh_=lax.div(z_, ZL), zl_=lax.rem(z_, ZL))

    parts = groups(bpd)
    size = bpd // parts
    sent = []

    def send(src, dst, name, i, to):
        cp = pltpu.make_async_remote_copy(
            src_ref=src, dst_ref=dst, send_sem=SS[name].at[i], recv_sem=RS[name].at[i],
            device_id=to, device_id_type=MESH,
        )
        cp.start()
        sent.append(cp)

    def got(dst, name, i):
        pltpu.make_async_remote_copy(
            src_ref=dst, dst_ref=dst, send_sem=SS[name].at[i], recv_sem=RS[name].at[i],
            device_id=sib, device_id_type=MESH,
        ).wait_recv()

    loads = [
        pltpu.make_async_copy(a, b, load_sem.at[i])
        for i, (a, b) in enumerate((
            (feat_hbm, feat), (w_hbm, w), (cot_hbm, cot), (tv_hbm, B["tv"]),
            (dst_hbm, B["dv"]), (src_hbm, B["sv"]), (edge_hbm, B["ev"]),
        ))
    ]
    for ld in loads:
        ld.start()

    barrier = pltpu.get_barrier_semaphore()
    partners = [anti, *(dev_z(d) for d in (1, -1, ZL - 1, 1 - ZL))]
    partners += [dev(x_=up(x, d, X), c_=(c if e == 0 else co)) for d in range(X) for e in range(C) if d or e]
    partners += [dev(zl_=up(zl, d, ZL)) for d in range(1, ZL)]
    partners += [dev(y_=up(y, d, Y)) for d in range(1, Y)]
    for p in partners:
        pl.semaphore_signal(barrier, inc=1, device_id=p, device_id_type=MESH)

    gown, goth, tv = B["gown"], B["goth"], B["tv"]
    loads[0].wait()
    for b in range(bpd):
        gown[me * bpd + b] = feat[:, b * tb:(b + 1) * tb]
    pl.semaphore_wait(barrier, len(partners))

    def seg(m):
        return pl.ds(m * bpd, bpd)

    def sub(m, i):
        return pl.ds(m * bpd + i * size, size)

    mine = seg(me)
    if parts > 1:
        send(gown.at[sub(me, 0)], B["ZR"], "zr", 0, dev_z(-1))
    last = sub(me, parts - 1)
    send(gown.at[last], goth.at[last], "fz", parts - 1, anti)
    for d in range(1, X):
        send(gown.at[mine], gown.at[mine], "fx0", d - 1, dev(x_=up(x, d, X)))
    send(gown.at[mine], gown.at[mine], "fc0", 0, sib)
    for ld in loads[4:]:
        ld.wait()
    if parts > 1:
        got(B["ZR"], "zr", 0)
        send(B["ZR"], goth.at[sub(me, 0)], "fz", 0, dev_z(1 - ZL))
    tables(bpd, B["dv"][...], B["sv"][...], B["ev"][...], B["itv"], B["ftv"])
    to_smem = [
        pltpu.make_async_copy(B["itv"], itab, load_sem.at[7]),
        pltpu.make_async_copy(B["ftv"], ftab, load_sem.at[8]),
    ]
    for cp in to_smem:
        cp.start()
    loads[1].wait()
    loads[2].wait()
    for b in range(bpd):
        B["cb"][b] = cot[:, b * tb:(b + 1) * tb]
    for q in range(Q):
        B["wb"][q] = w[:, q * qw:(q + 1) * qw]
    B["wg"][y, c, x, zl] = B["wb"][me]
    B["ct"][zl] = B["cb"][zl]
    wg, wb = B["wg"], B["wb"]
    for d in range(1, ZL):
        z = up(zl, d, ZL)
        send(wb.at[me], wg.at[y, c, x, zl], "w1", d - 1, dev(zl_=z))
    for d in range(1, X):
        part = gown.at[seg(down(x, d, X) * C + c)]
        got(part, "fx0", d - 1)
        send(part, part, "fc0", d, sib)
    loads[3].wait()
    for cp in to_smem:
        cp.wait()
    acc = tuple(ftab[2 * bpd, b] * dot(gown[me * bpd + b], tv[b], 1, 1) for b in range(bpd))

    def forward(g, half, i, acc):
        acc = list(acc)
        for j in range(C * PER):
            m = i * C + j // PER
            k = (half * Q + i * C) * PER + j
            out = dot(g[m * bpd + itab[1, k]], tv[itab[0, k]], 1, 1)
            for b in range(bpd):
                acc[b] = acc[b] + ftab[b, k] * out
        return tuple(acc)

    for d in range(1, ZL):
        got(wg.at[y, c, x, down(zl, d, ZL)], "w1", d - 1)
    for d in range(1, X):
        send(wg.at[y, c, x], wg.at[y, c, x], "w2", d - 1, dev(x_=up(x, d, X)))
    for i in reversed(range(parts)):
        part = goth.at[sub(me, i)]
        got(part, "fz", i)
        for d in range(1, X):
            send(part, part, "fx1", i * (X - 1) + d - 1, dev(x_=up(x, d, X)))
        send(part, part, "fc1", i * X, sib)
    for d in range(1, ZL):
        z = up(zl, d, ZL)
        send(B["cb"].at[z], B["ct"].at[zl], "ct", d - 1, dev(zl_=z))
    for d in range(X):
        got(gown.at[seg(down(x, d, X) * C + co)], "fc0", d)
    acc = lax.fori_loop(0, Q // C, lambda i, a: forward(gown, zh, i, a), acc)
    for d in range(1, X):
        got(wg.at[y, c, down(x, d, X)], "w2", d - 1)
    y_up, y_down, y_far = up(y, 1, Y), down(y, 1, Y), up(y, 2, Y)
    send(wg.at[y, c], wg.at[y, c], "w4", 0, dev(y_=y_up))
    if Y > 2:
        send(wg.at[y, c], wg.at[y, c], "w4", 1, dev(y_=y_down))
    send(wg.at[y, c], wg.at[y, c], "w3", 0, sib)
    for i in reversed(range(parts)):
        for d in range(1, X):
            part = goth.at[sub(down(x, d, X) * C + c, i)]
            got(part, "fx1", i * (X - 1) + d - 1)
            send(part, part, "fc1", i * X + d, sib)
    for d in range(1, ZL):
        got(B["ct"].at[down(zl, d, ZL)], "ct", d - 1)
    ctT, AT = B["ctT"], B["AT"]
    ctT[y] = B["ct"][...].reshape(rows, tb).astype(F32).T.astype(BF)
    for d in range(1, Y):
        send(ctT.at[y], ctT.at[y], "cty", d - 1, dev(y_=up(y, d, Y)))
    for i in range(parts):
        for d in range(X):
            got(goth.at[sub(down(x, d, X) * C + co, i)], "fc1", i * X + d)
    acc = lax.fori_loop(0, Q // C, lambda i, a: forward(goth, zo, i, a), acc)

    A = B["A"]
    for b in range(bpd):
        B["aggb"][b] = acc[b].astype(BF)
    A[zl] = B["aggb"][zl]
    for d in range(1, ZL):
        z = up(zl, d, ZL)
        send(B["aggb"].at[z], A.at[zl], "ag", d - 1, dev(zl_=z))
    half = X // 2
    got(wg.at[y_down, c], "w4", 0)
    send(wg.at[y_down, c], wg.at[y_down, c], "w3", 1, sib)
    if Y > 2:
        part = wg.at[y_down, c, pl.ds(0, half)]
        send(part, part, "w5", 0, dev(y_=y_up))
        got(wg.at[y_up, c], "w4", 1)
        send(wg.at[y_up, c], wg.at[y_up, c], "w3", 2, sib)
        part = wg.at[y_up, c, pl.ds(half, half)]
        send(part, part, "w5", 1, dev(y_=y_down))
    ng = groups(ZL)
    hz = ZL // ng
    near = lax.div(zl, hz)
    for n in range(ng):
        g = near if n == 0 else 1 - near
        for e in range(hz):
            if n == 0 and e == 0:
                continue
            from_z = g * hz + (lax.rem(zl - g * hz + e, hz) if n == 0 else e)
            got(A.at[from_z], "ag", lax.rem(zl - from_z + ZL, ZL) - 1)
        AT[y, g] = A[pl.ds(g * hz, hz)].reshape(rows // ng, tb).astype(F32).T.astype(BF)
        for d in range(1, Y):
            send(AT.at[y, g], AT.at[y, g], "agy", n * (Y - 1) + d - 1, dev(y_=up(y, d, Y)))
    a2 = A[...].reshape(rows, tb)

    def nodes_by_rows(y_):
        return jnp.concatenate([AT[y_, g] for g in range(ng)], axis=1)


    def weight_of(y_, i):
        return jnp.concatenate([wg[y_, e, i].reshape(rows, qw) for e in range(C)], axis=1)

    preT, gpT = B["preT"], B["gpT"]
    got(wg.at[y, co], "w3", 0)
    for i in range(X):
        preT[i] = dot(nodes_by_rows(y), weight_of(y, i), 1, 0)
    if Y > 2:
        got(wg.at[y_far, c, pl.ds(0, half)], "w5", 0)
        got(wg.at[y_far, c, pl.ds(half, half)], "w5", 1)
        send(wg.at[y_far, c], wg.at[y_far, c], "w3", 3, sib)
    for d in range(1, Y):
        got(ctT.at[down(y, d, Y)], "cty", d - 1)
    order = [(1, 1), (3, 2), (2, 3)] if Y > 2 else [(1, 1)]
    for n, (d, at) in enumerate(order):
        y_ = down(y, d, Y)
        got(wg.at[y_, co], "w3", at)
        for g in range(ng):
            got(AT.at[y_, near if g == 0 else 1 - near], "agy", g * (Y - 1) + d - 1)
        for i in range(X):
            pre = preT[i] + dot(nodes_by_rows(y_), weight_of(y_, i), 1, 0)
            preT[i] = pre
            if n == len(order) - 1:
                sig = jax.nn.sigmoid(pre)
                gp = (ctT[i].astype(F32) * sig * (1.0 + pre * (1.0 - sig))).astype(BF)
                for e in range(C):
                    gpT[i * C + e] = gp[:, e * qw:(e + 1) * qw]

    def grad_pre(i):
        return jnp.concatenate([gpT[i * C + e] for e in range(C)], axis=1)

    ga = dot(weight_of(y, 0), grad_pre(0), 1, 1)
    for i in range(1, X):
        ga = ga + dot(weight_of(y, i), grad_pre(i), 1, 1)
    gab, GA = B["gab"], B["GA"]
    gab[...] = ga.astype(BF).reshape(ZL, rb, tb)
    GA[zl] = gab[zl]
    for d in range(1, ZL):
        z = up(zl, d, ZL)
        send(gab.at[z], GA.at[zl], "ga", d - 1, dev(zl_=z))

    PS, PO, PR = B["PS"], B["PO"], B["PR"]
    for i in range(X):
        PS[i] = dot(a2, gpT[i * C + co], 1, 0).astype(BF).reshape(ZL, rb, qw)
    send(PS, PR, "p", 0, sib)
    for i in range(X):
        PO[i] = dot(a2, gpT[i * C + c], 1, 0).reshape(ZL, rb, qw)
    got(PR, "p", 0)
    DXs, DXr = B["DXs"], B["DXr"]
    for d in range(1, X):
        x_ = up(x, d, X)
        DXs[d - 1] = (PO[x_] + PR[x_].astype(F32)).astype(BF)
        send(DXs.at[d - 1], DXr.at[d - 1], "dx", d - 1, dev(x_=x_))
    for d in range(1, ZL):
        got(GA.at[down(zl, d, ZL)], "ga", d - 1)

    def backward(half, m):
        outs = [None] * bpd
        for j in range(PER):
            k = (half * Q + m) * PER + j
            back = dot(GA[itab[2, k]], tv[itab[0, k]], 1, 0)
            for b in range(bpd):
                term = ftab[bpd + b, k] * back
                outs[b] = term if j == 0 else outs[b] + term
        return outs

    def contribute(half, core, into):
        step = 2 if X % 2 == 0 else 1

        def some(i, carry):
            for n in range(step):
                for b, out in enumerate(backward(half, (i * step + n) * C + core)):
                    into[i * step + n, b] = out.astype(into.dtype)
            return carry
        lax.fori_loop(0, X // step, some, 0)

    Dsib, Drec, Dkeep = (B["Dsib0"], B["Dsib1"]), (B["Drec0"], B["Drec1"]), (B["Dkeep0"], B["Dkeep1"])
    EXs, EXr = (B["EXs0"], B["EXs1"]), (B["EXr0"], B["EXr1"])

    def cut(i):
        return pl.ds(i * size, size)

    whole = pl.ds(0, bpd)

    def to_x(n, at=whole, i=0):
        for d in range(1, X):
            x_ = up(x, d, X)
            EXs[n][d - 1, at] = (Dkeep[n][x_, at] + Drec[n][x_, at].astype(F32)).astype(BF)
            send(EXs[n].at[d - 1, at], EXr[n].at[d - 1, at], "e%d" % n, i * (X - 1) + d - 1, dev(x_=x_))

    def from_x(n, at=whole, i=0):
        total = Dkeep[n][x, at] + Drec[n][x, at].astype(F32)
        for d in range(1, X):
            got(EXr[n].at[d - 1, at], "e%d" % n, i * (X - 1) + d - 1)
            total = total + EXr[n][d - 1, at].astype(F32)
        return total

    contribute(zo, co, Dsib[0])
    send(Dsib[0], Drec[0], "d0", 0, sib)
    contribute(zo, c, Dkeep[0])

    got(Drec[0], "d0", 0)
    for i in range(parts):
        to_x(0, cut(i), i)
    S32, Sb, DZr = B["S32"], B["Sb"], B["DZr"]
    total = PO[x] + PR[x].astype(F32)
    for d in range(1, X):
        got(DXr.at[d - 1], "dx", d - 1)
        total = total + DXr[d - 1].astype(F32)
    S32[...] = total
    Sb[...] = total.astype(BF)
    for d in range(1, ZL):
        z = up(zl, d, ZL)
        send(Sb.at[z], DZr.at[d - 1], "dz", d - 1, dev(zl_=z))
    contribute(zh, co, Dsib[1])
    send(Dsib[1], Drec[1], "d1", 0, sib)
    actb, actr = B["actb"], B["actr"]
    pre = preT[y]
    actb[...] = (pre * jax.nn.sigmoid(pre)).T.astype(BF).reshape(ZL, rb, tb)
    actr[zl] = actb[zl]
    for d in range(1, ZL):
        z = up(zl, d, ZL)
        send(actb.at[z], actr.at[zl], "act", d - 1, dev(zl_=z))
    contribute(zh, c, Dkeep[1])
    for b in range(bpd):
        Dkeep[1][x, b] = ftab[2 * bpd, b] * dot(GA[b], tv[b], 1, 0)
    total = S32[zl]
    for d in range(1, ZL):
        got(DZr.at[d - 1], "dz", d - 1)
        total = total + DZr[d - 1].astype(F32)
    Ts, Tr, OutW = B["Ts"], B["Tr"], B["OutW"]
    Ts[...] = total
    send(Ts, Tr, "dt", 0, anti)
    FZs, FZr = B["FZs"], B["FZr"]
    for i in range(parts):
        at = cut(i)
        FZs[at] = from_x(0, at, i).astype(BF)
        if i < parts - 1:
            send(FZs.at[at], B["FR"], "fr", 0, dev_z(-1))
        else:
            send(FZs.at[at], FZr.at[at], "gz", i, anti)
    if parts > 1:
        got(B["FR"], "fr", 0)
        send(B["FR"], FZr.at[cut(0)], "gz", 0, dev_z(1 - ZL))
    got(Drec[1], "d1", 0)
    to_x(1)
    for d in range(1, ZL):
        got(actr.at[down(zl, d, ZL)], "act", d - 1)
    for b in range(bpd):
        act_o[:, b * tb:(b + 1) * tb] = actr[b]
    got(Tr, "dt", 0)
    OutW[me] = Ts[...] + Tr[...]
    others = [(d, e) for d in range(X) for e in range(C) if d or e]
    for n, (d, e) in enumerate(others):
        to = dev(x_=up(x, d, X), c_=(co if e else c))
        send(OutW.at[me], OutW.at[me], "ow", n, to)
    own = from_x(1)
    for n, (d, e) in enumerate(others):
        got(OutW.at[down(x, d, X) * C + (co if e else c)], "ow", n)
    for q in range(Q):
        gw_o[:, q * qw:(q + 1) * qw] = OutW[q]
    for i in range(parts):
        got(FZr.at[cut(i)], "gz", i)
    own = (own + FZr[...].astype(F32)).astype(BF)
    for b in range(bpd):
        gf_o[:, b * tb:(b + 1) * tb] = own[b]
    for cp in sent:
        cp.wait_send()


def on_device(cfg, features_t, tile_dst, tile_src, tile_edges, tile_values, weight, cotangent):
    rb = features_t.shape[0]
    nt, tb = tile_values.shape[:2]
    bufs, sems, smem = shapes(cfg, rb, tb, nt)
    vm, hbm = pl.BlockSpec(memory_space=pltpu.VMEM), pl.BlockSpec(memory_space=pltpu.HBM)
    kernel = functools.partial(body, cfg, tuple(bufs), tuple(sems))
    outs = (
        pltpu.VMEM(features_t.shape, BF),
        pltpu.VMEM(weight.shape, F32),
        pltpu.VMEM(features_t.shape, BF),
    )
    return pl.pallas_call(
        kernel,
        out_shape=outs,
        in_specs=[hbm] * 7,
        out_specs=(vm, vm, vm),
        scratch_shapes=[pltpu.VMEM(s, t) for s, t in bufs.values()]
        + [pltpu.SemaphoreType.DMA((n,)) for n in sems.values()] * 2
        + [pltpu.SemaphoreType.DMA((9,))]
        + [pltpu.SMEM(s, t) for s, t in smem.values()],
        compiler_params=pltpu.CompilerParams(
            collective_id=0, has_side_effects=True, vmem_limit_bytes=62 * 1024 * 1024
        ),
        name="graph_conv",
    )(features_t, tile_values, weight, cotangent, *(v.reshape(1, nt) for v in (tile_dst, tile_src, tile_edges)))


def solution(mesh, cfg=None):
    in_specs = (
        P("rep", "blk"),
        P("blk"),
        P("blk"),
        P("blk"),
        P("blk", None, None),
        P("rep", None),
        P("rep", "blk"),
    )
    out_specs = (P("rep", "blk"), P("rep", None), P("rep", "blk"))
    return jax.shard_map(
        functools.partial(on_device, cfg or FULL), mesh=mesh, in_specs=in_specs, out_specs=out_specs, check_vma=False
    )
```

```python
import functools

import jax
import jax.numpy as jnp
from jax import lax
from jax.experimental import pallas as pl
from jax.experimental.pallas import tpu as pltpu
from jax.sharding import PartitionSpec as P

FULL = dict(ZH=2, X=4, C=2, Y=4, ZL=8)
PER = 4
MESH = pl.DeviceIdType.MESH
BF = jnp.bfloat16
F32 = jnp.float32


def dot(a, b, ca, cb):
    return lax.dot_general(a, b, (((ca,), (cb,)), ((), ())), preferred_element_type=F32)


def shapes(cfg, rb, tb, nt):
    X, C, Y, ZL = cfg["X"], cfg["C"], cfg["Y"], cfg["ZL"]
    Q = X * C
    F = rb * Y * ZL
    qw = F // Q
    bpd = ZL
    x1, y1 = max(X - 1, 1), max(Y - 1, 1)
    nk = -(-cfg["ZH"] * Q * PER // 128) * 128
    bufs = dict(
        fv=((rb, bpd * tb), BF),
        wv=((rb, F), BF),
        cv=((rb, bpd * tb), BF),
        dv=((1, nt), jnp.int32),
        sv=((1, nt), jnp.int32),
        ev=((1, nt), jnp.int32),
        itv=((8, nk), jnp.int32),
        ftv=((2 * bpd + 8, nk), F32),
        gown=((X, C, bpd, rb, tb), BF),
        goth=((X, C, bpd, rb, tb), BF),
        tv=((nt, tb, tb), BF),
        CWs=((ZL, 2, rb, qw), BF),
        CWr=((ZL, 2, rb, qw), BF),
        wb=((Q, rb, qw), BF),
        wg=((Y, C, X, ZL, rb, qw), BF),
        aggb=((bpd, rb, tb), BF),
        A=((ZL, rb, tb), BF),
        ctT=((Y, tb, rb * ZL), BF),
        AT=((Y, tb, rb * ZL), BF),
        preT=((X, tb, C * qw), F32),
        gpT=((Q, tb, qw), BF),
        ADs=((ZL, 2, rb, tb), BF),
        ADr=((ZL, 2, rb, tb), BF),
        gab=((ZL, rb, tb), BF),
        GA=((bpd, rb, tb), BF),
        PS=((X, ZL, rb, qw), BF),
        PO=((X, ZL, rb, qw), F32),
        PR=((X, ZL, rb, qw), BF),
        DXs=((x1, ZL, rb, qw), BF),
        DXr=((x1, ZL, rb, qw), BF),
        S32=((ZL, rb, qw), F32),
        Ts=((rb, qw), F32),
        Tr=((rb, qw), F32),
        OutW=((Q, rb, qw), F32),
        Dsib0=((X, bpd, rb, tb), BF),
        Dsib1=((X, bpd, rb, tb), BF),
        Drec0=((X, bpd, rb, tb), BF),
        Drec1=((X, bpd, rb, tb), BF),
        Dkeep0=((X, bpd, rb, tb), F32),
        Dkeep1=((X, bpd, rb, tb), F32),
        EXs0=((x1, bpd, rb, tb), BF),
        EXs1=((x1, bpd, rb, tb), BF),
        EXr0=((x1, bpd, rb, tb), BF),
        EXr1=((x1, bpd, rb, tb), BF),
        FZs=((bpd, rb, tb), BF),
        FZr=((bpd, rb, tb), BF),
    )
    sems = dict(
        fz=1, fx0=1, fx1=x1, fc0=1, fc1=1, cw=1, w2=1, w3=Y, w4=2, w5=2, cty=1, ag=1, agy=y1, ga=1,
        p=1, dx=1, ad=1, dt=1, ow=1, d0=1, d1=1, e0=2, e1=1, gz=2,
    )
    smem = dict(itab=((8, nk), jnp.int32), ftab=((2 * bpd + 8, nk), F32))
    return bufs, sems, smem


def tables(bpd, dst, src, edges, itv, ftv):
    nt = dst.shape[1]
    nk = itv.shape[1]
    r0 = lax.broadcasted_iota(jnp.int32, (nt, nt), 0)
    r1 = lax.broadcasted_iota(jnp.int32, (nt, nt), 1)
    k1 = lax.broadcasted_iota(jnp.int32, (nt, nk), 1)
    t0 = lax.broadcasted_iota(jnp.int32, (nt, nk), 0)
    lane = lax.broadcasted_iota(jnp.int32, (1, nt), 1)

    def column(row):
        return jnp.sum(jnp.where(r0 == r1, row, jnp.zeros_like(row)), axis=1, keepdims=True)

    bits = bpd.bit_length() - 1
    group = jnp.where((edges > 0) & (lane >= bpd), lax.shift_right_logical(src, bits), -1)
    group_c = column(group)
    rank = jnp.sum(jnp.where((group_c == group) & (r1 < r0), 1, 0), axis=1, keepdims=True)
    pick = jnp.where(group_c >= 0, group_c * PER + rank, -1) == k1

    def by_k(col):
        return jnp.sum(jnp.where(pick, col, jnp.zeros_like(col)), axis=0, keepdims=True)

    at_src, at_dst = by_k(column(src & (bpd - 1))), by_k(column(dst))
    itv[0:1] = by_k(t0)
    itv[1:2] = at_src
    itv[2:3] = at_dst
    blocks = lax.broadcasted_iota(jnp.int32, (bpd, nt), 0)
    weights = jnp.where(dst == blocks, edges.astype(F32), 0.0)
    coef = jnp.sum(weights / jnp.sum(weights, axis=1, keepdims=True), axis=0, keepdims=True)
    coef_k = by_k(column(coef))
    blocks = lax.broadcasted_iota(jnp.int32, (bpd, nk), 0)
    ftv[0:bpd] = jnp.where(at_dst == blocks, coef_k, 0.0)
    ftv[bpd:2 * bpd] = jnp.where(at_src == blocks, coef_k, 0.0)
    ftv[2 * bpd:2 * bpd + 1, 0:nt] = coef


def body(cfg, buf_names, sem_names, feat_hbm, tv_hbm, w_hbm, cot_hbm, dst_hbm, src_hbm, edge_hbm, act_o, gw_o, gf_o, *scr):
    ZH, X, C, Y, ZL = cfg["ZH"], cfg["X"], cfg["C"], cfg["Y"], cfg["ZL"]
    nb, ns = len(buf_names), len(sem_names)
    B = dict(zip(buf_names, scr[:nb]))
    SS = dict(zip(sem_names, scr[nb:nb + ns]))
    RS = dict(zip(sem_names, scr[nb + ns:nb + 2 * ns]))
    load_sem, itab, ftab = scr[nb + 2 * ns:]
    feat, w, cot = B["fv"], B["wv"], B["cv"]
    Q = X * C
    bpd = ZL
    rb, tb = B["A"].shape[1:]
    qw = B["wb"].shape[2]
    rows = ZL * rb

    blk, rep = lax.axis_index("blk"), lax.axis_index("rep")
    zh = lax.div(blk, Q)
    me = lax.rem(blk, Q)
    x, c = lax.div(me, C), lax.rem(me, C)
    y, zl = lax.div(rep, ZL), lax.rem(rep, ZL)
    zo, co = 1 - zh, 1 - c

    def dev(zh_=zh, x_=x, c_=c, y_=y, zl_=zl):
        return ((zh_ * X + x_) * C + c_, y_ * ZL + zl_)

    def up(v, d, n):
        return lax.rem(v + d, n)

    def down(v, d, n):
        return lax.rem(v + n - d, n)

    anti, sib = dev(zh_=zo), dev(c_=co)
    sent = []

    def copy(src, dst, name, i, to):
        return pltpu.make_async_remote_copy(
            src_ref=src, dst_ref=dst, send_sem=SS[name].at[i], recv_sem=RS[name].at[i],
            device_id=to, device_id_type=MESH,
        )

    def send(src, dst, name, i, to):
        cp = copy(src, dst, name, i, to)
        cp.start()
        sent.append(cp)

    def send_all(copies, size_ref, name, i=0):
        for src, dst, to in copies:
            copy(src, dst, name, i, to).start()
        if copies:
            sent.append(copy(size_ref, size_ref, name, i, sib))

    def got(dst, name, i):
        copy(dst, dst, name, i, sib).wait_recv()

    loads = [
        pltpu.make_async_copy(a, b, load_sem.at[i])
        for i, (a, b) in enumerate((
            (feat_hbm, feat), (w_hbm, w), (cot_hbm, cot), (tv_hbm, B["tv"]),
            (dst_hbm, B["dv"]), (src_hbm, B["sv"]), (edge_hbm, B["ev"]),
        ))
    ]
    for ld in loads:
        ld.start()

    barrier = pltpu.get_barrier_semaphore()
    partners = [anti]
    partners += [dev(x_=up(x, d, X), c_=(c if e == 0 else co)) for d in range(X) for e in range(C) if d or e]
    partners += [dev(zl_=up(zl, d, ZL)) for d in range(1, ZL)]
    partners += [dev(y_=up(y, d, Y)) for d in range(1, Y)]
    for p in partners:
        pl.semaphore_signal(barrier, inc=1, device_id=p, device_id_type=MESH)

    gown, goth, tv = B["gown"], B["goth"], B["tv"]
    loads[0].wait()
    for b in range(bpd):
        gown[x, c, b] = feat[:, b * tb:(b + 1) * tb]
    pl.semaphore_wait(barrier, len(partners))

    xs = [up(x, d, X) for d in range(1, X)]
    zs = [up(zl, d, ZL) for d in range(1, ZL)]
    send(gown.at[x, c], goth.at[x, c], "fz", 0, anti)
    send_all([(gown.at[x, c], gown.at[x, c], dev(x_=v)) for v in xs], gown.at[pl.ds(0, X - 1), 0], "fx0")
    for ld in loads[4:]:
        ld.wait()
    tables(bpd, B["dv"][...], B["sv"][...], B["ev"][...], B["itv"], B["ftv"])
    to_smem = [
        pltpu.make_async_copy(B["itv"], itab, load_sem.at[7]),
        pltpu.make_async_copy(B["ftv"], ftab, load_sem.at[8]),
    ]
    for cp in to_smem:
        cp.start()
    loads[1].wait()
    loads[2].wait()
    for q in range(Q):
        B["wb"][q] = w[:, q * qw:(q + 1) * qw]
    CWs, CWr, wg = B["CWs"], B["CWr"], B["wg"]
    for b in range(bpd):
        CWs[b, 0] = cot[:, b * tb:(b + 1) * tb]
        CWs[b, 1] = B["wb"][me]
    CWr[zl] = CWs[zl]
    got(gown.at[pl.ds(0, X - 1), 0], "fx0", 0)
    send(gown.at[:, c], gown.at[:, c], "fc0", 0, sib)
    loads[3].wait()
    for cp in to_smem:
        cp.wait()
    acc = tuple(ftab[2 * bpd, b] * dot(gown[x, c, b], tv[b], 1, 1) for b in range(bpd))

    def forward(g, half, i, acc):
        acc = list(acc)
        for j in range(C * PER):
            k = (half * Q + i * C) * PER + j
            out = dot(g[i, j // PER, itab[1, k]], tv[itab[0, k]], 1, 1)
            for b in range(bpd):
                acc[b] = acc[b] + ftab[b, k] * out
        return tuple(acc)

    got(goth.at[x, c], "fz", 0)
    for d in range(1, X):
        send(goth.at[x, c], goth.at[x, c], "fx1", d - 1, dev(x_=up(x, d, X)))
    send_all([(CWs.at[z], CWr.at[zl], dev(zl_=z)) for z in zs], CWr.at[pl.ds(0, ZL - 1)], "cw")
    got(gown.at[:, co], "fc0", 0)
    acc = lax.fori_loop(0, Q // C, lambda i, a: forward(gown, zh, i, a), acc)
    fc1 = [(goth.at[x, c], goth.at[x, c], sib)]
    for d in range(1, X):
        part = goth.at[down(x, d, X), c]
        got(part, "fx1", d - 1)
        fc1.append((part, part, sib))
    send_all(fc1, goth.at[:, c], "fc1")
    if ZL > 1:
        got(CWr.at[pl.ds(0, ZL - 1)], "cw", 0)
    wg[y, c, x] = CWr[:, 1]
    part = wg.at[y, c, x]
    send_all([(part, part, dev(x_=v)) for v in xs], wg.at[y, c, pl.ds(0, X - 1)], "w2")
    ctT, AT = B["ctT"], B["AT"]
    ctT[y] = CWr[:, 0].reshape(rows, tb).astype(F32).T.astype(BF)
    ys = [up(y, d, Y) for d in range(1, Y)]
    send_all([(ctT.at[y], ctT.at[y], dev(y_=v)) for v in ys], ctT.at[pl.ds(0, Y - 1)], "cty")
    got(goth.at[:, co], "fc1", 0)
    acc = lax.fori_loop(0, Q // C, lambda i, a: forward(goth, zo, i, a), acc)

    A = B["A"]
    for b in range(bpd):
        B["aggb"][b] = acc[b].astype(BF)
    A[zl] = B["aggb"][zl]
    send_all([(B["aggb"].at[z], A.at[zl], dev(zl_=z)) for z in zs], A.at[pl.ds(0, ZL - 1)], "ag")
    got(wg.at[y, c, pl.ds(0, X - 1)], "w2", 0)
    y_up, y_down, y_far = up(y, 1, Y), down(y, 1, Y), up(y, 2, Y)
    send(wg.at[y, c], wg.at[y, c], "w4", 0, dev(y_=y_up))
    if Y > 2:
        send(wg.at[y, c], wg.at[y, c], "w4", 1, dev(y_=y_down))
    send(wg.at[y, c], wg.at[y, c], "w3", 0, sib)
    if ZL > 1:
        got(A.at[pl.ds(0, ZL - 1)], "ag", 0)

    a2 = A[...].reshape(rows, tb)
    AT[y] = a2.astype(F32).T.astype(BF)
    for d in range(1, Y):
        send(AT.at[y], AT.at[y], "agy", d - 1, dev(y_=up(y, d, Y)))

    def weight_of(y_, i):
        return jnp.concatenate([wg[y_, e, i].reshape(rows, qw) for e in range(C)], axis=1)

    preT, gpT = B["preT"], B["gpT"]
    got(wg.at[y, co], "w3", 0)
    for i in range(X):
        preT[i] = dot(AT[y], weight_of(y, i), 1, 0)
    half = X // 2
    got(wg.at[y_down, c], "w4", 0)
    send(wg.at[y_down, c], wg.at[y_down, c], "w3", 1, sib)
    if Y > 2:
        part = wg.at[y_down, c, pl.ds(0, half)]
        send(part, part, "w5", 0, dev(y_=y_up))
        got(wg.at[y_up, c], "w4", 1)
        part = wg.at[y_up, c, pl.ds(half, half)]
        send(part, part, "w5", 1, dev(y_=y_down))
        send(wg.at[y_up, c], wg.at[y_up, c], "w3", 2, sib)
    got(ctT.at[pl.ds(0, Y - 1)], "cty", 0)
    order = [(1, 1), (3, 2), (2, 3)] if Y > 2 else [(1, 1)]
    for n, (d, at) in enumerate(order):
        y_ = down(y, d, Y)
        if d == 2:
            got(wg.at[y_far, c, pl.ds(0, half)], "w5", 0)
            got(wg.at[y_far, c, pl.ds(half, half)], "w5", 1)
            send(wg.at[y_far, c], wg.at[y_far, c], "w3", 3, sib)
        got(AT.at[y_], "agy", d - 1)
        got(wg.at[y_, co], "w3", at)
        for i in range(X):
            pre = preT[i] + dot(AT[y_], weight_of(y_, i), 1, 0)
            preT[i] = pre
            if n == len(order) - 1:
                sig = jax.nn.sigmoid(pre)
                gp = (ctT[i].astype(F32) * sig * (1.0 + pre * (1.0 - sig))).astype(BF)
                for e in range(C):
                    gpT[i * C + e] = gp[:, e * qw:(e + 1) * qw]

    def grad_pre(i):
        return jnp.concatenate([gpT[i * C + e] for e in range(C)], axis=1)

    ga = dot(weight_of(y, 0), grad_pre(0), 1, 1)
    for i in range(1, X):
        ga = ga + dot(weight_of(y, i), grad_pre(i), 1, 1)
    gab, GA = B["gab"], B["GA"]
    gab[...] = ga.astype(BF).reshape(ZL, rb, tb)
    GA[zl] = gab[zl]
    send_all([(gab.at[z], GA.at[zl], dev(zl_=z)) for z in zs], GA.at[pl.ds(0, ZL - 1)], "ga")

    PS, PO, PR = B["PS"], B["PO"], B["PR"]
    for i in range(X):
        PS[i] = dot(a2, gpT[i * C + co], 1, 0).astype(BF).reshape(ZL, rb, qw)
    send(PS, PR, "p", 0, sib)
    for i in range(X):
        PO[i] = dot(a2, gpT[i * C + c], 1, 0).reshape(ZL, rb, qw)
    got(PR, "p", 0)
    DXs, DXr = B["DXs"], B["DXr"]
    for d in range(1, X):
        x_ = up(x, d, X)
        DXs[d - 1] = (PO[x_] + PR[x_].astype(F32)).astype(BF)
    send_all([(DXs.at[n], DXr.at[n], dev(x_=v)) for n, v in enumerate(xs)], DXr, "dx")
    ADs, ADr = B["ADs"], B["ADr"]
    pre = preT[y]
    ADs[:, 0] = (pre * jax.nn.sigmoid(pre)).T.astype(BF).reshape(ZL, rb, tb)
    if ZL > 1:
        got(GA.at[pl.ds(0, ZL - 1)], "ga", 0)

    def backward(half, m):
        outs = [None] * bpd
        for j in range(PER):
            k = (half * Q + m) * PER + j
            back = dot(GA[itab[2, k]], tv[itab[0, k]], 1, 0)
            for b in range(bpd):
                term = ftab[bpd + b, k] * back
                outs[b] = term if j == 0 else outs[b] + term
        return outs

    def contribute(half, core, into):
        step = 2 if X % 2 == 0 else 1

        def some(i, carry):
            for n in range(step):
                for b, out in enumerate(backward(half, (i * step + n) * C + core)):
                    into[i * step + n, b] = out.astype(into.dtype)
            return carry
        lax.fori_loop(0, X // step, some, 0)

    Dsib, Drec, Dkeep = (B["Dsib0"], B["Dsib1"]), (B["Drec0"], B["Drec1"]), (B["Dkeep0"], B["Dkeep1"])
    EXs, EXr = (B["EXs0"], B["EXs1"]), (B["EXr0"], B["EXr1"])

    parts = 2 if bpd % 2 == 0 else 1

    def cut(i):
        return pl.ds(i * (bpd // parts), bpd // parts)

    whole = pl.ds(0, bpd)

    def to_x(n, at=whole, i=0):
        for d, v in enumerate(xs):
            EXs[n][d, at] = (Dkeep[n][v, at] + Drec[n][v, at].astype(F32)).astype(BF)
        send_all(
            [(EXs[n].at[d, at], EXr[n].at[d, at], dev(x_=v)) for d, v in enumerate(xs)],
            EXr[n].at[:, at], "e%d" % n, i,
        )

    def from_x(n, at=whole, i=0):
        got(EXr[n].at[:, at], "e%d" % n, i)
        total = Dkeep[n][x, at] + Drec[n][x, at].astype(F32)
        for d in range(X - 1):
            total = total + EXr[n][d, at].astype(F32)
        return total

    contribute(zo, co, Dsib[0])
    send(Dsib[0], Drec[0], "d0", 0, sib)
    contribute(zo, c, Dkeep[0])

    got(Drec[0], "d0", 0)
    for i in range(parts):
        to_x(0, cut(i), i)
    S32 = B["S32"]
    got(DXr, "dx", 0)
    total = PO[x] + PR[x].astype(F32)
    for d in range(X - 1):
        total = total + DXr[d].astype(F32)
    S32[...] = total
    ADs[:, 1] = total.astype(BF)
    ADr[zl] = ADs[zl]
    send_all([(ADs.at[z], ADr.at[zl], dev(zl_=z)) for z in zs], ADr.at[pl.ds(0, ZL - 1)], "ad")
    contribute(zh, co, Dsib[1])
    send(Dsib[1], Drec[1], "d1", 0, sib)
    contribute(zh, c, Dkeep[1])
    for b in range(bpd):
        Dkeep[1][x, b] = ftab[2 * bpd, b] * dot(GA[b], tv[b], 1, 0)
    total = S32[zl]
    if ZL > 1:
        got(ADr.at[pl.ds(0, ZL - 1)], "ad", 0)
    for d in range(1, ZL):
        total = total + ADr[down(zl, d, ZL), 1].astype(F32)
    Ts, Tr, OutW = B["Ts"], B["Tr"], B["OutW"]
    Ts[...] = total
    send(Ts, Tr, "dt", 0, anti)
    FZs, FZr = B["FZs"], B["FZr"]
    for i in range(parts):
        at = cut(i)
        FZs[at] = from_x(0, at, i).astype(BF)
        send(FZs.at[at], FZr.at[at], "gz", i, anti)
    got(Drec[1], "d1", 0)
    to_x(1)
    for b in range(bpd):
        act_o[:, b * tb:(b + 1) * tb] = ADr[b, 0]
    got(Tr, "dt", 0)
    OutW[me] = Ts[...] + Tr[...]
    others = [(d, e) for d in range(X) for e in range(C) if d or e]
    tos = [dev(x_=up(x, d, X), c_=(co if e else c)) for d, e in others]
    send_all([(OutW.at[me], OutW.at[me], to) for to in tos], OutW.at[pl.ds(0, Q - 1)], "ow")
    own = from_x(1)
    got(OutW.at[pl.ds(0, Q - 1)], "ow", 0)
    for q in range(Q):
        gw_o[:, q * qw:(q + 1) * qw] = OutW[q]
    for cp in sent:
        cp.wait_send()
    for i in range(parts):
        got(FZr.at[cut(i)], "gz", i)
    own = (own + FZr[...].astype(F32)).astype(BF)
    for b in range(bpd):
        gf_o[:, b * tb:(b + 1) * tb] = own[b]


def on_device(cfg, features_t, tile_dst, tile_src, tile_edges, tile_values, weight, cotangent):
    rb = features_t.shape[0]
    nt, tb = tile_values.shape[:2]
    bufs, sems, smem = shapes(cfg, rb, tb, nt)
    vm, hbm = pl.BlockSpec(memory_space=pltpu.VMEM), pl.BlockSpec(memory_space=pltpu.HBM)
    kernel = functools.partial(body, cfg, tuple(bufs), tuple(sems))
    outs = (
        pltpu.VMEM(features_t.shape, BF),
        pltpu.VMEM(weight.shape, F32),
        pltpu.VMEM(features_t.shape, BF),
    )
    return pl.pallas_call(
        kernel,
        out_shape=outs,
        in_specs=[hbm] * 7,
        out_specs=(vm, vm, vm),
        scratch_shapes=[pltpu.VMEM(s, t) for s, t in bufs.values()]
        + [pltpu.SemaphoreType.DMA((n,)) for n in sems.values()] * 2
        + [pltpu.SemaphoreType.DMA((9,))]
        + [pltpu.SMEM(s, t) for s, t in smem.values()],
        compiler_params=pltpu.CompilerParams(
            collective_id=0, has_side_effects=True, vmem_limit_bytes=62 * 1024 * 1024
        ),
        name="graph_conv",
    )(features_t, tile_values, weight, cotangent, *(v.reshape(1, nt) for v in (tile_dst, tile_src, tile_edges)))


def solution(mesh, cfg=None):
    in_specs = (
        P("rep", "blk"),
        P("blk"),
        P("blk"),
        P("blk"),
        P("blk", None, None),
        P("rep", None),
        P("rep", "blk"),
    )
    out_specs = (P("rep", "blk"), P("rep", None), P("rep", "blk"))
    return jax.shard_map(
        functools.partial(on_device, cfg or FULL), mesh=mesh, in_specs=in_specs, out_specs=out_specs, check_vma=False
    )
```

```python
import functools

import jax
import jax.numpy as jnp
from jax import lax
from jax.experimental import pallas as pl
from jax.experimental.pallas import tpu as pltpu
from jax.sharding import PartitionSpec as P

FULL = dict(ZH=2, X=4, C=2, Y=4, ZL=8)
PER = 4
MESH = pl.DeviceIdType.MESH
BF = jnp.bfloat16
F32 = jnp.float32


def dot(a, b, ca, cb):
    return lax.dot_general(a, b, (((ca,), (cb,)), ((), ())), preferred_element_type=F32)


def shapes(cfg, rb, tb, nt):
    X, C, Y, ZL = cfg["X"], cfg["C"], cfg["Y"], cfg["ZL"]
    Q = X * C
    F = rb * Y * ZL
    qw = F // Q
    bpd = ZL
    x1, y1 = max(X - 1, 1), max(Y - 1, 1)
    nk = -(-cfg["ZH"] * Q * PER // 128) * 128
    bufs = dict(
        fv=((rb, bpd * tb), BF),
        wv=((rb, F), BF),
        cv=((rb, bpd * tb), BF),
        dv=((1, nt), jnp.int32),
        sv=((1, nt), jnp.int32),
        ev=((1, nt), jnp.int32),
        itv=((8, nk), jnp.int32),
        ftv=((2 * bpd + 8, nk), F32),
        gown=((X, C, bpd, rb, tb), BF),
        goth=((X, C, bpd, rb, tb), BF),
        tv=((nt, tb, tb), BF),
        cb=((bpd, rb, tb), BF),
        ct=((ZL, rb, tb), BF),
        wb=((Q, rb, qw), BF),
        wg=((Y, C, X, ZL, rb, qw), BF),
        aggb=((bpd, rb, tb), BF),
        A=((ZL, rb, tb), BF),
        ctT=((Y, tb, rb * ZL), BF),
        AT=((Y, tb, rb * ZL), BF),
        preT=((X, tb, C * qw), F32),
        gpT=((Q, tb, qw), BF),
        ADs=((ZL, 2, rb, tb), BF),
        ADr=((ZL, 2, rb, tb), BF),
        gab=((ZL, rb, tb), BF),
        GA=((bpd, rb, tb), BF),
        PS=((X, ZL, rb, qw), BF),
        PO=((X, ZL, rb, qw), F32),
        PR=((X, ZL, rb, qw), BF),
        DXs=((x1, ZL, rb, qw), BF),
        DXr=((x1, ZL, rb, qw), BF),
        S32=((ZL, rb, qw), F32),
        Ts=((rb, qw), F32),
        Tr=((rb, qw), F32),
        OutW=((Q, rb, qw), F32),
        Dsib0=((X, bpd, rb, tb), BF),
        Dsib1=((X, bpd, rb, tb), BF),
        Drec0=((X, bpd, rb, tb), BF),
        Drec1=((X, bpd, rb, tb), BF),
        Dkeep0=((X, bpd, rb, tb), F32),
        Dkeep1=((X, bpd, rb, tb), F32),
        EXs0=((x1, bpd, rb, tb), BF),
        EXs1=((x1, bpd, rb, tb), BF),
        EXr0=((x1, bpd, rb, tb), BF),
        EXr1=((x1, bpd, rb, tb), BF),
        FZs=((bpd, rb, tb), BF),
        FZr=((bpd, rb, tb), BF),
    )
    sems = dict(
        fz=1, fx0=1, fx1=x1, fc0=1, fc1=1, w1=1, ct=1, w2=1, w3=Y, w4=2, w5=2, cty=1, ag=1, agy=y1, ga=1,
        p=1, dx=1, ad=1, dt=1, ow=1, d0=1, d1=1, e0=2, e1=1, gz=2,
    )
    smem = dict(itab=((8, nk), jnp.int32), ftab=((2 * bpd + 8, nk), F32))
    return bufs, sems, smem


def tables(bpd, dst, src, edges, itv, ftv):
    nt = dst.shape[1]
    nk = itv.shape[1]
    r0 = lax.broadcasted_iota(jnp.int32, (nt, nt), 0)
    r1 = lax.broadcasted_iota(jnp.int32, (nt, nt), 1)
    k1 = lax.broadcasted_iota(jnp.int32, (nt, nk), 1)
    t0 = lax.broadcasted_iota(jnp.int32, (nt, nk), 0)
    lane = lax.broadcasted_iota(jnp.int32, (1, nt), 1)

    def column(row):
        return jnp.sum(jnp.where(r0 == r1, row, jnp.zeros_like(row)), axis=1, keepdims=True)

    bits = bpd.bit_length() - 1
    group = jnp.where((edges > 0) & (lane >= bpd), lax.shift_right_logical(src, bits), -1)
    group_c = column(group)
    rank = jnp.sum(jnp.where((group_c == group) & (r1 < r0), 1, 0), axis=1, keepdims=True)
    pick = jnp.where(group_c >= 0, group_c * PER + rank, -1) == k1

    def by_k(col):
        return jnp.sum(jnp.where(pick, col, jnp.zeros_like(col)), axis=0, keepdims=True)

    at_src, at_dst = by_k(column(src & (bpd - 1))), by_k(column(dst))
    itv[0:1] = by_k(t0)
    itv[1:2] = at_src
    itv[2:3] = at_dst
    blocks = lax.broadcasted_iota(jnp.int32, (bpd, nt), 0)
    weights = jnp.where(dst == blocks, edges.astype(F32), 0.0)
    coef = jnp.sum(weights / jnp.sum(weights, axis=1, keepdims=True), axis=0, keepdims=True)
    coef_k = by_k(column(coef))
    blocks = lax.broadcasted_iota(jnp.int32, (bpd, nk), 0)
    ftv[0:bpd] = jnp.where(at_dst == blocks, coef_k, 0.0)
    ftv[bpd:2 * bpd] = jnp.where(at_src == blocks, coef_k, 0.0)
    ftv[2 * bpd:2 * bpd + 1, 0:nt] = coef


def body(cfg, buf_names, sem_names, feat_hbm, tv_hbm, w_hbm, cot_hbm, dst_hbm, src_hbm, edge_hbm, act_o, gw_o, gf_o, *scr):
    ZH, X, C, Y, ZL = cfg["ZH"], cfg["X"], cfg["C"], cfg["Y"], cfg["ZL"]
    nb, ns = len(buf_names), len(sem_names)
    B = dict(zip(buf_names, scr[:nb]))
    SS = dict(zip(sem_names, scr[nb:nb + ns]))
    RS = dict(zip(sem_names, scr[nb + ns:nb + 2 * ns]))
    load_sem, itab, ftab = scr[nb + 2 * ns:]
    feat, w, cot = B["fv"], B["wv"], B["cv"]
    Q = X * C
    bpd = ZL
    rb, tb = B["A"].shape[1:]
    qw = B["wb"].shape[2]
    rows = ZL * rb

    blk, rep = lax.axis_index("blk"), lax.axis_index("rep")
    zh = lax.div(blk, Q)
    me = lax.rem(blk, Q)
    x, c = lax.div(me, C), lax.rem(me, C)
    y, zl = lax.div(rep, ZL), lax.rem(rep, ZL)
    zo, co = 1 - zh, 1 - c

    def dev(zh_=zh, x_=x, c_=c, y_=y, zl_=zl):
        return ((zh_ * X + x_) * C + c_, y_ * ZL + zl_)

    def up(v, d, n):
        return lax.rem(v + d, n)

    def down(v, d, n):
        return lax.rem(v + n - d, n)

    anti, sib = dev(zh_=zo), dev(c_=co)
    sent = []

    def copy(src, dst, name, i, to):
        return pltpu.make_async_remote_copy(
            src_ref=src, dst_ref=dst, send_sem=SS[name].at[i], recv_sem=RS[name].at[i],
            device_id=to, device_id_type=MESH,
        )

    def send(src, dst, name, i, to):
        cp = copy(src, dst, name, i, to)
        cp.start()
        sent.append(cp)

    def send_all(copies, size_ref, name, i=0):
        for src, dst, to in copies:
            copy(src, dst, name, i, to).start()
        if copies:
            sent.append(copy(size_ref, size_ref, name, i, sib))

    def got(dst, name, i):
        copy(dst, dst, name, i, sib).wait_recv()

    loads = [
        pltpu.make_async_copy(a, b, load_sem.at[i])
        for i, (a, b) in enumerate((
            (feat_hbm, feat), (w_hbm, w), (cot_hbm, cot), (tv_hbm, B["tv"]),
            (dst_hbm, B["dv"]), (src_hbm, B["sv"]), (edge_hbm, B["ev"]),
        ))
    ]
    for ld in loads:
        ld.start()

    barrier = pltpu.get_barrier_semaphore()
    partners = [anti]
    partners += [dev(x_=up(x, d, X), c_=(c if e == 0 else co)) for d in range(X) for e in range(C) if d or e]
    partners += [dev(zl_=up(zl, d, ZL)) for d in range(1, ZL)]
    partners += [dev(y_=up(y, d, Y)) for d in range(1, Y)]
    for p in partners:
        pl.semaphore_signal(barrier, inc=1, device_id=p, device_id_type=MESH)

    gown, goth, tv = B["gown"], B["goth"], B["tv"]
    loads[0].wait()
    for b in range(bpd):
        gown[x, c, b] = feat[:, b * tb:(b + 1) * tb]
    loads[1].wait()
    wg, wb = B["wg"], B["wb"]
    for q in range(Q):
        wb[q] = w[:, q * qw:(q + 1) * qw]
    wg[y, c, x, zl] = wb[me]
    pl.semaphore_wait(barrier, len(partners))

    xs = [up(x, d, X) for d in range(1, X)]
    zs = [up(zl, d, ZL) for d in range(1, ZL)]
    send(gown.at[x, c], goth.at[x, c], "fz", 0, anti)
    send_all([(gown.at[x, c], gown.at[x, c], dev(x_=v)) for v in xs], gown.at[pl.ds(0, X - 1), 0], "fx0")
    send_all([(wb.at[me], wg.at[y, c, x, zl], dev(zl_=z)) for z in zs], wg.at[y, c, x, pl.ds(0, ZL - 1)], "w1")
    for ld in loads[4:]:
        ld.wait()
    tables(bpd, B["dv"][...], B["sv"][...], B["ev"][...], B["itv"], B["ftv"])
    to_smem = [
        pltpu.make_async_copy(B["itv"], itab, load_sem.at[7]),
        pltpu.make_async_copy(B["ftv"], ftab, load_sem.at[8]),
    ]
    for cp in to_smem:
        cp.start()
    loads[2].wait()
    cb, ct = B["cb"], B["ct"]
    for b in range(bpd):
        cb[b] = cot[:, b * tb:(b + 1) * tb]
    ct[zl] = cb[zl]
    got(gown.at[pl.ds(0, X - 1), 0], "fx0", 0)
    send(gown.at[:, c], gown.at[:, c], "fc0", 0, sib)
    loads[3].wait()
    for cp in to_smem:
        cp.wait()
    acc = tuple(ftab[2 * bpd, b] * dot(gown[x, c, b], tv[b], 1, 1) for b in range(bpd))

    def forward(g, half, i, acc):
        acc = list(acc)
        for j in range(C * PER):
            k = (half * Q + i * C) * PER + j
            out = dot(g[i, j // PER, itab[1, k]], tv[itab[0, k]], 1, 1)
            for b in range(bpd):
                acc[b] = acc[b] + ftab[b, k] * out
        return tuple(acc)

    part = wg.at[y, c, x]
    if ZL > 1:
        got(wg.at[y, c, x, pl.ds(0, ZL - 1)], "w1", 0)
    send_all([(part, part, dev(x_=v)) for v in xs], wg.at[y, c, pl.ds(0, X - 1)], "w2")
    got(goth.at[x, c], "fz", 0)
    for d in range(1, X):
        send(goth.at[x, c], goth.at[x, c], "fx1", d - 1, dev(x_=up(x, d, X)))
    copy(goth.at[x, c], goth.at[x, c], "fc1", 0, sib).start()
    send_all([(cb.at[z], ct.at[zl], dev(zl_=z)) for z in zs], ct.at[pl.ds(0, ZL - 1)], "ct")
    got(wg.at[y, c, pl.ds(0, X - 1)], "w2", 0)
    y_up, y_down, y_far = up(y, 1, Y), down(y, 1, Y), up(y, 2, Y)
    send(wg.at[y, c], wg.at[y, c], "w4", 0, dev(y_=y_up))
    if Y > 2:
        send(wg.at[y, c], wg.at[y, c], "w4", 1, dev(y_=y_down))
    send(wg.at[y, c], wg.at[y, c], "w3", 0, sib)
    got(gown.at[:, co], "fc0", 0)
    acc = lax.fori_loop(0, Q // C, lambda i, a: forward(gown, zh, i, a), acc)
    for d in range(1, X):
        part = goth.at[down(x, d, X), c]
        got(part, "fx1", d - 1)
        copy(part, part, "fc1", 0, sib).start()
    sent.append(copy(goth.at[:, c], goth.at[:, c], "fc1", 0, sib))
    if ZL > 1:
        got(ct.at[pl.ds(0, ZL - 1)], "ct", 0)
    ctT, AT = B["ctT"], B["AT"]
    ctT[y] = ct[...].reshape(rows, tb).astype(F32).T.astype(BF)
    ys = [up(y, d, Y) for d in range(1, Y)]
    send_all([(ctT.at[y], ctT.at[y], dev(y_=v)) for v in ys], ctT.at[pl.ds(0, Y - 1)], "cty")
    got(goth.at[:, co], "fc1", 0)
    acc = lax.fori_loop(0, Q // C, lambda i, a: forward(goth, zo, i, a), acc)

    A = B["A"]
    for b in range(bpd):
        B["aggb"][b] = acc[b].astype(BF)
    A[zl] = B["aggb"][zl]
    send_all([(B["aggb"].at[z], A.at[zl], dev(zl_=z)) for z in zs], A.at[pl.ds(0, ZL - 1)], "ag")
    half = X // 2
    got(wg.at[y_down, c], "w4", 0)
    send(wg.at[y_down, c], wg.at[y_down, c], "w3", 1, sib)
    if Y > 2:
        part = wg.at[y_down, c, pl.ds(0, half)]
        send(part, part, "w5", 0, dev(y_=y_up))
        got(wg.at[y_up, c], "w4", 1)
        part = wg.at[y_up, c, pl.ds(half, half)]
        send(part, part, "w5", 1, dev(y_=y_down))
        send(wg.at[y_up, c], wg.at[y_up, c], "w3", 2, sib)
    if ZL > 1:
        got(A.at[pl.ds(0, ZL - 1)], "ag", 0)

    a2 = A[...].reshape(rows, tb)
    AT[y] = a2.astype(F32).T.astype(BF)
    for d in range(1, Y):
        send(AT.at[y], AT.at[y], "agy", d - 1, dev(y_=up(y, d, Y)))

    def weight_of(y_, i):
        return jnp.concatenate([wg[y_, e, i].reshape(rows, qw) for e in range(C)], axis=1)

    preT, gpT = B["preT"], B["gpT"]
    got(wg.at[y, co], "w3", 0)
    for i in range(X):
        preT[i] = dot(AT[y], weight_of(y, i), 1, 0)
    got(ctT.at[pl.ds(0, Y - 1)], "cty", 0)
    order = [(1, 1), (3, 2), (2, 3)] if Y > 2 else [(1, 1)]
    for n, (d, at) in enumerate(order):
        y_ = down(y, d, Y)
        if d == 2:
            got(wg.at[y_far, c, pl.ds(0, half)], "w5", 0)
            got(wg.at[y_far, c, pl.ds(half, half)], "w5", 1)
            send(wg.at[y_far, c], wg.at[y_far, c], "w3", 3, sib)
        got(AT.at[y_], "agy", d - 1)
        got(wg.at[y_, co], "w3", at)
        for i in range(X):
            pre = preT[i] + dot(AT[y_], weight_of(y_, i), 1, 0)
            preT[i] = pre
            if n == len(order) - 1:
                sig = jax.nn.sigmoid(pre)
                gp = (ctT[i].astype(F32) * sig * (1.0 + pre * (1.0 - sig))).astype(BF)
                for e in range(C):
                    gpT[i * C + e] = gp[:, e * qw:(e + 1) * qw]

    def grad_pre(i):
        return jnp.concatenate([gpT[i * C + e] for e in range(C)], axis=1)

    ga = dot(weight_of(y, 0), grad_pre(0), 1, 1)
    for i in range(1, X):
        ga = ga + dot(weight_of(y, i), grad_pre(i), 1, 1)
    gab, GA = B["gab"], B["GA"]
    gab[...] = ga.astype(BF).reshape(ZL, rb, tb)
    GA[zl] = gab[zl]
    send_all([(gab.at[z], GA.at[zl], dev(zl_=z)) for z in zs], GA.at[pl.ds(0, ZL - 1)], "ga")

    PS, PO, PR = B["PS"], B["PO"], B["PR"]
    for i in range(X):
        PS[i] = dot(a2, gpT[i * C + co], 1, 0).astype(BF).reshape(ZL, rb, qw)
    send(PS, PR, "p", 0, sib)
    for i in range(X):
        PO[i] = dot(a2, gpT[i * C + c], 1, 0).reshape(ZL, rb, qw)
    got(PR, "p", 0)
    DXs, DXr = B["DXs"], B["DXr"]
    for d in range(1, X):
        x_ = up(x, d, X)
        DXs[d - 1] = (PO[x_] + PR[x_].astype(F32)).astype(BF)
    send_all([(DXs.at[n], DXr.at[n], dev(x_=v)) for n, v in enumerate(xs)], DXr, "dx")
    ADs, ADr = B["ADs"], B["ADr"]
    pre = preT[y]
    ADs[:, 0] = (pre * jax.nn.sigmoid(pre)).T.astype(BF).reshape(ZL, rb, tb)
    if ZL > 1:
        got(GA.at[pl.ds(0, ZL - 1)], "ga", 0)

    def backward(half, m):
        outs = [None] * bpd
        for j in range(PER):
            k = (half * Q + m) * PER + j
            back = dot(GA[itab[2, k]], tv[itab[0, k]], 1, 0)
            for b in range(bpd):
                term = ftab[bpd + b, k] * back
                outs[b] = term if j == 0 else outs[b] + term
        return outs

    def contribute(half, core, into):
        step = 2 if X % 2 == 0 else 1

        def some(i, carry):
            for n in range(step):
                for b, out in enumerate(backward(half, (i * step + n) * C + core)):
                    into[i * step + n, b] = out.astype(into.dtype)
            return carry
        lax.fori_loop(0, X // step, some, 0)

    Dsib, Drec, Dkeep = (B["Dsib0"], B["Dsib1"]), (B["Drec0"], B["Drec1"]), (B["Dkeep0"], B["Dkeep1"])
    EXs, EXr = (B["EXs0"], B["EXs1"]), (B["EXr0"], B["EXr1"])

    parts = 2 if bpd % 2 == 0 else 1

    def cut(i):
        return pl.ds(i * (bpd // parts), bpd // parts)

    whole = pl.ds(0, bpd)

    def to_x(n, at=whole, i=0):
        for d, v in enumerate(xs):
            EXs[n][d, at] = (Dkeep[n][v, at] + Drec[n][v, at].astype(F32)).astype(BF)
            copy(EXs[n].at[d, at], EXr[n].at[d, at], "e%d" % n, i, dev(x_=v)).start()
        sent.append(copy(EXr[n].at[:, at], EXr[n].at[:, at], "e%d" % n, i, sib))

    def from_x(n, at=whole, i=0):
        got(EXr[n].at[:, at], "e%d" % n, i)
        total = Dkeep[n][x, at] + Drec[n][x, at].astype(F32)
        for d in range(X - 1):
            total = total + EXr[n][d, at].astype(F32)
        return total

    contribute(zo, co, Dsib[0])
    send(Dsib[0], Drec[0], "d0", 0, sib)
    contribute(zo, c, Dkeep[0])

    got(Drec[0], "d0", 0)
    for i in range(parts):
        to_x(0, cut(i), i)
    S32 = B["S32"]
    got(DXr, "dx", 0)
    total = PO[x] + PR[x].astype(F32)
    for d in range(X - 1):
        total = total + DXr[d].astype(F32)
    S32[...] = total
    ADs[:, 1] = total.astype(BF)
    ADr[zl] = ADs[zl]
    send_all([(ADs.at[z], ADr.at[zl], dev(zl_=z)) for z in zs], ADr.at[pl.ds(0, ZL - 1)], "ad")
    contribute(zh, co, Dsib[1])
    send(Dsib[1], Drec[1], "d1", 0, sib)
    contribute(zh, c, Dkeep[1])
    for b in range(bpd):
        Dkeep[1][x, b] = ftab[2 * bpd, b] * dot(GA[b], tv[b], 1, 0)
    total = S32[zl]
    if ZL > 1:
        got(ADr.at[pl.ds(0, ZL - 1)], "ad", 0)
    for d in range(1, ZL):
        total = total + ADr[down(zl, d, ZL), 1].astype(F32)
    Ts, Tr, OutW = B["Ts"], B["Tr"], B["OutW"]
    Ts[...] = total
    send(Ts, Tr, "dt", 0, anti)
    FZs, FZr = B["FZs"], B["FZr"]
    for i in range(parts):
        at = cut(i)
        FZs[at] = from_x(0, at, i).astype(BF)
        send(FZs.at[at], FZr.at[at], "gz", i, anti)
    got(Drec[1], "d1", 0)
    to_x(1)
    for b in range(bpd):
        act_o[:, b * tb:(b + 1) * tb] = ADr[b, 0]
    got(Tr, "dt", 0)
    OutW[me] = Ts[...] + Tr[...]
    others = [(d, e) for d in range(X) for e in range(C) if d or e]
    tos = [dev(x_=up(x, d, X), c_=(co if e else c)) for d, e in others]
    send_all([(OutW.at[me], OutW.at[me], to) for to in tos], OutW.at[pl.ds(0, Q - 1)], "ow")
    own = from_x(1)
    got(OutW.at[pl.ds(0, Q - 1)], "ow", 0)
    for q in range(Q):
        gw_o[:, q * qw:(q + 1) * qw] = OutW[q]
    for cp in sent:
        cp.wait_send()
    for i in range(parts):
        got(FZr.at[cut(i)], "gz", i)
    own = (own + FZr[...].astype(F32)).astype(BF)
    for b in range(bpd):
        gf_o[:, b * tb:(b + 1) * tb] = own[b]


def on_device(cfg, features_t, tile_dst, tile_src, tile_edges, tile_values, weight, cotangent):
    rb = features_t.shape[0]
    nt, tb = tile_values.shape[:2]
    bufs, sems, smem = shapes(cfg, rb, tb, nt)
    vm, hbm = pl.BlockSpec(memory_space=pltpu.VMEM), pl.BlockSpec(memory_space=pltpu.HBM)
    kernel = functools.partial(body, cfg, tuple(bufs), tuple(sems))
    outs = (
        pltpu.VMEM(features_t.shape, BF),
        pltpu.VMEM(weight.shape, F32),
        pltpu.VMEM(features_t.shape, BF),
    )
    return pl.pallas_call(
        kernel,
        out_shape=outs,
        in_specs=[hbm] * 7,
        out_specs=(vm, vm, vm),
        scratch_shapes=[pltpu.VMEM(s, t) for s, t in bufs.values()]
        + [pltpu.SemaphoreType.DMA((n,)) for n in sems.values()] * 2
        + [pltpu.SemaphoreType.DMA((9,))]
        + [pltpu.SMEM(s, t) for s, t in smem.values()],
        compiler_params=pltpu.CompilerParams(
            collective_id=0, has_side_effects=True, vmem_limit_bytes=62 * 1024 * 1024
        ),
        name="graph_conv",
    )(features_t, tile_values, weight, cotangent, *(v.reshape(1, nt) for v in (tile_dst, tile_src, tile_edges)))


def solution(mesh, cfg=None):
    in_specs = (
        P("rep", "blk"),
        P("blk"),
        P("blk"),
        P("blk"),
        P("blk", None, None),
        P("rep", None),
        P("rep", "blk"),
    )
    out_specs = (P("rep", "blk"), P("rep", None), P("rep", "blk"))
    return jax.shard_map(
        functools.partial(on_device, cfg or FULL), mesh=mesh, in_specs=in_specs, out_specs=out_specs, check_vma=False
    )
```

```python
import functools

import jax
import jax.numpy as jnp
from jax import lax
from jax.experimental import pallas as pl
from jax.experimental.pallas import tpu as pltpu
from jax.sharding import PartitionSpec as P

FULL = dict(ZH=2, X=4, C=2, Y=4, ZL=8)
PER = 4
MESH = pl.DeviceIdType.MESH
BF = jnp.bfloat16
F32 = jnp.float32


def dot(a, b, ca, cb):
    return lax.dot_general(a, b, (((ca,), (cb,)), ((), ())), preferred_element_type=F32)


def groups(n):
    return 2 if n % 2 == 0 else 1


def shapes(cfg, rb, tb, nt):
    X, C, Y, ZL = cfg["X"], cfg["C"], cfg["Y"], cfg["ZL"]
    Q = X * C
    F = rb * Y * ZL
    qw = F // Q
    bpd = ZL
    x1, y1 = max(X - 1, 1), max(Y - 1, 1)
    nk = -(-cfg["ZH"] * Q * PER // 128) * 128
    bufs = dict(
        fv=((rb, bpd * tb), BF),
        wv=((rb, F), BF),
        cv=((rb, bpd * tb), BF),
        dv=((1, nt), jnp.int32),
        sv=((1, nt), jnp.int32),
        ev=((1, nt), jnp.int32),
        itv=((8, nk), jnp.int32),
        ftv=((2 * bpd + 8, nk), F32),
        gown=((X, C, bpd, rb, tb), BF),
        goth=((X, C, bpd, rb, tb), BF),
        tv=((nt, tb, tb), BF),
        cb=((bpd, rb, tb), BF),
        ct=((ZL, rb, tb), BF),
        wb=((Q, rb, qw), BF),
        wg=((Y, C, X, ZL, rb, qw), BF),
        aggb=((bpd, rb, tb), BF),
        A=((ZL, rb, tb), BF),
        ctT=((Y, tb, rb * ZL), BF),
        AT=((Y, groups(ZL), tb, rb * ZL // groups(ZL)), BF),
        preT=((X, tb, C * qw), F32),
        gpT=((Q, tb, qw), BF),
        ADs=((ZL, 2, rb, tb), BF),
        ADr=((ZL, 2, rb, tb), BF),
        gab=((ZL, rb, tb), BF),
        GA=((bpd, rb, tb), BF),
        PS=((X, ZL, rb, qw), BF),
        PO=((X, ZL, rb, qw), F32),
        PR=((X, ZL, rb, qw), BF),
        DXs=((x1, ZL, rb, qw), BF),
        DXr=((x1, ZL, rb, qw), BF),
        S32=((ZL, rb, qw), F32),
        Ts=((rb, qw), F32),
        Tr=((rb, qw), F32),
        OutW=((Q, rb, qw), F32),
        Dsib0=((X, bpd, rb, tb), BF),
        Dsib1=((X, bpd, rb, tb), BF),
        Drec0=((X, bpd, rb, tb), BF),
        Drec1=((X, bpd, rb, tb), BF),
        Dkeep0=((X, bpd, rb, tb), F32),
        Dkeep1=((X, bpd, rb, tb), F32),
        EXs0=((x1, bpd, rb, tb), BF),
        EXs1=((x1, bpd, rb, tb), BF),
        EXr0=((x1, bpd, rb, tb), BF),
        EXr1=((x1, bpd, rb, tb), BF),
        FZs=((bpd, rb, tb), BF),
        FZr=((bpd, rb, tb), BF),
    )
    sems = dict(
        fz=2, fx0=1, fx1=2 * x1, fc0=1, fc1=2, w1=1, ct=1, w2=1, w3=Y, w4=2, w5=2, cty=1, ag=2, agy=2 * y1, ga=1,
        p=1, dx=1, ad=1, dt=1, ow=1, d0=1, d1=1, e0=2, e1=1, gz=2,
    )
    smem = dict(itab=((8, nk), jnp.int32), ftab=((2 * bpd + 8, nk), F32))
    return bufs, sems, smem


def tables(bpd, dst, src, edges, itv, ftv):
    nt = dst.shape[1]
    nk = itv.shape[1]
    r0 = lax.broadcasted_iota(jnp.int32, (nt, nt), 0)
    r1 = lax.broadcasted_iota(jnp.int32, (nt, nt), 1)
    k1 = lax.broadcasted_iota(jnp.int32, (nt, nk), 1)
    t0 = lax.broadcasted_iota(jnp.int32, (nt, nk), 0)
    lane = lax.broadcasted_iota(jnp.int32, (1, nt), 1)

    def column(row):
        return jnp.sum(jnp.where(r0 == r1, row, jnp.zeros_like(row)), axis=1, keepdims=True)

    bits = bpd.bit_length() - 1
    group = jnp.where((edges > 0) & (lane >= bpd), lax.shift_right_logical(src, bits), -1)
    group_c = column(group)
    rank = jnp.sum(jnp.where((group_c == group) & (r1 < r0), 1, 0), axis=1, keepdims=True)
    pick = jnp.where(group_c >= 0, group_c * PER + rank, -1) == k1

    def by_k(col):
        return jnp.sum(jnp.where(pick, col, jnp.zeros_like(col)), axis=0, keepdims=True)

    at_src, at_dst = by_k(column(src & (bpd - 1))), by_k(column(dst))
    itv[0:1] = by_k(t0)
    itv[1:2] = at_src
    itv[2:3] = at_dst
    blocks = lax.broadcasted_iota(jnp.int32, (bpd, nt), 0)
    weights = jnp.where(dst == blocks, edges.astype(F32), 0.0)
    coef = jnp.sum(weights / jnp.sum(weights, axis=1, keepdims=True), axis=0, keepdims=True)
    coef_k = by_k(column(coef))
    blocks = lax.broadcasted_iota(jnp.int32, (bpd, nk), 0)
    ftv[0:bpd] = jnp.where(at_dst == blocks, coef_k, 0.0)
    ftv[bpd:2 * bpd] = jnp.where(at_src == blocks, coef_k, 0.0)
    ftv[2 * bpd:2 * bpd + 1, 0:nt] = coef


def body(cfg, buf_names, sem_names, feat_hbm, tv_hbm, w_hbm, cot_hbm, dst_hbm, src_hbm, edge_hbm, act_o, gw_o, gf_o, *scr):
    ZH, X, C, Y, ZL = cfg["ZH"], cfg["X"], cfg["C"], cfg["Y"], cfg["ZL"]
    nb, ns = len(buf_names), len(sem_names)
    B = dict(zip(buf_names, scr[:nb]))
    SS = dict(zip(sem_names, scr[nb:nb + ns]))
    RS = dict(zip(sem_names, scr[nb + ns:nb + 2 * ns]))
    load_sem, itab, ftab = scr[nb + 2 * ns:]
    feat, w, cot = B["fv"], B["wv"], B["cv"]
    Q = X * C
    bpd = ZL
    rb, tb = B["A"].shape[1:]
    qw = B["wb"].shape[2]
    rows = ZL * rb

    blk, rep = lax.axis_index("blk"), lax.axis_index("rep")
    zh = lax.div(blk, Q)
    me = lax.rem(blk, Q)
    x, c = lax.div(me, C), lax.rem(me, C)
    y, zl = lax.div(rep, ZL), lax.rem(rep, ZL)
    zo, co = 1 - zh, 1 - c

    def dev(zh_=zh, x_=x, c_=c, y_=y, zl_=zl):
        return ((zh_ * X + x_) * C + c_, y_ * ZL + zl_)

    def up(v, d, n):
        return lax.rem(v + d, n)

    def down(v, d, n):
        return lax.rem(v + n - d, n)

    anti, sib = dev(zh_=zo), dev(c_=co)
    sent = []

    def copy(src, dst, name, i, to):
        return pltpu.make_async_remote_copy(
            src_ref=src, dst_ref=dst, send_sem=SS[name].at[i], recv_sem=RS[name].at[i],
            device_id=to, device_id_type=MESH,
        )

    def send(src, dst, name, i, to):
        cp = copy(src, dst, name, i, to)
        cp.start()
        sent.append(cp)

    def send_all(copies, size_ref, name, i=0):
        for src, dst, to in copies:
            copy(src, dst, name, i, to).start()
        if copies:
            sent.append(copy(size_ref, size_ref, name, i, sib))

    def got(dst, name, i):
        copy(dst, dst, name, i, sib).wait_recv()

    loads = [
        pltpu.make_async_copy(a, b, load_sem.at[i])
        for i, (a, b) in enumerate((
            (feat_hbm, feat), (w_hbm, w), (cot_hbm, cot), (tv_hbm, B["tv"]),
            (dst_hbm, B["dv"]), (src_hbm, B["sv"]), (edge_hbm, B["ev"]),
        ))
    ]
    for ld in loads:
        ld.start()

    barrier = pltpu.get_barrier_semaphore()
    partners = [anti]
    partners += [dev(x_=up(x, d, X), c_=(c if e == 0 else co)) for d in range(X) for e in range(C) if d or e]
    partners += [dev(zl_=up(zl, d, ZL)) for d in range(1, ZL)]
    partners += [dev(y_=up(y, d, Y)) for d in range(1, Y)]
    for p in partners:
        pl.semaphore_signal(barrier, inc=1, device_id=p, device_id_type=MESH)

    gown, goth, tv = B["gown"], B["goth"], B["tv"]
    loads[0].wait()
    for b in range(bpd):
        gown[x, c, b] = feat[:, b * tb:(b + 1) * tb]
    loads[1].wait()
    wg, wb = B["wg"], B["wb"]
    for q in range(Q):
        wb[q] = w[:, q * qw:(q + 1) * qw]
    wg[y, c, x, zl] = wb[me]
    pl.semaphore_wait(barrier, len(partners))

    xs = [up(x, d, X) for d in range(1, X)]
    zs = [up(zl, d, ZL) for d in range(1, ZL)]
    parts = groups(bpd)

    def cut(i):
        return pl.ds(i * (bpd // parts), bpd // parts)

    send(gown.at[x, c, cut(0)], goth.at[x, c, cut(0)], "fz", 0, anti)
    send_all([(gown.at[x, c], gown.at[x, c], dev(x_=v)) for v in xs], gown.at[pl.ds(0, X - 1), 0], "fx0")
    send_all([(wb.at[me], wg.at[y, c, x, zl], dev(zl_=z)) for z in zs], wg.at[y, c, x, pl.ds(0, ZL - 1)], "w1")
    for i in range(1, parts):
        send(gown.at[x, c, cut(i)], goth.at[x, c, cut(i)], "fz", i, anti)
    for ld in loads[4:]:
        ld.wait()
    tables(bpd, B["dv"][...], B["sv"][...], B["ev"][...], B["itv"], B["ftv"])
    to_smem = [
        pltpu.make_async_copy(B["itv"], itab, load_sem.at[7]),
        pltpu.make_async_copy(B["ftv"], ftab, load_sem.at[8]),
    ]
    for cp in to_smem:
        cp.start()
    loads[2].wait()
    cb, ct = B["cb"], B["ct"]
    for b in range(bpd):
        cb[b] = cot[:, b * tb:(b + 1) * tb]
    ct[zl] = cb[zl]
    got(gown.at[pl.ds(0, X - 1), 0], "fx0", 0)
    send(gown.at[:, c], gown.at[:, c], "fc0", 0, sib)
    loads[3].wait()
    for cp in to_smem:
        cp.wait()
    acc = tuple(ftab[2 * bpd, b] * dot(gown[x, c, b], tv[b], 1, 1) for b in range(bpd))

    def forward(g, half, i, acc):
        acc = list(acc)
        for j in range(C * PER):
            k = (half * Q + i * C) * PER + j
            out = dot(g[i, j // PER, itab[1, k]], tv[itab[0, k]], 1, 1)
            for b in range(bpd):
                acc[b] = acc[b] + ftab[b, k] * out
        return tuple(acc)

    part = wg.at[y, c, x]
    if ZL > 1:
        got(wg.at[y, c, x, pl.ds(0, ZL - 1)], "w1", 0)
    send_all([(part, part, dev(x_=v)) for v in xs], wg.at[y, c, pl.ds(0, X - 1)], "w2")
    for i in range(parts):
        part = goth.at[x, c, cut(i)]
        got(part, "fz", i)
        for d in range(1, X):
            send(part, part, "fx1", i * (X - 1) + d - 1, dev(x_=up(x, d, X)))
        copy(part, part, "fc1", i, sib).start()
    send_all([(cb.at[z], ct.at[zl], dev(zl_=z)) for z in zs], ct.at[pl.ds(0, ZL - 1)], "ct")
    got(wg.at[y, c, pl.ds(0, X - 1)], "w2", 0)
    y_up, y_down, y_far = up(y, 1, Y), down(y, 1, Y), up(y, 2, Y)
    send(wg.at[y, c], wg.at[y, c], "w4", 0, dev(y_=y_up))
    if Y > 2:
        send(wg.at[y, c], wg.at[y, c], "w4", 1, dev(y_=y_down))
    send(wg.at[y, c], wg.at[y, c], "w3", 0, sib)
    got(gown.at[:, co], "fc0", 0)
    acc = lax.fori_loop(0, Q // C, lambda i, a: forward(gown, zh, i, a), acc)
    for i in range(parts):
        for d in range(1, X):
            part = goth.at[down(x, d, X), c, cut(i)]
            got(part, "fx1", i * (X - 1) + d - 1)
            copy(part, part, "fc1", i, sib).start()
        sent.append(copy(goth.at[:, c, cut(i)], goth.at[:, c, cut(i)], "fc1", i, sib))
    if ZL > 1:
        got(ct.at[pl.ds(0, ZL - 1)], "ct", 0)
    ctT, AT = B["ctT"], B["AT"]
    ctT[y] = ct[...].reshape(rows, tb).astype(F32).T.astype(BF)
    ys = [up(y, d, Y) for d in range(1, Y)]
    send_all([(ctT.at[y], ctT.at[y], dev(y_=v)) for v in ys], ctT.at[pl.ds(0, Y - 1)], "cty")
    for i in range(parts):
        got(goth.at[:, co, cut(i)], "fc1", i)
    acc = lax.fori_loop(0, Q // C, lambda i, a: forward(goth, zo, i, a), acc)

    A = B["A"]
    for b in range(bpd):
        B["aggb"][b] = acc[b].astype(BF)
    A[zl] = B["aggb"][zl]
    ng = groups(ZL)
    hz = ZL // ng
    near = lax.div(zl, hz)
    for z in zs:
        copy(B["aggb"].at[z], A.at[zl], "ag", (lax.div(z, hz) + near) % ng, dev(zl_=z)).start()
    ag_sizes = [A.at[pl.ds(0, hz - 1 if n == 0 else hz)] for n in range(ng)]
    ag_groups = [(n, r) for n, r in enumerate(ag_sizes) if n > 0 or hz > 1]
    for n, r in ag_groups:
        sent.append(copy(r, r, "ag", n, sib))
    half = X // 2
    got(wg.at[y_down, c], "w4", 0)
    send(wg.at[y_down, c], wg.at[y_down, c], "w3", 1, sib)
    if Y > 2:
        part = wg.at[y_down, c, pl.ds(0, half)]
        send(part, part, "w5", 0, dev(y_=y_up))
        got(wg.at[y_up, c], "w4", 1)
        part = wg.at[y_up, c, pl.ds(half, half)]
        send(part, part, "w5", 1, dev(y_=y_down))
        send(wg.at[y_up, c], wg.at[y_up, c], "w3", 2, sib)

    for n in range(ng):
        if n > 0 or hz > 1:
            got(ag_sizes[n], "ag", n)
        g = near if n == 0 else 1 - near
        AT[y, g] = A[pl.ds(g * hz, hz)].reshape(rows // ng, tb).astype(F32).T.astype(BF)
        for d in range(1, Y):
            send(AT.at[y, g], AT.at[y, g], "agy", n * (Y - 1) + d - 1, dev(y_=up(y, d, Y)))
    a2 = A[...].reshape(rows, tb)

    def nodes_by_rows(y_):
        return jnp.concatenate([AT[y_, g] for g in range(ng)], axis=1)

    def weight_of(y_, i):
        return jnp.concatenate([wg[y_, e, i].reshape(rows, qw) for e in range(C)], axis=1)

    preT, gpT = B["preT"], B["gpT"]
    got(wg.at[y, co], "w3", 0)
    for i in range(X):
        preT[i] = dot(nodes_by_rows(y), weight_of(y, i), 1, 0)
    got(ctT.at[pl.ds(0, Y - 1)], "cty", 0)
    order = [(1, 1), (3, 2), (2, 3)] if Y > 2 else [(1, 1)]
    for n, (d, at) in enumerate(order):
        y_ = down(y, d, Y)
        if d == 2:
            got(wg.at[y_far, c, pl.ds(0, half)], "w5", 0)
            got(wg.at[y_far, c, pl.ds(half, half)], "w5", 1)
            send(wg.at[y_far, c], wg.at[y_far, c], "w3", 3, sib)
        for g in range(ng):
            got(AT.at[y_, near if g == 0 else 1 - near], "agy", g * (Y - 1) + d - 1)
        got(wg.at[y_, co], "w3", at)
        for i in range(X):
            pre = preT[i] + dot(nodes_by_rows(y_), weight_of(y_, i), 1, 0)
            preT[i] = pre
            if n == len(order) - 1:
                sig = jax.nn.sigmoid(pre)
                gp = (ctT[i].astype(F32) * sig * (1.0 + pre * (1.0 - sig))).astype(BF)
                for e in range(C):
                    gpT[i * C + e] = gp[:, e * qw:(e + 1) * qw]

    def grad_pre(i):
        return jnp.concatenate([gpT[i * C + e] for e in range(C)], axis=1)

    ga = dot(weight_of(y, 0), grad_pre(0), 1, 1)
    for i in range(1, X):
        ga = ga + dot(weight_of(y, i), grad_pre(i), 1, 1)
    gab, GA = B["gab"], B["GA"]
    gab[...] = ga.astype(BF).reshape(ZL, rb, tb)
    GA[zl] = gab[zl]
    send_all([(gab.at[z], GA.at[zl], dev(zl_=z)) for z in zs], GA.at[pl.ds(0, ZL - 1)], "ga")

    PS, PO, PR = B["PS"], B["PO"], B["PR"]
    for i in range(X):
        PS[i] = dot(a2, gpT[i * C + co], 1, 0).astype(BF).reshape(ZL, rb, qw)
    send(PS, PR, "p", 0, sib)
    for i in range(X):
        PO[i] = dot(a2, gpT[i * C + c], 1, 0).reshape(ZL, rb, qw)
    got(PR, "p", 0)
    DXs, DXr = B["DXs"], B["DXr"]
    for d in range(1, X):
        x_ = up(x, d, X)
        DXs[d - 1] = (PO[x_] + PR[x_].astype(F32)).astype(BF)
    send_all([(DXs.at[n], DXr.at[n], dev(x_=v)) for n, v in enumerate(xs)], DXr, "dx")
    ADs, ADr = B["ADs"], B["ADr"]
    pre = preT[y]
    ADs[:, 0] = (pre * jax.nn.sigmoid(pre)).T.astype(BF).reshape(ZL, rb, tb)
    if ZL > 1:
        got(GA.at[pl.ds(0, ZL - 1)], "ga", 0)

    def backward(half, m):
        outs = [None] * bpd
        for j in range(PER):
            k = (half * Q + m) * PER + j
            back = dot(GA[itab[2, k]], tv[itab[0, k]], 1, 0)
            for b in range(bpd):
                term = ftab[bpd + b, k] * back
                outs[b] = term if j == 0 else outs[b] + term
        return outs

    def contribute(half, core, into):
        step = 2 if X % 2 == 0 else 1

        def some(i, carry):
            for n in range(step):
                for b, out in enumerate(backward(half, (i * step + n) * C + core)):
                    into[i * step + n, b] = out.astype(into.dtype)
            return carry
        lax.fori_loop(0, X // step, some, 0)

    Dsib, Drec, Dkeep = (B["Dsib0"], B["Dsib1"]), (B["Drec0"], B["Drec1"]), (B["Dkeep0"], B["Dkeep1"])
    EXs, EXr = (B["EXs0"], B["EXs1"]), (B["EXr0"], B["EXr1"])

    whole = pl.ds(0, bpd)

    def to_x(n, at=whole, i=0):
        for d, v in enumerate(xs):
            EXs[n][d, at] = (Dkeep[n][v, at] + Drec[n][v, at].astype(F32)).astype(BF)
            copy(EXs[n].at[d, at], EXr[n].at[d, at], "e%d" % n, i, dev(x_=v)).start()
        sent.append(copy(EXr[n].at[:, at], EXr[n].at[:, at], "e%d" % n, i, sib))

    def from_x(n, at=whole, i=0):
        got(EXr[n].at[:, at], "e%d" % n, i)
        total = Dkeep[n][x, at] + Drec[n][x, at].astype(F32)
        for d in range(X - 1):
            total = total + EXr[n][d, at].astype(F32)
        return total

    contribute(zo, co, Dsib[0])
    send(Dsib[0], Drec[0], "d0", 0, sib)
    contribute(zo, c, Dkeep[0])

    got(Drec[0], "d0", 0)
    for i in range(parts):
        to_x(0, cut(i), i)
    S32 = B["S32"]
    got(DXr, "dx", 0)
    total = PO[x] + PR[x].astype(F32)
    for d in range(X - 1):
        total = total + DXr[d].astype(F32)
    S32[...] = total
    ADs[:, 1] = total.astype(BF)
    ADr[zl] = ADs[zl]
    send_all([(ADs.at[z], ADr.at[zl], dev(zl_=z)) for z in zs], ADr.at[pl.ds(0, ZL - 1)], "ad")
    contribute(zh, co, Dsib[1])
    send(Dsib[1], Drec[1], "d1", 0, sib)
    contribute(zh, c, Dkeep[1])
    for b in range(bpd):
        Dkeep[1][x, b] = ftab[2 * bpd, b] * dot(GA[b], tv[b], 1, 0)
    total = S32[zl]
    if ZL > 1:
        got(ADr.at[pl.ds(0, ZL - 1)], "ad", 0)
    for d in range(1, ZL):
        total = total + ADr[down(zl, d, ZL), 1].astype(F32)
    Ts, Tr, OutW = B["Ts"], B["Tr"], B["OutW"]
    Ts[...] = total
    send(Ts, Tr, "dt", 0, anti)
    FZs, FZr = B["FZs"], B["FZr"]
    for i in range(parts):
        at = cut(i)
        FZs[at] = from_x(0, at, i).astype(BF)
        send(FZs.at[at], FZr.at[at], "gz", i, anti)
    got(Drec[1], "d1", 0)
    to_x(1)
    for b in range(bpd):
        act_o[:, b * tb:(b + 1) * tb] = ADr[b, 0]
    got(Tr, "dt", 0)
    OutW[me] = Ts[...] + Tr[...]
    others = [(d, e) for d in range(X) for e in range(C) if d or e]
    tos = [dev(x_=up(x, d, X), c_=(co if e else c)) for d, e in others]
    send_all([(OutW.at[me], OutW.at[me], to) for to in tos], OutW.at[pl.ds(0, Q - 1)], "ow")
    own = from_x(1)
    got(OutW.at[pl.ds(0, Q - 1)], "ow", 0)
    for q in range(Q):
        gw_o[:, q * qw:(q + 1) * qw] = OutW[q]
    for cp in sent:
        cp.wait_send()
    for i in range(parts):
        got(FZr.at[cut(i)], "gz", i)
    own = (own + FZr[...].astype(F32)).astype(BF)
    for b in range(bpd):
        gf_o[:, b * tb:(b + 1) * tb] = own[b]


def on_device(cfg, features_t, tile_dst, tile_src, tile_edges, tile_values, weight, cotangent):
    rb = features_t.shape[0]
    nt, tb = tile_values.shape[:2]
    bufs, sems, smem = shapes(cfg, rb, tb, nt)
    vm, hbm = pl.BlockSpec(memory_space=pltpu.VMEM), pl.BlockSpec(memory_space=pltpu.HBM)
    kernel = functools.partial(body, cfg, tuple(bufs), tuple(sems))
    outs = (
        pltpu.VMEM(features_t.shape, BF),
        pltpu.VMEM(weight.shape, F32),
        pltpu.VMEM(features_t.shape, BF),
    )
    return pl.pallas_call(
        kernel,
        out_shape=outs,
        in_specs=[hbm] * 7,
        out_specs=(vm, vm, vm),
        scratch_shapes=[pltpu.VMEM(s, t) for s, t in bufs.values()]
        + [pltpu.SemaphoreType.DMA((n,)) for n in sems.values()] * 2
        + [pltpu.SemaphoreType.DMA((9,))]
        + [pltpu.SMEM(s, t) for s, t in smem.values()],
        compiler_params=pltpu.CompilerParams(
            collective_id=0, has_side_effects=True, vmem_limit_bytes=62 * 1024 * 1024
        ),
        name="graph_conv",
    )(features_t, tile_values, weight, cotangent, *(v.reshape(1, nt) for v in (tile_dst, tile_src, tile_edges)))


def solution(mesh, cfg=None):
    in_specs = (
        P("rep", "blk"),
        P("blk"),
        P("blk"),
        P("blk"),
        P("blk", None, None),
        P("rep", None),
        P("rep", "blk"),
    )
    out_specs = (P("rep", "blk"), P("rep", None), P("rep", "blk"))
    return jax.shard_map(
        functools.partial(on_device, cfg or FULL), mesh=mesh, in_specs=in_specs, out_specs=out_specs, check_vma=False
    )
```

```python
import functools

import jax
import jax.numpy as jnp
from jax import lax
from jax.experimental import pallas as pl
from jax.experimental.pallas import tpu as pltpu
from jax.sharding import PartitionSpec as P

FULL = dict(ZH=2, X=4, C=2, Y=4, ZL=8)
PER = 4
MESH = pl.DeviceIdType.MESH
BF = jnp.bfloat16
F32 = jnp.float32


def dot(a, b, ca, cb):
    return lax.dot_general(a, b, (((ca,), (cb,)), ((), ())), preferred_element_type=F32)


def shapes(cfg, rb, tb, nt):
    X, C, Y, ZL = cfg["X"], cfg["C"], cfg["Y"], cfg["ZL"]
    Q = X * C
    F = rb * Y * ZL
    qw = F // Q
    bpd = ZL
    x1, y1 = max(X - 1, 1), max(Y - 1, 1)
    nk = -(-cfg["ZH"] * Q * PER // 128) * 128
    bufs = dict(
        fv=((rb, bpd * tb), BF),
        wv=((rb, F), BF),
        cv=((rb, bpd * tb), BF),
        dv=((1, nt), jnp.int32),
        sv=((1, nt), jnp.int32),
        ev=((1, nt), jnp.int32),
        itv=((8, nk), jnp.int32),
        ftv=((2 * bpd + 8, nk), F32),
        gown=((X, C, bpd, rb, tb), BF),
        goth=((X, C, bpd, rb, tb), BF),
        tv=((nt, tb, tb), BF),
        cb=((bpd, rb, tb), BF),
        ct=((ZL, rb, tb), BF),
        wb=((Q, rb, qw), BF),
        wg=((Y, C, X, ZL, rb, qw), BF),
        aggb=((bpd, rb, tb), BF),
        A=((ZL, rb, tb), BF),
        ctT=((Y, tb, rb * ZL), BF),
        AT=((Y, tb, rb * ZL), BF),
        preT=((X, tb, C * qw), F32),
        gpT=((Q, tb, qw), BF),
        ADs=((ZL, 2, rb, tb), BF),
        ADr=((ZL, 2, rb, tb), BF),
        gab=((ZL, rb, tb), BF),
        GA=((bpd, rb, tb), BF),
        PS=((X, ZL, rb, qw), BF),
        PO=((X, ZL, rb, qw), F32),
        PR=((X, ZL, rb, qw), BF),
        DXs=((x1, ZL, rb, qw), BF),
        DXr=((x1, ZL, rb, qw), BF),
        S32=((ZL, rb, qw), F32),
        Ts=((rb, qw), F32),
        Tr=((rb, qw), F32),
        OutW=((Q, rb, qw), F32),
        Dsib0=((X, bpd, rb, tb), BF),
        Dsib1=((X, bpd, rb, tb), BF),
        Drec0=((X, bpd, rb, tb), BF),
        Drec1=((X, bpd, rb, tb), BF),
        Dkeep0=((X, bpd, rb, tb), F32),
        Dkeep1=((X, bpd, rb, tb), F32),
        EXs0=((x1, bpd, rb, tb), BF),
        EXs1=((x1, bpd, rb, tb), BF),
        EXr0=((x1, bpd, rb, tb), BF),
        EXr1=((x1, bpd, rb, tb), BF),
        FZs=((bpd, rb, tb), BF),
        FZr=((bpd, rb, tb), BF),
    )
    sems = dict(
        fz=1, fx0=1, fx1=x1, fc0=1, fc1=1, w1=1, ct=1, w2=1, w3=Y, w4=2, w5=2, cty=1, ag=1, agy=y1, ga=1,
        p=1, dx=1, ad=1, dt=1, ow=1, d0=1, d1=1, e0=2, e1=1, gz=2,
    )
    smem = dict(itab=((8, nk), jnp.int32), ftab=((2 * bpd + 8, nk), F32))
    return bufs, sems, smem


def tables(bpd, dst, src, edges, itv, ftv):
    nt = dst.shape[1]
    nk = itv.shape[1]
    r0 = lax.broadcasted_iota(jnp.int32, (nt, nt), 0)
    r1 = lax.broadcasted_iota(jnp.int32, (nt, nt), 1)
    k1 = lax.broadcasted_iota(jnp.int32, (nt, nk), 1)
    t0 = lax.broadcasted_iota(jnp.int32, (nt, nk), 0)
    lane = lax.broadcasted_iota(jnp.int32, (1, nt), 1)

    def column(row):
        return jnp.sum(jnp.where(r0 == r1, row, jnp.zeros_like(row)), axis=1, keepdims=True)

    bits = bpd.bit_length() - 1
    group = jnp.where((edges > 0) & (lane >= bpd), lax.shift_right_logical(src, bits), -1)
    group_c = column(group)
    rank = jnp.sum(jnp.where((group_c == group) & (r1 < r0), 1, 0), axis=1, keepdims=True)
    pick = jnp.where(group_c >= 0, group_c * PER + rank, -1) == k1

    def by_k(col):
        return jnp.sum(jnp.where(pick, col, jnp.zeros_like(col)), axis=0, keepdims=True)

    at_src, at_dst = by_k(column(src & (bpd - 1))), by_k(column(dst))
    itv[0:1] = by_k(t0)
    itv[1:2] = at_src
    itv[2:3] = at_dst
    blocks = lax.broadcasted_iota(jnp.int32, (bpd, nt), 0)
    weights = jnp.where(dst == blocks, edges.astype(F32), 0.0)
    coef = jnp.sum(weights / jnp.sum(weights, axis=1, keepdims=True), axis=0, keepdims=True)
    coef_k = by_k(column(coef))
    blocks = lax.broadcasted_iota(jnp.int32, (bpd, nk), 0)
    ftv[0:bpd] = jnp.where(at_dst == blocks, coef_k, 0.0)
    ftv[bpd:2 * bpd] = jnp.where(at_src == blocks, coef_k, 0.0)
    ftv[2 * bpd:2 * bpd + 1, 0:nt] = coef


def body(cfg, buf_names, sem_names, feat_hbm, tv_hbm, w_hbm, cot_hbm, dst_hbm, src_hbm, edge_hbm, act_o, gw_o, gf_o, *scr):
    ZH, X, C, Y, ZL = cfg["ZH"], cfg["X"], cfg["C"], cfg["Y"], cfg["ZL"]
    nb, ns = len(buf_names), len(sem_names)
    B = dict(zip(buf_names, scr[:nb]))
    SS = dict(zip(sem_names, scr[nb:nb + ns]))
    RS = dict(zip(sem_names, scr[nb + ns:nb + 2 * ns]))
    load_sem, itab, ftab = scr[nb + 2 * ns:]
    feat, w, cot = B["fv"], B["wv"], B["cv"]
    Q = X * C
    bpd = ZL
    rb, tb = B["A"].shape[1:]
    qw = B["wb"].shape[2]
    rows = ZL * rb

    blk, rep = lax.axis_index("blk"), lax.axis_index("rep")
    zh = lax.div(blk, Q)
    me = lax.rem(blk, Q)
    x, c = lax.div(me, C), lax.rem(me, C)
    y, zl = lax.div(rep, ZL), lax.rem(rep, ZL)
    zo, co = 1 - zh, 1 - c

    def dev(zh_=zh, x_=x, c_=c, y_=y, zl_=zl):
        return ((zh_ * X + x_) * C + c_, y_ * ZL + zl_)

    def up(v, d, n):
        return lax.rem(v + d, n)

    def down(v, d, n):
        return lax.rem(v + n - d, n)

    anti, sib = dev(zh_=zo), dev(c_=co)
    sent = []

    def copy(src, dst, name, i, to):
        return pltpu.make_async_remote_copy(
            src_ref=src, dst_ref=dst, send_sem=SS[name].at[i], recv_sem=RS[name].at[i],
            device_id=to, device_id_type=MESH,
        )

    def send(src, dst, name, i, to):
        cp = copy(src, dst, name, i, to)
        cp.start()
        sent.append(cp)

    def send_all(copies, size_ref, name, i=0):
        for src, dst, to in copies:
            copy(src, dst, name, i, to).start()
        if copies:
            sent.append(copy(size_ref, size_ref, name, i, sib))

    def got(dst, name, i):
        copy(dst, dst, name, i, sib).wait_recv()

    loads = [
        pltpu.make_async_copy(a, b, load_sem.at[i])
        for i, (a, b) in enumerate((
            (feat_hbm, feat), (w_hbm, w), (cot_hbm, cot), (tv_hbm, B["tv"]),
            (dst_hbm, B["dv"]), (src_hbm, B["sv"]), (edge_hbm, B["ev"]),
        ))
    ]
    for ld in loads:
        ld.start()

    barrier = pltpu.get_barrier_semaphore()
    partners = [anti]
    partners += [dev(x_=up(x, d, X), c_=(c if e == 0 else co)) for d in range(X) for e in range(C) if d or e]
    partners += [dev(zl_=up(zl, d, ZL)) for d in range(1, ZL)]
    partners += [dev(y_=up(y, d, Y)) for d in range(1, Y)]
    for p in partners:
        pl.semaphore_signal(barrier, inc=1, device_id=p, device_id_type=MESH)

    gown, goth, tv = B["gown"], B["goth"], B["tv"]
    loads[0].wait()
    for b in range(bpd):
        gown[x, c, b] = feat[:, b * tb:(b + 1) * tb]
    loads[1].wait()
    wg, wb = B["wg"], B["wb"]
    for q in range(Q):
        wb[q] = w[:, q * qw:(q + 1) * qw]
    wg[y, c, x, zl] = wb[me]
    pl.semaphore_wait(barrier, len(partners))

    xs = [up(x, d, X) for d in range(1, X)]
    zs = [up(zl, d, ZL) for d in range(1, ZL)]
    send(gown.at[x, c], goth.at[x, c], "fz", 0, anti)
    send_all([(gown.at[x, c], gown.at[x, c], dev(x_=v)) for v in xs], gown.at[pl.ds(0, X - 1), 0], "fx0")
    send_all([(wb.at[me], wg.at[y, c, x, zl], dev(zl_=z)) for z in zs], wg.at[y, c, x, pl.ds(0, ZL - 1)], "w1")
    for ld in loads[4:]:
        ld.wait()
    tables(bpd, B["dv"][...], B["sv"][...], B["ev"][...], B["itv"], B["ftv"])
    to_smem = [
        pltpu.make_async_copy(B["itv"], itab, load_sem.at[7]),
        pltpu.make_async_copy(B["ftv"], ftab, load_sem.at[8]),
    ]
    for cp in to_smem:
        cp.start()
    loads[2].wait()
    cb, ct = B["cb"], B["ct"]
    for b in range(bpd):
        cb[b] = cot[:, b * tb:(b + 1) * tb]
    ct[zl] = cb[zl]
    got(gown.at[pl.ds(0, X - 1), 0], "fx0", 0)
    send(gown.at[:, c], gown.at[:, c], "fc0", 0, sib)
    loads[3].wait()
    for cp in to_smem:
        cp.wait()
    acc = tuple(ftab[2 * bpd, b] * dot(gown[x, c, b], tv[b], 1, 1) for b in range(bpd))

    def forward(g, half, i, acc):
        acc = list(acc)
        for j in range(C * PER):
            k = (half * Q + i * C) * PER + j
            out = dot(g[i, j // PER, itab[1, k]], tv[itab[0, k]], 1, 1)
            for b in range(bpd):
                acc[b] = acc[b] + ftab[b, k] * out
        return tuple(acc)

    part = wg.at[y, c, x]
    if ZL > 1:
        got(wg.at[y, c, x, pl.ds(0, ZL - 1)], "w1", 0)
    send_all([(part, part, dev(x_=v)) for v in xs], wg.at[y, c, pl.ds(0, X - 1)], "w2")
    got(goth.at[x, c], "fz", 0)
    for d in range(1, X):
        send(goth.at[x, c], goth.at[x, c], "fx1", d - 1, dev(x_=up(x, d, X)))
    copy(goth.at[x, c], goth.at[x, c], "fc1", 0, sib).start()
    send_all([(cb.at[z], ct.at[zl], dev(zl_=z)) for z in zs], ct.at[pl.ds(0, ZL - 1)], "ct")
    got(wg.at[y, c, pl.ds(0, X - 1)], "w2", 0)
    y_up, y_down, y_far = up(y, 1, Y), down(y, 1, Y), up(y, 2, Y)
    send(wg.at[y, c], wg.at[y, c], "w4", 0, dev(y_=y_up))
    if Y > 2:
        send(wg.at[y, c], wg.at[y, c], "w4", 1, dev(y_=y_down))
    send(wg.at[y, c], wg.at[y, c], "w3", 0, sib)
    got(gown.at[:, co], "fc0", 0)
    acc = lax.fori_loop(0, Q // C, lambda i, a: forward(gown, zh, i, a), acc)
    for d in range(1, X):
        part = goth.at[down(x, d, X), c]
        got(part, "fx1", d - 1)
        copy(part, part, "fc1", 0, sib).start()
    sent.append(copy(goth.at[:, c], goth.at[:, c], "fc1", 0, sib))
    if ZL > 1:
        got(ct.at[pl.ds(0, ZL - 1)], "ct", 0)
    ctT, AT = B["ctT"], B["AT"]
    ctT[y] = ct[...].reshape(rows, tb).astype(F32).T.astype(BF)
    ys = [up(y, d, Y) for d in range(1, Y)]
    send_all([(ctT.at[y], ctT.at[y], dev(y_=v)) for v in ys], ctT.at[pl.ds(0, Y - 1)], "cty")
    got(goth.at[:, co], "fc1", 0)
    acc = lax.fori_loop(0, Q // C, lambda i, a: forward(goth, zo, i, a), acc)

    A = B["A"]
    for b in range(bpd):
        B["aggb"][b] = acc[b].astype(BF)
    A[zl] = B["aggb"][zl]
    send_all([(B["aggb"].at[z], A.at[zl], dev(zl_=z)) for z in zs], A.at[pl.ds(0, ZL - 1)], "ag")
    half = X // 2
    got(wg.at[y_down, c], "w4", 0)
    send(wg.at[y_down, c], wg.at[y_down, c], "w3", 1, sib)
    if Y > 2:
        part = wg.at[y_down, c, pl.ds(0, half)]
        send(part, part, "w5", 0, dev(y_=y_up))
        got(wg.at[y_up, c], "w4", 1)
        part = wg.at[y_up, c, pl.ds(half, half)]
        send(part, part, "w5", 1, dev(y_=y_down))
        send(wg.at[y_up, c], wg.at[y_up, c], "w3", 2, sib)
    if ZL > 1:
        got(A.at[pl.ds(0, ZL - 1)], "ag", 0)

    a2 = A[...].reshape(rows, tb)
    AT[y] = a2.astype(F32).T.astype(BF)
    for d in range(1, Y):
        send(AT.at[y], AT.at[y], "agy", d - 1, dev(y_=up(y, d, Y)))

    def weight_of(y_, i):
        return jnp.concatenate([wg[y_, e, i].reshape(rows, qw) for e in range(C)], axis=1)

    preT, gpT = B["preT"], B["gpT"]
    got(wg.at[y, co], "w3", 0)
    for i in range(X):
        preT[i] = dot(AT[y], weight_of(y, i), 1, 0)
    got(ctT.at[pl.ds(0, Y - 1)], "cty", 0)
    order = [(1, 1), (3, 2), (2, 3)] if Y > 2 else [(1, 1)]
    for n, (d, at) in enumerate(order):
        y_ = down(y, d, Y)
        if d == 2:
            got(wg.at[y_far, c, pl.ds(0, half)], "w5", 0)
            got(wg.at[y_far, c, pl.ds(half, half)], "w5", 1)
            send(wg.at[y_far, c], wg.at[y_far, c], "w3", 3, sib)
        got(AT.at[y_], "agy", d - 1)
        got(wg.at[y_, co], "w3", at)
        for i in range(X):
            pre = preT[i] + dot(AT[y_], weight_of(y_, i), 1, 0)
            preT[i] = pre
            if n == len(order) - 1:
                sig = jax.nn.sigmoid(pre)
                gp = (ctT[i].astype(F32) * sig * (1.0 + pre * (1.0 - sig))).astype(BF)
                for e in range(C):
                    gpT[i * C + e] = gp[:, e * qw:(e + 1) * qw]

    def grad_pre(i):
        return jnp.concatenate([gpT[i * C + e] for e in range(C)], axis=1)

    ga = dot(weight_of(y, 0), grad_pre(0), 1, 1)
    for i in range(1, X):
        ga = ga + dot(weight_of(y, i), grad_pre(i), 1, 1)
    gab, GA = B["gab"], B["GA"]
    gab[...] = ga.astype(BF).reshape(ZL, rb, tb)
    GA[zl] = gab[zl]
    send_all([(gab.at[z], GA.at[zl], dev(zl_=z)) for z in zs], GA.at[pl.ds(0, ZL - 1)], "ga")

    PS, PO, PR = B["PS"], B["PO"], B["PR"]
    for i in range(X):
        PS[i] = dot(a2, gpT[i * C + co], 1, 0).astype(BF).reshape(ZL, rb, qw)
    send(PS, PR, "p", 0, sib)
    for i in range(X):
        PO[i] = dot(a2, gpT[i * C + c], 1, 0).reshape(ZL, rb, qw)
    got(PR, "p", 0)
    DXs, DXr = B["DXs"], B["DXr"]
    for d in range(1, X):
        x_ = up(x, d, X)
        DXs[d - 1] = (PO[x_] + PR[x_].astype(F32)).astype(BF)
    send_all([(DXs.at[n], DXr.at[n], dev(x_=v)) for n, v in enumerate(xs)], DXr, "dx")
    ADs, ADr = B["ADs"], B["ADr"]
    pre = preT[y]
    ADs[:, 0] = (pre * jax.nn.sigmoid(pre)).T.astype(BF).reshape(ZL, rb, tb)
    if ZL > 1:
        got(GA.at[pl.ds(0, ZL - 1)], "ga", 0)

    def backward(half, m):
        outs = [None] * bpd
        for j in range(PER):
            k = (half * Q + m) * PER + j
            back = dot(GA[itab[2, k]], tv[itab[0, k]], 1, 0)
            for b in range(bpd):
                term = ftab[bpd + b, k] * back
                outs[b] = term if j == 0 else outs[b] + term
        return outs

    def contribute(half, core, into):
        step = 2 if X % 2 == 0 else 1

        def some(i, carry):
            for n in range(step):
                for b, out in enumerate(backward(half, (i * step + n) * C + core)):
                    into[i * step + n, b] = out.astype(into.dtype)
            return carry
        lax.fori_loop(0, X // step, some, 0)

    Dsib, Drec, Dkeep = (B["Dsib0"], B["Dsib1"]), (B["Drec0"], B["Drec1"]), (B["Dkeep0"], B["Dkeep1"])
    EXs, EXr = (B["EXs0"], B["EXs1"]), (B["EXr0"], B["EXr1"])

    parts = 2 if bpd % 2 == 0 else 1

    def cut(i):
        return pl.ds(i * (bpd // parts), bpd // parts)

    whole = pl.ds(0, bpd)

    def to_x(n, at=whole, i=0):
        for d, v in enumerate(xs):
            EXs[n][d, at] = (Dkeep[n][v, at] + Drec[n][v, at].astype(F32)).astype(BF)
            copy(EXs[n].at[d, at], EXr[n].at[d, at], "e%d" % n, i, dev(x_=v)).start()
        sent.append(copy(EXr[n].at[:, at], EXr[n].at[:, at], "e%d" % n, i, sib))

    def from_x(n, at=whole, i=0):
        got(EXr[n].at[:, at], "e%d" % n, i)
        total = Dkeep[n][x, at] + Drec[n][x, at].astype(F32)
        for d in range(X - 1):
            total = total + EXr[n][d, at].astype(F32)
        return total

    contribute(zo, co, Dsib[0])
    send(Dsib[0], Drec[0], "d0", 0, sib)
    S32 = B["S32"]
    got(DXr, "dx", 0)
    total = PO[x] + PR[x].astype(F32)
    for d in range(X - 1):
        total = total + DXr[d].astype(F32)
    S32[...] = total
    ADs[:, 1] = total.astype(BF)
    ADr[zl] = ADs[zl]
    send_all([(ADs.at[z], ADr.at[zl], dev(zl_=z)) for z in zs], ADr.at[pl.ds(0, ZL - 1)], "ad")
    contribute(zo, c, Dkeep[0])

    got(Drec[0], "d0", 0)
    for i in range(parts):
        to_x(0, cut(i), i)
    contribute(zh, co, Dsib[1])
    send(Dsib[1], Drec[1], "d1", 0, sib)
    total = S32[zl]
    if ZL > 1:
        got(ADr.at[pl.ds(0, ZL - 1)], "ad", 0)
    for d in range(1, ZL):
        total = total + ADr[down(zl, d, ZL), 1].astype(F32)
    Ts, Tr, OutW = B["Ts"], B["Tr"], B["OutW"]
    Ts[...] = total
    send(Ts, Tr, "dt", 0, anti)
    FZs, FZr = B["FZs"], B["FZr"]
    for i in range(parts):
        at = cut(i)
        FZs[at] = from_x(0, at, i).astype(BF)
        send(FZs.at[at], FZr.at[at], "gz", i, anti)
    contribute(zh, c, Dkeep[1])
    for b in range(bpd):
        Dkeep[1][x, b] = ftab[2 * bpd, b] * dot(GA[b], tv[b], 1, 0)
    got(Drec[1], "d1", 0)
    to_x(1)
    for b in range(bpd):
        act_o[:, b * tb:(b + 1) * tb] = ADr[b, 0]
    got(Tr, "dt", 0)
    OutW[me] = Ts[...] + Tr[...]
    others = [(d, e) for d in range(X) for e in range(C) if d or e]
    tos = [dev(x_=up(x, d, X), c_=(co if e else c)) for d, e in others]
    send_all([(OutW.at[me], OutW.at[me], to) for to in tos], OutW.at[pl.ds(0, Q - 1)], "ow")
    own = from_x(1)
    got(OutW.at[pl.ds(0, Q - 1)], "ow", 0)
    for q in range(Q):
        gw_o[:, q * qw:(q + 1) * qw] = OutW[q]
    for cp in sent:
        cp.wait_send()
    for i in range(parts):
        got(FZr.at[cut(i)], "gz", i)
    own = (own + FZr[...].astype(F32)).astype(BF)
    for b in range(bpd):
        gf_o[:, b * tb:(b + 1) * tb] = own[b]


def on_device(cfg, features_t, tile_dst, tile_src, tile_edges, tile_values, weight, cotangent):
    rb = features_t.shape[0]
    nt, tb = tile_values.shape[:2]
    bufs, sems, smem = shapes(cfg, rb, tb, nt)
    vm, hbm = pl.BlockSpec(memory_space=pltpu.VMEM), pl.BlockSpec(memory_space=pltpu.HBM)
    kernel = functools.partial(body, cfg, tuple(bufs), tuple(sems))
    outs = (
        pltpu.VMEM(features_t.shape, BF),
        pltpu.VMEM(weight.shape, F32),
        pltpu.VMEM(features_t.shape, BF),
    )
    return pl.pallas_call(
        kernel,
        out_shape=outs,
        in_specs=[hbm] * 7,
        out_specs=(vm, vm, vm),
        scratch_shapes=[pltpu.VMEM(s, t) for s, t in bufs.values()]
        + [pltpu.SemaphoreType.DMA((n,)) for n in sems.values()] * 2
        + [pltpu.SemaphoreType.DMA((9,))]
        + [pltpu.SMEM(s, t) for s, t in smem.values()],
        compiler_params=pltpu.CompilerParams(
            collective_id=0, has_side_effects=True, vmem_limit_bytes=62 * 1024 * 1024
        ),
        name="graph_conv",
    )(features_t, tile_values, weight, cotangent, *(v.reshape(1, nt) for v in (tile_dst, tile_src, tile_edges)))


def solution(mesh, cfg=None):
    in_specs = (
        P("rep", "blk"),
        P("blk"),
        P("blk"),
        P("blk"),
        P("blk", None, None),
        P("rep", None),
        P("rep", "blk"),
    )
    out_specs = (P("rep", "blk"), P("rep", None), P("rep", "blk"))
    return jax.shard_map(
        functools.partial(on_device, cfg or FULL), mesh=mesh, in_specs=in_specs, out_specs=out_specs, check_vma=False
    )
```

```python
import functools

import jax
import jax.numpy as jnp
from jax import lax
from jax.experimental import pallas as pl
from jax.experimental.pallas import tpu as pltpu
from jax.sharding import PartitionSpec as P

FULL = dict(ZH=2, X=4, C=2, Y=4, ZL=8)
PER = 4
MESH = pl.DeviceIdType.MESH
BF = jnp.bfloat16
F32 = jnp.float32


def dot(a, b, ca, cb):
    return lax.dot_general(a, b, (((ca,), (cb,)), ((), ())), preferred_element_type=F32)


def groups(n):
    return 2 if n % 2 == 0 else 1


def shapes(cfg, rb, tb, nt):
    X, C, Y, ZL = cfg["X"], cfg["C"], cfg["Y"], cfg["ZL"]
    Q = X * C
    F = rb * Y * ZL
    qw = F // Q
    bpd = ZL
    x1, y1 = max(X - 1, 1), max(Y - 1, 1)
    nk = -(-cfg["ZH"] * Q * PER // 128) * 128
    bufs = dict(
        fv=((rb, bpd * tb), BF),
        wv=((rb, F), BF),
        cv=((rb, bpd * tb), BF),
        dv=((1, nt), jnp.int32),
        sv=((1, nt), jnp.int32),
        ev=((1, nt), jnp.int32),
        itv=((8, nk), jnp.int32),
        ftv=((2 * bpd + 8, nk), F32),
        gown=((X, C, bpd, rb, tb), BF),
        goth=((X, C, bpd, rb, tb), BF),
        tv=((nt, tb, tb), BF),
        cb=((bpd, rb, tb), BF),
        ct=((ZL, rb, tb), BF),
        wb=((Q, rb, qw), BF),
        wg=((Y, C, X, ZL, rb, qw), BF),
        aggb=((bpd, rb, tb), BF),
        A=((ZL, rb, tb), BF),
        ctT=((Y, tb, rb * ZL), BF),
        AT=((Y, groups(ZL), tb, rb * ZL // groups(ZL)), BF),
        preT=((X, tb, C * qw), F32),
        gpT=((Q, tb, qw), BF),
        ADs=((ZL, 2, rb, tb), BF),
        ADr=((ZL, 2, rb, tb), BF),
        gab=((ZL, rb, tb), BF),
        GA=((bpd, rb, tb), BF),
        PS=((X, ZL, rb, qw), BF),
        PO=((X, ZL, rb, qw), F32),
        PR=((X, ZL, rb, qw), BF),
        DXs=((x1, ZL, rb, qw), BF),
        DXr=((x1, ZL, rb, qw), BF),
        S32=((ZL, rb, qw), F32),
        Ts=((rb, qw), F32),
        Tr=((rb, qw), F32),
        OutW=((Q, rb, qw), F32),
        Dsib0=((X, bpd, rb, tb), BF),
        Dsib1=((X, bpd, rb, tb), BF),
        Drec0=((X, bpd, rb, tb), BF),
        Drec1=((X, bpd, rb, tb), BF),
        Dkeep0=((X, bpd, rb, tb), F32),
        Dkeep1=((X, bpd, rb, tb), F32),
        EXs0=((x1, bpd, rb, tb), BF),
        EXs1=((x1, bpd, rb, tb), BF),
        EXr0=((x1, bpd, rb, tb), BF),
        EXr1=((x1, bpd, rb, tb), BF),
        FZs=((bpd, rb, tb), BF),
        FZr=((bpd, rb, tb), BF),
    )
    sems = dict(
        fz=2, fx0=1, fx1=2 * x1, fc0=1, fc1=2, w1=1, ct=1, w2=1, w3=Y, w4=2, w5=2, cty=1, ag=2, agy=2 * y1, ga=1,
        p=1, dx=1, ad=1, dt=1, ow=1, d0=1, d1=1, e0=2, e1=1, gz=2,
    )
    smem = dict(itab=((8, nk), jnp.int32), ftab=((2 * bpd + 8, nk), F32))
    return bufs, sems, smem


def tables(bpd, dst, src, edges, itv, ftv):
    nt = dst.shape[1]
    nk = itv.shape[1]
    r0 = lax.broadcasted_iota(jnp.int32, (nt, nt), 0)
    r1 = lax.broadcasted_iota(jnp.int32, (nt, nt), 1)
    k1 = lax.broadcasted_iota(jnp.int32, (nt, nk), 1)
    t0 = lax.broadcasted_iota(jnp.int32, (nt, nk), 0)
    lane = lax.broadcasted_iota(jnp.int32, (1, nt), 1)

    def column(row):
        return jnp.sum(jnp.where(r0 == r1, row, jnp.zeros_like(row)), axis=1, keepdims=True)

    bits = bpd.bit_length() - 1
    group = jnp.where((edges > 0) & (lane >= bpd), lax.shift_right_logical(src, bits), -1)
    group_c = column(group)
    rank = jnp.sum(jnp.where((group_c == group) & (r1 < r0), 1, 0), axis=1, keepdims=True)
    pick = jnp.where(group_c >= 0, group_c * PER + rank, -1) == k1

    def by_k(col):
        return jnp.sum(jnp.where(pick, col, jnp.zeros_like(col)), axis=0, keepdims=True)

    at_src, at_dst = by_k(column(src & (bpd - 1))), by_k(column(dst))
    itv[0:1] = by_k(t0)
    itv[1:2] = at_src
    itv[2:3] = at_dst
    blocks = lax.broadcasted_iota(jnp.int32, (bpd, nt), 0)
    weights = jnp.where(dst == blocks, edges.astype(F32), 0.0)
    coef = jnp.sum(weights / jnp.sum(weights, axis=1, keepdims=True), axis=0, keepdims=True)
    coef_k = by_k(column(coef))
    blocks = lax.broadcasted_iota(jnp.int32, (bpd, nk), 0)
    ftv[0:bpd] = jnp.where(at_dst == blocks, coef_k, 0.0)
    ftv[bpd:2 * bpd] = jnp.where(at_src == blocks, coef_k, 0.0)
    ftv[2 * bpd:2 * bpd + 1, 0:nt] = coef


def body(cfg, buf_names, sem_names, feat_hbm, tv_hbm, w_hbm, cot_hbm, dst_hbm, src_hbm, edge_hbm, act_o, gw_o, gf_o, *scr):
    ZH, X, C, Y, ZL = cfg["ZH"], cfg["X"], cfg["C"], cfg["Y"], cfg["ZL"]
    nb, ns = len(buf_names), len(sem_names)
    B = dict(zip(buf_names, scr[:nb]))
    SS = dict(zip(sem_names, scr[nb:nb + ns]))
    RS = dict(zip(sem_names, scr[nb + ns:nb + 2 * ns]))
    load_sem, itab, ftab = scr[nb + 2 * ns:]
    feat, w, cot = B["fv"], B["wv"], B["cv"]
    Q = X * C
    bpd = ZL
    rb, tb = B["A"].shape[1:]
    qw = B["wb"].shape[2]
    rows = ZL * rb

    blk, rep = lax.axis_index("blk"), lax.axis_index("rep")
    zh = lax.div(blk, Q)
    me = lax.rem(blk, Q)
    x, c = lax.div(me, C), lax.rem(me, C)
    y, zl = lax.div(rep, ZL), lax.rem(rep, ZL)
    zo, co = 1 - zh, 1 - c

    def dev(zh_=zh, x_=x, c_=c, y_=y, zl_=zl):
        return ((zh_ * X + x_) * C + c_, y_ * ZL + zl_)

    def up(v, d, n):
        return lax.rem(v + d, n)

    def down(v, d, n):
        return lax.rem(v + n - d, n)

    anti, sib = dev(zh_=zo), dev(c_=co)
    sent = []

    def copy(src, dst, name, i, to):
        return pltpu.make_async_remote_copy(
            src_ref=src, dst_ref=dst, send_sem=SS[name].at[i], recv_sem=RS[name].at[i],
            device_id=to, device_id_type=MESH,
        )

    def send(src, dst, name, i, to):
        cp = copy(src, dst, name, i, to)
        cp.start()
        sent.append(cp)

    def send_all(copies, size_ref, name, i=0):
        for src, dst, to in copies:
            copy(src, dst, name, i, to).start()
        if copies:
            sent.append(copy(size_ref, size_ref, name, i, sib))

    def got(dst, name, i):
        copy(dst, dst, name, i, sib).wait_recv()

    loads = [
        pltpu.make_async_copy(a, b, load_sem.at[i])
        for i, (a, b) in enumerate((
            (feat_hbm, feat), (w_hbm, w), (cot_hbm, cot), (tv_hbm, B["tv"]),
            (dst_hbm, B["dv"]), (src_hbm, B["sv"]), (edge_hbm, B["ev"]),
        ))
    ]
    for ld in loads:
        ld.start()

    barrier = pltpu.get_barrier_semaphore()
    partners = [anti]
    partners += [dev(x_=up(x, d, X), c_=(c if e == 0 else co)) for d in range(X) for e in range(C) if d or e]
    partners += [dev(zl_=up(zl, d, ZL)) for d in range(1, ZL)]
    partners += [dev(y_=up(y, d, Y)) for d in range(1, Y)]
    for p in partners:
        pl.semaphore_signal(barrier, inc=1, device_id=p, device_id_type=MESH)

    gown, goth, tv = B["gown"], B["goth"], B["tv"]
    loads[0].wait()
    for b in range(bpd):
        gown[x, c, b] = feat[:, b * tb:(b + 1) * tb]
    loads[1].wait()
    wg, wb = B["wg"], B["wb"]
    for q in range(Q):
        wb[q] = w[:, q * qw:(q + 1) * qw]
    wg[y, c, x, zl] = wb[me]
    pl.semaphore_wait(barrier, len(partners))

    xs = [up(x, d, X) for d in range(1, X)]
    zs = [up(zl, d, ZL) for d in range(1, ZL)]
    parts = groups(bpd)

    def cut(i):
        return pl.ds(i * (bpd // parts), bpd // parts)

    send(gown.at[x, c, cut(0)], goth.at[x, c, cut(0)], "fz", 0, anti)
    send_all([(gown.at[x, c], gown.at[x, c], dev(x_=v)) for v in xs], gown.at[pl.ds(0, X - 1), 0], "fx0")
    send_all([(wb.at[me], wg.at[y, c, x, zl], dev(zl_=z)) for z in zs], wg.at[y, c, x, pl.ds(0, ZL - 1)], "w1")
    for i in range(1, parts):
        send(gown.at[x, c, cut(i)], goth.at[x, c, cut(i)], "fz", i, anti)
    for ld in loads[4:]:
        ld.wait()
    tables(bpd, B["dv"][...], B["sv"][...], B["ev"][...], B["itv"], B["ftv"])
    to_smem = [
        pltpu.make_async_copy(B["itv"], itab, load_sem.at[7]),
        pltpu.make_async_copy(B["ftv"], ftab, load_sem.at[8]),
    ]
    for cp in to_smem:
        cp.start()
    loads[2].wait()
    cb, ct = B["cb"], B["ct"]
    for b in range(bpd):
        cb[b] = cot[:, b * tb:(b + 1) * tb]
    ct[zl] = cb[zl]
    got(gown.at[pl.ds(0, X - 1), 0], "fx0", 0)
    send(gown.at[:, c], gown.at[:, c], "fc0", 0, sib)
    loads[3].wait()
    for cp in to_smem:
        cp.wait()
    acc = tuple(ftab[2 * bpd, b] * dot(gown[x, c, b], tv[b], 1, 1) for b in range(bpd))

    def forward(g, half, i, acc):
        acc = list(acc)
        for j in range(C * PER):
            k = (half * Q + i * C) * PER + j
            out = dot(g[i, j // PER, itab[1, k]], tv[itab[0, k]], 1, 1)
            for b in range(bpd):
                acc[b] = acc[b] + ftab[b, k] * out
        return tuple(acc)

    part = wg.at[y, c, x]
    if ZL > 1:
        got(wg.at[y, c, x, pl.ds(0, ZL - 1)], "w1", 0)
    send_all([(part, part, dev(x_=v)) for v in xs], wg.at[y, c, pl.ds(0, X - 1)], "w2")
    for i in range(parts):
        part = goth.at[x, c, cut(i)]
        got(part, "fz", i)
        for d in range(1, X):
            send(part, part, "fx1", i * (X - 1) + d - 1, dev(x_=up(x, d, X)))
        copy(part, part, "fc1", i, sib).start()
    send_all([(cb.at[z], ct.at[zl], dev(zl_=z)) for z in zs], ct.at[pl.ds(0, ZL - 1)], "ct")
    got(wg.at[y, c, pl.ds(0, X - 1)], "w2", 0)
    y_up, y_down, y_far = up(y, 1, Y), down(y, 1, Y), up(y, 2, Y)
    send(wg.at[y, c], wg.at[y, c], "w4", 0, dev(y_=y_up))
    if Y > 2:
        send(wg.at[y, c], wg.at[y, c], "w4", 1, dev(y_=y_down))
    send(wg.at[y, c], wg.at[y, c], "w3", 0, sib)
    got(gown.at[:, co], "fc0", 0)
    acc = lax.fori_loop(0, Q // C, lambda i, a: forward(gown, zh, i, a), acc)
    for i in range(parts):
        for d in range(1, X):
            part = goth.at[down(x, d, X), c, cut(i)]
            got(part, "fx1", i * (X - 1) + d - 1)
            copy(part, part, "fc1", i, sib).start()
        sent.append(copy(goth.at[:, c, cut(i)], goth.at[:, c, cut(i)], "fc1", i, sib))
    if ZL > 1:
        got(ct.at[pl.ds(0, ZL - 1)], "ct", 0)
    ctT, AT = B["ctT"], B["AT"]
    ctT[y] = ct[...].reshape(rows, tb).astype(F32).T.astype(BF)
    ys = [up(y, d, Y) for d in range(1, Y)]
    send_all([(ctT.at[y], ctT.at[y], dev(y_=v)) for v in ys], ctT.at[pl.ds(0, Y - 1)], "cty")
    for i in range(parts):
        got(goth.at[:, co, cut(i)], "fc1", i)
    acc = lax.fori_loop(0, Q // C, lambda i, a: forward(goth, zo, i, a), acc)

    A = B["A"]
    for b in range(bpd):
        B["aggb"][b] = acc[b].astype(BF)
    A[zl] = B["aggb"][zl]
    ng = groups(ZL)
    hz = ZL // ng
    near = lax.div(zl, hz)
    for z in zs:
        copy(B["aggb"].at[z], A.at[zl], "ag", (lax.div(z, hz) + near) % ng, dev(zl_=z)).start()
    ag_sizes = [A.at[pl.ds(0, hz - 1 if n == 0 else hz)] for n in range(ng)]
    ag_groups = [(n, r) for n, r in enumerate(ag_sizes) if n > 0 or hz > 1]
    for n, r in ag_groups:
        sent.append(copy(r, r, "ag", n, sib))
    half = X // 2
    got(wg.at[y_down, c], "w4", 0)
    send(wg.at[y_down, c], wg.at[y_down, c], "w3", 1, sib)
    if Y > 2:
        part = wg.at[y_down, c, pl.ds(0, half)]
        send(part, part, "w5", 0, dev(y_=y_up))
        got(wg.at[y_up, c], "w4", 1)
        part = wg.at[y_up, c, pl.ds(half, half)]
        send(part, part, "w5", 1, dev(y_=y_down))
        send(wg.at[y_up, c], wg.at[y_up, c], "w3", 2, sib)

    for n in range(ng):
        if n > 0 or hz > 1:
            got(ag_sizes[n], "ag", n)
        g = near if n == 0 else 1 - near
        AT[y, g] = A[pl.ds(g * hz, hz)].reshape(rows // ng, tb).astype(F32).T.astype(BF)
        for d in range(1, Y):
            send(AT.at[y, g], AT.at[y, g], "agy", n * (Y - 1) + d - 1, dev(y_=up(y, d, Y)))
    a2 = A[...].reshape(rows, tb)

    def nodes_by_rows(y_):
        return jnp.concatenate([AT[y_, g] for g in range(ng)], axis=1)

    def weight_of(y_, i):
        return jnp.concatenate([wg[y_, e, i].reshape(rows, qw) for e in range(C)], axis=1)

    preT, gpT = B["preT"], B["gpT"]
    got(wg.at[y, co], "w3", 0)
    for i in range(X):
        preT[i] = dot(nodes_by_rows(y), weight_of(y, i), 1, 0)
    got(ctT.at[pl.ds(0, Y - 1)], "cty", 0)
    order = [(1, 1), (3, 2), (2, 3)] if Y > 2 else [(1, 1)]
    for n, (d, at) in enumerate(order):
        y_ = down(y, d, Y)
        if d == 2:
            got(wg.at[y_far, c, pl.ds(0, half)], "w5", 0)
            got(wg.at[y_far, c, pl.ds(half, half)], "w5", 1)
            send(wg.at[y_far, c], wg.at[y_far, c], "w3", 3, sib)
        for g in range(ng):
            got(AT.at[y_, near if g == 0 else 1 - near], "agy", g * (Y - 1) + d - 1)
        got(wg.at[y_, co], "w3", at)
        for i in range(X):
            pre = preT[i] + dot(nodes_by_rows(y_), weight_of(y_, i), 1, 0)
            preT[i] = pre
            if n == len(order) - 1:
                sig = jax.nn.sigmoid(pre)
                gp = (ctT[i].astype(F32) * sig * (1.0 + pre * (1.0 - sig))).astype(BF)
                for e in range(C):
                    gpT[i * C + e] = gp[:, e * qw:(e + 1) * qw]

    def grad_pre(i):
        return jnp.concatenate([gpT[i * C + e] for e in range(C)], axis=1)

    ga = dot(weight_of(y, 0), grad_pre(0), 1, 1)
    for i in range(1, X):
        ga = ga + dot(weight_of(y, i), grad_pre(i), 1, 1)
    gab, GA = B["gab"], B["GA"]
    gab[...] = ga.astype(BF).reshape(ZL, rb, tb)
    GA[zl] = gab[zl]
    send_all([(gab.at[z], GA.at[zl], dev(zl_=z)) for z in zs], GA.at[pl.ds(0, ZL - 1)], "ga")

    PS, PO, PR = B["PS"], B["PO"], B["PR"]
    for i in range(X):
        PS[i] = dot(a2, gpT[i * C + co], 1, 0).astype(BF).reshape(ZL, rb, qw)
    send(PS, PR, "p", 0, sib)
    for i in range(X):
        PO[i] = dot(a2, gpT[i * C + c], 1, 0).reshape(ZL, rb, qw)
    got(PR, "p", 0)
    DXs, DXr = B["DXs"], B["DXr"]
    for d in range(1, X):
        x_ = up(x, d, X)
        DXs[d - 1] = (PO[x_] + PR[x_].astype(F32)).astype(BF)
    send_all([(DXs.at[n], DXr.at[n], dev(x_=v)) for n, v in enumerate(xs)], DXr, "dx")
    ADs, ADr = B["ADs"], B["ADr"]
    pre = preT[y]
    ADs[:, 0] = (pre * jax.nn.sigmoid(pre)).T.astype(BF).reshape(ZL, rb, tb)
    if ZL > 1:
        got(GA.at[pl.ds(0, ZL - 1)], "ga", 0)

    def backward(half, m):
        outs = [None] * bpd
        for j in range(PER):
            k = (half * Q + m) * PER + j
            back = dot(GA[itab[2, k]], tv[itab[0, k]], 1, 0)
            for b in range(bpd):
                term = ftab[bpd + b, k] * back
                outs[b] = term if j == 0 else outs[b] + term
        return outs

    def contribute(half, core, into):
        step = 2 if X % 2 == 0 else 1

        def some(i, carry):
            for n in range(step):
                for b, out in enumerate(backward(half, (i * step + n) * C + core)):
                    into[i * step + n, b] = out.astype(into.dtype)
            return carry
        lax.fori_loop(0, X // step, some, 0)

    Dsib, Drec, Dkeep = (B["Dsib0"], B["Dsib1"]), (B["Drec0"], B["Drec1"]), (B["Dkeep0"], B["Dkeep1"])
    EXs, EXr = (B["EXs0"], B["EXs1"]), (B["EXr0"], B["EXr1"])

    whole = pl.ds(0, bpd)

    def to_x(n, at=whole, i=0):
        for d, v in enumerate(xs):
            EXs[n][d, at] = (Dkeep[n][v, at] + Drec[n][v, at].astype(F32)).astype(BF)
            copy(EXs[n].at[d, at], EXr[n].at[d, at], "e%d" % n, i, dev(x_=v)).start()
        sent.append(copy(EXr[n].at[:, at], EXr[n].at[:, at], "e%d" % n, i, sib))

    def from_x(n, at=whole, i=0):
        got(EXr[n].at[:, at], "e%d" % n, i)
        total = Dkeep[n][x, at] + Drec[n][x, at].astype(F32)
        for d in range(X - 1):
            total = total + EXr[n][d, at].astype(F32)
        return total

    contribute(zo, co, Dsib[0])
    send(Dsib[0], Drec[0], "d0", 0, sib)
    S32 = B["S32"]
    got(DXr, "dx", 0)
    total = PO[x] + PR[x].astype(F32)
    for d in range(X - 1):
        total = total + DXr[d].astype(F32)
    S32[...] = total
    ADs[:, 1] = total.astype(BF)
    ADr[zl] = ADs[zl]
    send_all([(ADs.at[z], ADr.at[zl], dev(zl_=z)) for z in zs], ADr.at[pl.ds(0, ZL - 1)], "ad")
    contribute(zo, c, Dkeep[0])

    got(Drec[0], "d0", 0)
    for i in range(parts):
        to_x(0, cut(i), i)
    contribute(zh, co, Dsib[1])
    send(Dsib[1], Drec[1], "d1", 0, sib)
    total = S32[zl]
    if ZL > 1:
        got(ADr.at[pl.ds(0, ZL - 1)], "ad", 0)
    for d in range(1, ZL):
        total = total + ADr[down(zl, d, ZL), 1].astype(F32)
    Ts, Tr, OutW = B["Ts"], B["Tr"], B["OutW"]
    Ts[...] = total
    send(Ts, Tr, "dt", 0, anti)
    FZs, FZr = B["FZs"], B["FZr"]
    for i in range(parts):
        at = cut(i)
        FZs[at] = from_x(0, at, i).astype(BF)
        send(FZs.at[at], FZr.at[at], "gz", i, anti)
    contribute(zh, c, Dkeep[1])
    for b in range(bpd):
        Dkeep[1][x, b] = ftab[2 * bpd, b] * dot(GA[b], tv[b], 1, 0)
    got(Drec[1], "d1", 0)
    to_x(1)
    for b in range(bpd):
        act_o[:, b * tb:(b + 1) * tb] = ADr[b, 0]
    got(Tr, "dt", 0)
    OutW[me] = Ts[...] + Tr[...]
    others = [(d, e) for d in range(X) for e in range(C) if d or e]
    tos = [dev(x_=up(x, d, X), c_=(co if e else c)) for d, e in others]
    send_all([(OutW.at[me], OutW.at[me], to) for to in tos], OutW.at[pl.ds(0, Q - 1)], "ow")
    own = from_x(1)
    got(OutW.at[pl.ds(0, Q - 1)], "ow", 0)
    for q in range(Q):
        gw_o[:, q * qw:(q + 1) * qw] = OutW[q]
    for cp in sent:
        cp.wait_send()
    for i in range(parts):
        got(FZr.at[cut(i)], "gz", i)
    own = (own + FZr[...].astype(F32)).astype(BF)
    for b in range(bpd):
        gf_o[:, b * tb:(b + 1) * tb] = own[b]


def on_device(cfg, features_t, tile_dst, tile_src, tile_edges, tile_values, weight, cotangent):
    rb = features_t.shape[0]
    nt, tb = tile_values.shape[:2]
    bufs, sems, smem = shapes(cfg, rb, tb, nt)
    vm, hbm = pl.BlockSpec(memory_space=pltpu.VMEM), pl.BlockSpec(memory_space=pltpu.HBM)
    kernel = functools.partial(body, cfg, tuple(bufs), tuple(sems))
    outs = (
        pltpu.VMEM(features_t.shape, BF),
        pltpu.VMEM(weight.shape, F32),
        pltpu.VMEM(features_t.shape, BF),
    )
    return pl.pallas_call(
        kernel,
        out_shape=outs,
        in_specs=[hbm] * 7,
        out_specs=(vm, vm, vm),
        scratch_shapes=[pltpu.VMEM(s, t) for s, t in bufs.values()]
        + [pltpu.SemaphoreType.DMA((n,)) for n in sems.values()] * 2
        + [pltpu.SemaphoreType.DMA((9,))]
        + [pltpu.SMEM(s, t) for s, t in smem.values()],
        compiler_params=pltpu.CompilerParams(
            collective_id=0, has_side_effects=True, vmem_limit_bytes=62 * 1024 * 1024
        ),
        name="graph_conv",
    )(features_t, tile_values, weight, cotangent, *(v.reshape(1, nt) for v in (tile_dst, tile_src, tile_edges)))


def solution(mesh, cfg=None):
    in_specs = (
        P("rep", "blk"),
        P("blk"),
        P("blk"),
        P("blk"),
        P("blk", None, None),
        P("rep", None),
        P("rep", "blk"),
    )
    out_specs = (P("rep", "blk"), P("rep", None), P("rep", "blk"))
    return jax.shard_map(
        functools.partial(on_device, cfg or FULL), mesh=mesh, in_specs=in_specs, out_specs=out_specs, check_vma=False
    )
```
